128 devices in a mesh: dp: 32 (over y, x, core), mp: 4 (over z).
Axes of the slice: x: 4, y: 4, z: 4, core: 2. Of those that a mesh axis runs over, the one named last changes fastest.
Arguments:
- residual: float32 [32, 512, 2048], P('dp', 'mp'), may hold values from -6 to 6
- cotangent: float32 [32, 512, 2048], P('dp', 'mp'), may hold values from -6 to 6
- document_lengths: int32 [32, 4], P('dp'), may hold values from 1 to 448, 512 in all within a row
- norm_gains: float32 [2, 2048], P(None, 'dp'), may hold values from 0.5 to 1.5
- query_weight: float32 [2048, 2048], P('dp', 'mp'), may hold values from -0.125 to 0.125
- keyvalue_weight: float32 [2, 2048, 256], P(None, 'dp', 'mp'), may hold values from -0.125 to 0.125
- output_weight: float32 [2048, 2048], P('mp', 'dp'), may hold values from -1.5 to 1.5
- gateup_weight: float32 [2, 2048, 5632], P(None, 'dp', 'mp'), may hold values from -0.125 to 0.125
- down_weight: float32 [5632, 2048], P('mp', 'dp'), may hold values from -0.078125 to 0.078125
- moment_gains: float32 [2, 2048], P(None, 'dp'), may hold values from -80 to 80
- moment_query: float32 [2048, 2048], P('dp', 'mp'), may hold values from -80 to 80
- moment_keyvalue: float32 [2, 2048, 256], P(None, 'dp', 'mp'), may hold values from -80 to 80
- moment_output: float32 [2048, 2048], P('mp', 'dp'), may hold values from -10 to 10
- moment_gateup: float32 [2, 2048, 5632], P(None, 'dp', 'mp'), may hold values from -24 to 24
- moment_down: float32 [5632, 2048], P('mp', 'dp'), may hold values from -48 to 48
- square_gains: float32 [2, 2048], P(None, 'dp'), may hold values from 868.352 to 3440.64
- square_query: float32 [2048, 2048], P('dp', 'mp'), may hold values from 868.352 to 3440.64
- square_keyvalue: float32 [2, 2048, 256], P(None, 'dp', 'mp'), may hold values from 868.352 to 3440.64
- square_output: float32 [2048, 2048], P('mp', 'dp'), may hold values from 13.1072 to 52.4288
- square_gateup: float32 [2, 2048, 5632], P(None, 'dp', 'mp'), may hold values from 78.6432 to 311.296
- square_down: float32 [5632, 2048], P('mp', 'dp'), may hold values from 311.296 to 1245.184
Outputs:
- block_output: float32 [32, 512, 2048], P('dp', 'mp')
- input_gradient: float32 [32, 512, 2048], P('dp', 'mp')
- gradient_gains: float32 [2, 2048], P(None, 'dp')
- gradient_query: float32 [2048, 2048], P('dp', 'mp')
- gradient_keyvalue: float32 [2, 2048, 256], P(None, 'dp', 'mp')
- gradient_output: float32 [2048, 2048], P('mp', 'dp')
- gradient_gateup: float32 [2, 2048, 5632], P(None, 'dp', 'mp')
- gradient_down: float32 [5632, 2048], P('mp', 'dp')
- momentum_gains: float32 [2, 2048], P(None, 'dp')
- momentum_query: float32 [2048, 2048], P('dp', 'mp')
- momentum_keyvalue: float32 [2, 2048, 256], P(None, 'dp', 'mp')
- momentum_output: float32 [2048, 2048], P('mp', 'dp')
- momentum_gateup: float32 [2, 2048, 5632], P(None, 'dp', 'mp')
- momentum_down: float32 [5632, 2048], P('mp', 'dp')
- variance_gains: float32 [2, 2048], P(None, 'dp')
- variance_query: float32 [2048, 2048], P('dp', 'mp')
- variance_keyvalue: float32 [2, 2048, 256], P(None, 'dp', 'mp')
- variance_output: float32 [2048, 2048], P('mp', 'dp')
- variance_gateup: float32 [2, 2048, 5632], P(None, 'dp', 'mp')
- variance_down: float32 [5632, 2048], P('mp', 'dp')
- updated_gains: float32 [2, 2048], P(None, 'dp')
- updated_query: float32 [2048, 2048], P('dp', 'mp')
- updated_keyvalue: float32 [2, 2048, 256], P(None, 'dp', 'mp')
- updated_output: float32 [2048, 2048], P('mp', 'dp')
- updated_gateup: float32 [2, 2048, 5632], P(None, 'dp', 'mp')
- updated_down: float32 [5632, 2048], P('mp', 'dp')
The draws below stay inside these ranges and needn't reach their ends.
Inputs may be any that keep to these rules, and one draw needn't show every extreme that they name: `document_lengths`: the 4 lengths of a row sum to 512; every row has one document of exactly 448 tokens.
All inputs are finite; a program needn't handle non-finite values.
Results may differ from the reference program's by a relative error of at most 0.025.
Values may be sent and summed in bfloat16 or wider, within the bound.
No kernel may reach another device: no remote copies, remote signals or barrier semaphores. Data moves between devices by JAX's collectives and lax.ppermute only.
A program may use at most 192 MiB of HBM per device.

```python
import math
import jax
import jax.numpy as jnp
import numpy as np
from jax import lax

D = 2048
HEADS = 32
KV_HEADS = 4
HEAD_DIM = 64
FF = 5632
SEQ = 512
DOCS = 4
STEP = 10
BATCH = 32


def block_levels(stream_key, shape, pieces, low, largest):
    loudness = 1.0
    for dim, shards_of in pieces:
        draws = jax.random.uniform(jax.random.fold_in(jax.random.fold_in(stream_key, 6), dim), (shards_of,), jnp.float32, low / len(pieces), largest / len(pieces))
        loudness = loudness * jnp.repeat(jnp.exp(draws), shape[dim] // shards_of).reshape((-1,) + (1,) * (len(shape) - 1 - dim))
    return loudness


def split_up(count, total, bound, skew):
    weights = [(1 << 20) // math.isqrt(grade ** skew) + 1 for grade in range(2, count + 1)]
    surplus, holding = total - bound - (count - 1), [1] * (count - 1)
    while surplus > 0:
        free = [i for i in range(count - 1) if holding[i] < bound]
        mass, left = sum([weights[i] for i in free]), surplus
        for i in free:
            extra = min(bound - holding[i], max(1, left * weights[i] // mass), surplus)
            holding[i] = holding[i] + extra
            surplus = surplus - extra
    return np.array([bound] + holding)


def uneven_parts(stream_key, amount, total, bound, skew):
    if amount == 2:
        one = jax.random.randint(stream_key, (), max(1, total - bound), min(bound, total - 1) + 1)
        return jnp.stack([one, total - one])
    sizes = jnp.asarray(split_up(amount, total, bound, skew), jnp.int32)
    pairs = (amount - 1) // 2
    giver, taker = sizes[1:1 + 2 * pairs:2], sizes[2:2 + 2 * pairs:2]
    margin = jnp.minimum(giver - 1, bound - taker)
    passed = jax.random.randint(jax.random.fold_in(stream_key, 1), (pairs,), 0, 1 << 20) % (margin + 1)
    sizes = sizes.at[1:1 + 2 * pairs:2].set(giver - passed).at[2:2 + 2 * pairs:2].set(taker + passed)
    return sizes[jax.random.permutation(jax.random.fold_in(stream_key, 2), amount)]


def centred(own_key, dims, spread, most, split=(), dtype=jnp.bfloat16):
    entries = spread * jax.random.normal(own_key, dims, jnp.float32)
    if split:
        entries = entries * block_levels(own_key, dims, split, -0.22, 0.18)
    return jnp.clip(entries, -most, most).astype(dtype)


def setup_inputs(seed: int = 0) -> dict:
    keys = jax.random.split(jax.random.key(seed), 22)
    residual = centred(keys[0], (BATCH, SEQ, D), 1.0, 6.0, ((0, 32), (1, 4)), jnp.float32)
    cotangent = centred(keys[1], (BATCH, SEQ, D), 1.0, 6.0, ((0, 32), (1, 4)), jnp.float32)
    document_lengths = jax.vmap(lambda own: uneven_parts(own, DOCS, SEQ, SEQ - SEQ // 8, 1))(jax.random.split(keys[2], BATCH)).reshape((BATCH, DOCS)).astype(jnp.int32)
    norm_gains = jnp.clip(1.0 + 0.1 * jax.random.normal(keys[3], (2, D), jnp.float32), 0.5, 1.5)
    query_weight = centred(keys[4], (D, HEADS * HEAD_DIM), D ** -0.5, 0.125, ((0, 32), (1, 4)), jnp.float32)
    keyvalue_weight = centred(keys[5], (2, D, KV_HEADS * HEAD_DIM), D ** -0.5, 0.125, ((1, 32), (2, 4)), jnp.float32)
    output_weight = centred(keys[6], (HEADS * HEAD_DIM, D), (HEADS * HEAD_DIM * 4 // SEQ) ** -0.5, 1.5, ((0, 4), (1, 32)), jnp.float32)
    gateup_weight = centred(keys[7], (2, D, FF), D ** -0.5, 0.125, ((1, 32), (2, 4)), jnp.float32)
    down_weight = centred(keys[8], (FF, D), FF ** -0.5, 0.078125, ((0, 4), (1, 32)), jnp.float32)
    moment_gains = centred(keys[9], (2, D), (0.111 * (BATCH * SEQ) ** 0.5), 80.0, ((1, 32),), jnp.float32)
    moment_query = centred(keys[10], (D, HEADS * HEAD_DIM), (0.111 * (BATCH * SEQ) ** 0.5), 80.0, ((0, 32), (1, 4)), jnp.float32)
    moment_keyvalue = centred(keys[11], (2, D, KV_HEADS * HEAD_DIM), (0.111 * (BATCH * SEQ) ** 0.5), 80.0, ((1, 32), (2, 4)), jnp.float32)
    moment_output = centred(keys[12], (HEADS * HEAD_DIM, D), (0.0133 * (BATCH * SEQ) ** 0.5), 10.0, ((0, 4), (1, 32)), jnp.float32)
    moment_gateup = centred(keys[13], (2, D, FF), (0.0333 * (BATCH * SEQ) ** 0.5), 24.0, ((1, 32), (2, 4)), jnp.float32)
    moment_down = centred(keys[14], (FF, D), (0.0666 * (BATCH * SEQ) ** 0.5), 48.0, ((0, 4), (1, 32)), jnp.float32)
    square_gains = jnp.clip(jnp.exp(math.log(3440.64) - 1.3768156 * jax.random.uniform(keys[15], (2, D), jnp.float32) ** block_levels(keys[15], (2, D), ((1, 32),), -0.2, 0.2)), 868.352, 3440.64)
    square_query = jnp.clip(jnp.exp(math.log(3440.64) - 1.3768156 * jax.random.uniform(keys[16], (D, HEADS * HEAD_DIM), jnp.float32) ** block_levels(keys[16], (D, HEADS * HEAD_DIM), ((0, 32), (1, 4)), -0.2, 0.2)), 868.352, 3440.64)
    square_keyvalue = jnp.clip(jnp.exp(math.log(3440.64) - 1.3768156 * jax.random.uniform(keys[17], (2, D, KV_HEADS * HEAD_DIM), jnp.float32) ** block_levels(keys[17], (2, D, KV_HEADS * HEAD_DIM), ((1, 32), (2, 4)), -0.2, 0.2)), 868.352, 3440.64)
    square_output = jnp.clip(jnp.exp(math.log(52.4288) - 1.3862944 * jax.random.uniform(keys[18], (HEADS * HEAD_DIM, D), jnp.float32) ** block_levels(keys[18], (HEADS * HEAD_DIM, D), ((0, 4), (1, 32)), -0.2, 0.2)), 13.1072, 52.4288)
    square_gateup = jnp.clip(jnp.exp(math.log(311.296) - 1.375823 * jax.random.uniform(keys[19], (2, D, FF), jnp.float32) ** block_levels(keys[19], (2, D, FF), ((1, 32), (2, 4)), -0.2, 0.2)), 78.6432, 311.296)
    square_down = jnp.clip(jnp.exp(math.log(1245.184) - 1.3862944 * jax.random.uniform(keys[20], (FF, D), jnp.float32) ** block_levels(keys[20], (FF, D), ((0, 4), (1, 32)), -0.2, 0.2)), 311.296, 1245.184)
    return {"residual": residual, "cotangent": cotangent, "document_lengths": document_lengths, "norm_gains": norm_gains, "query_weight": query_weight, "keyvalue_weight": keyvalue_weight, "output_weight": output_weight, "gateup_weight": gateup_weight, "down_weight": down_weight, "moment_gains": moment_gains, "moment_query": moment_query, "moment_keyvalue": moment_keyvalue, "moment_output": moment_output, "moment_gateup": moment_gateup, "moment_down": moment_down, "square_gains": square_gains, "square_query": square_query, "square_keyvalue": square_keyvalue, "square_output": square_output, "square_gateup": square_gateup, "square_down": square_down}


EPS = 1e-05
THETA = 10000.0
BETA_ONE = 0.9
BETA_TWO = 0.95
ADAM_EPS = 1e-08
RATES = (1.0, 0.05, 0.05, 0.5, 0.05, 0.025)
DECAYS = (0.0, 0.1, 0.1, 0.1, 0.1, 0.1)
HIGH = lax.Precision.HIGHEST

@jax.custom_vjp
def low(v):
    return lax.optimization_barrier(v.astype(jnp.bfloat16)).astype(jnp.float32)

@jax.custom_vjp
def low_back(v):
    return v

def low_keep(v):
    return (low(v), None)

def low_pass(kept, grad):
    return (grad,)

def back_keep(v):
    return (v, None)

def back_low(kept, grad):
    return (low(grad),)
low.defvjp(low_keep, low_pass)
low_back.defvjp(back_keep, back_low)

def rope_angles(position, head_size):
    half_size = head_size // 2
    indices = jnp.arange(half_size).astype(jnp.float32)
    frequency = 1.0 / THETA ** (2.0 * indices / head_size)
    angles = position.astype(jnp.float32)[..., None] * frequency
    return (jnp.cos(angles), jnp.sin(angles))

def rotate(tensor, cosine, sine_table):
    half_size = tensor.shape[-1] // 2
    leading = tensor[..., :half_size]
    trailing = tensor[..., half_size:]
    cosine = cosine[..., None, :]
    sine_table = sine_table[..., None, :]
    return jnp.concatenate([leading * cosine - trailing * sine_table, trailing * cosine + leading * sine_table], axis=-1)

def doc_layout(lengths_row, length):
    boundary = jnp.cumsum(lengths_row).astype(jnp.int32)
    starts = boundary - lengths_row.astype(jnp.int32)
    positions = jnp.arange(length).astype(jnp.int32)
    segment = lax.optimization_barrier(jnp.sum((positions[:, None] >= boundary[None, :]).astype(jnp.int32), axis=1))
    leading = lax.optimization_barrier(jnp.max(jnp.where(starts[None, :] <= positions[:, None], starts[None, :], 0), axis=1))
    return (segment, positions - leading)

def rms_norm(tensor, gain):
    return tensor * lax.rsqrt(lax.optimization_barrier(jnp.mean(tensor * tensor, axis=-1, keepdims=True)) + EPS) * gain

def attend(queries, key_rows, value_rows, segment):
    length, heads, head_size = queries.shape
    groups = key_rows.shape[1]
    grouped = queries.reshape(length, groups, heads // groups, head_size)
    scores = jnp.einsum('qkgd,skd->kgqs', grouped, key_rows, precision=HIGH) * head_size ** (-0.5)
    scores = low_back(scores)
    positions = jnp.arange(length)
    allowed = (segment[:, None] == segment[None, :]) & (positions[None, :] <= positions[:, None])
    scores = jnp.where(allowed, scores, -1e+30)
    maximum = lax.optimization_barrier(jnp.max(scores, axis=-1, keepdims=True))
    exponent = jnp.exp(scores - maximum)
    probability = low(exponent / lax.optimization_barrier(jnp.sum(exponent, axis=-1, keepdims=True)))
    result = jnp.einsum('kgqs,skd->qkgd', probability, value_rows, precision=HIGH)
    return result.reshape(length, heads * head_size)

def matmul(left, right):
    return jnp.dot(left, right, precision=HIGH, preferred_element_type=jnp.float32)

def layer(residual, norm_gains, query_weight, keyvalue_weight, output_weight, gateup_weight, down_weight, segment, position):
    row_count, length, features = residual.shape
    heads = query_weight.shape[1] // HEAD_DIM
    groups = keyvalue_weight.shape[2] // HEAD_DIM
    gain_low = low(norm_gains)
    query_low = low(query_weight)
    keyvalue_low = low(keyvalue_weight)
    output_low = low(output_weight)
    gateup_low = low(gateup_weight)
    down_low = low(down_weight)
    tokens = residual.reshape(row_count * length, features)
    normed_one = low(rms_norm(tokens, gain_low[0]))
    query_raw = low_back(matmul(normed_one, query_low))
    key_raw = low_back(matmul(normed_one, keyvalue_low[0]))
    value_raw = low_back(matmul(normed_one, keyvalue_low[1]))
    cosine, sine_table = rope_angles(position, HEAD_DIM)
    queries = low(rotate(query_raw.reshape(row_count, length, heads, HEAD_DIM), cosine, sine_table))
    key_rows = low(rotate(key_raw.reshape(row_count, length, groups, HEAD_DIM), cosine, sine_table))
    value_rows = low(value_raw.reshape(row_count, length, groups, HEAD_DIM))
    checked = jax.checkpoint(attend)
    mixed = lax.map(lambda element: checked(*element), (queries, key_rows, value_rows, segment))
    attended = low(low_back(mixed.reshape(row_count * length, heads * HEAD_DIM)))
    attention = low_back(matmul(attended, output_low))
    middle = tokens + attention
    normed_two = low(rms_norm(middle, gain_low[1]))
    gate_act = low_back(matmul(normed_two, gateup_low[0]))
    up_act = low_back(matmul(normed_two, gateup_low[1]))
    hidden = low(jax.nn.silu(gate_act) * up_act)
    feedfwd = low_back(matmul(hidden, down_low))
    return (middle + feedfwd).reshape(row_count, length, features)

def adamw(weight, gradient, moment, square, rate, decay):
    momentum = BETA_ONE * moment + (1.0 - BETA_ONE) * gradient
    variance = BETA_TWO * square + (1.0 - BETA_TWO) * gradient * gradient
    moment_hat = momentum / (1.0 - BETA_ONE ** STEP)
    square_hat = variance / (1.0 - BETA_TWO ** STEP)
    updated = weight - rate * (moment_hat / (jnp.sqrt(square_hat) + ADAM_EPS) + decay * weight)
    return (momentum, variance, updated)

def reference(residual, cotangent, document_lengths, norm_gains, query_weight, keyvalue_weight, output_weight, gateup_weight, down_weight, moment_gains, moment_query, moment_keyvalue, moment_output, moment_gateup, moment_down, square_gains, square_query, square_keyvalue, square_output, square_gateup, square_down):
    segment, position = jax.vmap(lambda lengths_row: doc_layout(lengths_row, SEQ))(document_lengths)

    def wrapped(block_in, gains_in, query_in, keyvalue_in, output_in, gateup_in, down_in):
        return layer(block_in, gains_in, query_in, keyvalue_in, output_in, gateup_in, down_in, segment, position)
    block_output, pullback = jax.vjp(wrapped, residual, norm_gains, query_weight, keyvalue_weight, output_weight, gateup_weight, down_weight)
    grads = pullback(cotangent)
    input_gradient = grads[0]
    weights = (norm_gains, query_weight, keyvalue_weight, output_weight, gateup_weight, down_weight)
    moments = (moment_gains, moment_query, moment_keyvalue, moment_output, moment_gateup, moment_down)
    squares = (square_gains, square_query, square_keyvalue, square_output, square_gateup, square_down)
    results = [adamw(weights[i], grads[i + 1], moments[i], squares[i], RATES[i], DECAYS[i]) for i in range(6)]
    return (block_output, input_gradient, grads[1], grads[2], grads[3], grads[4], grads[5], grads[6], results[0][0], results[1][0], results[2][0], results[3][0], results[4][0], results[5][0], results[0][1], results[1][1], results[2][1], results[3][1], results[4][1], results[5][1], results[0][2], results[1][2], results[2][2], results[3][2], results[4][2], results[5][2])
```

```python
import functools

import jax
import jax.numpy as jnp
from jax import lax
from jax.experimental import pallas as pl
from jax.experimental.pallas import tpu as pltpu
from jax.sharding import PartitionSpec as P

HEAD_DIM = 64
HEADS_LOCAL = 8
QUERY_COLS = 512
QKV_COLS = 640
HIDDEN = 1408
SEQ = 512
PART = 128
D = 2048
STEP = 10

EPS = 1e-05
THETA = 10000.0
BETA_ONE = 0.9
BETA_TWO = 0.95
ADAM_EPS = 1e-08
RATES = (1.0, 0.05, 0.05, 0.5, 0.05, 0.025)
DECAYS = (0.0, 0.1, 0.1, 0.1, 0.1, 0.1)
SIDE = 4
BF16 = jnp.bfloat16
F32 = jnp.float32


def shift_z(x, by):
    return lax.ppermute(x, "mp", [(i, (i + by) % SIDE) for i in range(SIDE)])


def dp_index(y, x, core):
    return (y * SIDE + x) * 2 + core


def shift_x(a, by):
    pairs = [
        (dp_index(y, x, c), dp_index(y, (x + by) % SIDE, c))
        for y in range(SIDE)
        for x in range(SIDE)
        for c in range(2)
    ]
    return lax.ppermute(a, "dp", pairs)


def shift_y(a, by):
    pairs = [
        (dp_index(y, x, c), dp_index((y + by) % SIDE, x, c))
        for y in range(SIDE)
        for x in range(SIDE)
        for c in range(2)
    ]
    return lax.ppermute(a, "dp", pairs)


def swap_core(a):
    return lax.ppermute(a, "dp", [(i, i ^ 1) for i in range(32)])


def place():
    i = lax.axis_index("dp")
    return i // (2 * SIDE), (i // 2) % SIDE, i % 2


def gather_z(x):
    half = x.shape[0] // 2
    before = shift_z(x, 1)
    after = shift_z(x, -1)
    far_top = shift_z(before[:half], 1)
    far_bottom = shift_z(after[half:], -1)
    return jnp.concatenate([x, before, after, far_top, far_bottom], axis=0)


def scatter_z(parts):
    own, before, after, far = (parts[k * PART : (k + 1) * PART] for k in range(4))
    half = PART // 2
    far_low = far.astype(BF16)
    got_top = shift_z(far_low[:half], 1)
    got_bottom = shift_z(far_low[half:], -1)
    to_after = jnp.concatenate([after[:half] + got_top.astype(F32), after[half:]], axis=0)
    to_before = jnp.concatenate([before[:half], before[half:] + got_bottom.astype(F32)], axis=0)
    from_before = shift_z(to_after.astype(BF16), 1)
    from_after = shift_z(to_before.astype(BF16), -1)
    return own + from_before.astype(F32) + from_after.astype(F32)


def spread(x, move, at):
    out = jnp.zeros((SIDE, *x.shape), x.dtype)
    out = lax.dynamic_update_index_in_dim(out, x, at, 0)
    for by in (1, -1, 2):
        out = lax.dynamic_update_index_in_dim(out, move(x, by), (at - by) % SIDE, 0)
    return out


def gather_dp(x, first):
    y, xx, core = place()
    if first == "x":
        blocks = spread(spread(x, shift_x, xx), shift_y, y)
    else:
        blocks = jnp.swapaxes(spread(spread(x, shift_y, y), shift_x, xx), 0, 1)
    blocks = blocks.reshape(SIDE * SIDE, *x.shape)
    other = swap_core(blocks)
    pair = jnp.zeros((SIDE * SIDE, 2, *x.shape), x.dtype)
    pair = lax.dynamic_update_index_in_dim(pair, blocks, core, 1)
    pair = lax.dynamic_update_index_in_dim(pair, other, 1 - core, 1)
    return pair.reshape(-1, x.shape[1])


def collect(x, move, at, dim):
    total = lax.dynamic_index_in_dim(x, at, dim, keepdims=False).astype(F32)
    for by in (1, -1, 2):
        piece = lax.dynamic_index_in_dim(x, (at + by) % SIDE, dim, keepdims=False)
        total = total + move(piece, by).astype(F32)
    return total


def scatter_dp(g, first):
    y, xx, core = place()
    n = g.shape[1]
    blocks = g.reshape(SIDE, SIDE, 2, 64, n)
    mine = lax.dynamic_index_in_dim(blocks, core, 2, keepdims=False)
    other = lax.dynamic_index_in_dim(blocks, 1 - core, 2, keepdims=False)
    both = (mine.astype(F32) + swap_core(other).astype(F32)).astype(BF16)
    if first == "x":
        line = collect(both, shift_x, xx, 1).astype(BF16)
        return collect(line, shift_y, y, 0)
    line = collect(both, shift_y, y, 0).astype(BF16)
    return collect(line, shift_x, xx, 0)


def turn(x, cosine, sine):
    lane = lax.broadcasted_iota(jnp.int32, x.shape, 1)
    ahead = pltpu.roll(x, 96, 1)
    behind = pltpu.roll(x, 32, 1)
    return x * cosine + jnp.where(lane % HEAD_DIM < HEAD_DIM // 2, ahead, behind) * sine


def nt(a, b):
    return lax.dot_general(a, b, (((1,), (1,)), ((), ())), preferred_element_type=F32)


def tn(a, b):
    return lax.dot_general(a, b, (((0,), (0,)), ((), ())), preferred_element_type=F32)


def nn(a, b):
    return lax.dot_general(a, b, (((1,), (0,)), ((), ())), preferred_element_type=F32)


def make_bias(tok_q, tok_k, seg_q, seg_k):
    allowed = (seg_q == seg_k) & (tok_k <= tok_q)
    return jnp.where(allowed, 0.0, -1e30)


def forward_kernel(
    qkv_ref, cos_ref, sin_ref, tokq_ref, tokk_ref, segq_ref, segk_ref,
    att_ref, q_ref, kv_ref, lse_ref, bias_ref,
):
    cosine, sine = cos_ref[...], sin_ref[...]
    for pair in range(HEADS_LOCAL // 2):
        cols = slice(pair * 128, pair * 128 + 128)
        q_ref[:, cols] = (turn(qkv_ref[:, cols], cosine, sine).astype(BF16)) * BF16(0.125)
    kv = qkv_ref[:, QUERY_COLS:QKV_COLS]
    lane = lax.broadcasted_iota(jnp.int32, kv.shape, 1)
    kv = jnp.where(lane < HEAD_DIM, turn(kv, cosine, sine), kv).astype(BF16)
    kv_ref[...] = kv
    keys, values = kv[:, :HEAD_DIM], kv[:, HEAD_DIM:]
    bias_ref[...] = make_bias(tokq_ref[...], tokk_ref[...], segq_ref[...], segk_ref[...])
    for block in range(SEQ // PART):
        rows = slice(block * PART, block * PART + PART)
        bias = bias_ref[rows, :]
        outs, sums = [], []
        for h in range(HEADS_LOCAL):
            q = q_ref[rows, h * HEAD_DIM : (h + 1) * HEAD_DIM]
            s = nt(q, keys) + bias
            top = jnp.max(s, axis=1, keepdims=True)
            e = jnp.exp(s - top)
            total = jnp.sum(e, axis=1, keepdims=True)
            p = (e * (1.0 / total)).astype(BF16)
            outs.append(nn(p, values).astype(BF16))
            sums.append(top + jnp.log(total))
        att_ref[rows, :] = jnp.concatenate(outs, axis=1)
        lse_ref[rows, :] = jnp.concatenate(sums, axis=1)


def backward_kernel(
    q_ref, kv_ref, lse_ref, up_ref, cos_ref, sin_ref, tokq_ref, tokk_ref, segq_ref, segk_ref,
    out_ref, bias_ref, dkv_ref,
):
    cosine, sine = cos_ref[...], -sin_ref[...]
    kv = kv_ref[...]
    keys, values = kv[:, :HEAD_DIM], kv[:, HEAD_DIM:]
    bias_ref[...] = make_bias(tokq_ref[...], tokk_ref[...], segq_ref[...], segk_ref[...])
    dkv_ref[...] = jnp.zeros_like(dkv_ref)
    for block in range(SEQ // PART):
        rows = slice(block * PART, block * PART + PART)
        bias = bias_ref[rows, :]
        dqs = []
        dk = jnp.zeros((SEQ, HEAD_DIM), F32)
        dv = jnp.zeros((SEQ, HEAD_DIM), F32)
        for h in range(HEADS_LOCAL):
            cols = slice(h * HEAD_DIM, (h + 1) * HEAD_DIM)
            q, up = q_ref[rows, cols], up_ref[rows, cols]
            s = nt(q, keys) + bias
            p = jnp.exp(s - lse_ref[rows, h : h + 1])
            dp = nt(up, values)
            inner = jnp.sum(p * dp, axis=1, keepdims=True)
            ds = (p * (dp - inner)).astype(BF16)
            dqs.append(nn(ds, keys) * 0.125)
            dk = dk + tn(ds, q)
            dv = dv + tn(p.astype(BF16), up)
        dkv_ref[...] += jnp.concatenate([dk, dv], axis=1)
        for pair in range(HEADS_LOCAL // 2):
            dq = jnp.concatenate(dqs[2 * pair : 2 * pair + 2], axis=1)
            dq = turn(dq, cosine[rows], sine[rows])
            out_ref[rows, pair * 128 : pair * 128 + 128] = dq.astype(BF16)
    dkv = dkv_ref[...]
    lane = lax.broadcasted_iota(jnp.int32, dkv.shape, 1)
    dkv = jnp.where(lane < HEAD_DIM, turn(dkv, cosine, sine), dkv)
    out_ref[:, QUERY_COLS:QKV_COLS] = dkv.astype(BF16)


def whole(n):
    return [pl.BlockSpec(memory_space=pltpu.VMEM)] * n


def attend_forward(qkv, tables):
    return pl.pallas_call(
        forward_kernel,
        out_shape=(
            jax.ShapeDtypeStruct((SEQ, QUERY_COLS), BF16),
            jax.ShapeDtypeStruct((SEQ, QUERY_COLS), BF16),
            jax.ShapeDtypeStruct((SEQ, 128), BF16),
            jax.ShapeDtypeStruct((SEQ, HEADS_LOCAL), F32),
        ),
        in_specs=whole(7),
        out_specs=whole(4),
        scratch_shapes=[pltpu.VMEM((SEQ, SEQ), F32)],
        compiler_params=pltpu.CompilerParams(vmem_limit_bytes=24 * 2**20),
        cost_estimate=pl.CostEstimate(
            flops=4 * HEADS_LOCAL * SEQ * SEQ * HEAD_DIM,
            bytes_accessed=4 * 2**20,
            transcendentals=HEADS_LOCAL * SEQ * SEQ,
        ),
    )(qkv, *tables)


def attend_backward(q, kv, lse, upstream, tables):
    return pl.pallas_call(
        backward_kernel,
        out_shape=jax.ShapeDtypeStruct((SEQ, QKV_COLS), BF16),
        in_specs=whole(10),
        out_specs=pl.BlockSpec(memory_space=pltpu.VMEM),
        scratch_shapes=[pltpu.VMEM((SEQ, SEQ), F32), pltpu.VMEM((SEQ, 128), F32)],
        compiler_params=pltpu.CompilerParams(vmem_limit_bytes=24 * 2**20),
        cost_estimate=pl.CostEstimate(
            flops=10 * HEADS_LOCAL * SEQ * SEQ * HEAD_DIM,
            bytes_accessed=4 * 2**20,
            transcendentals=HEADS_LOCAL * SEQ * SEQ,
        ),
    )(q, kv, lse, upstream, *tables)


def attention_tables(lengths):
    z = lax.axis_index("mp")
    block = jnp.stack([z, (z + 3) % SIDE, (z + 1) % SIDE, (z + 2) % SIDE])
    token = (block[:, None] * PART + jnp.arange(PART)[None, :]).reshape(SEQ)
    boundary = jnp.cumsum(lengths)
    starts = boundary - lengths
    segment = jnp.sum((token[:, None] >= boundary[None, :]).astype(jnp.int32), axis=1)
    leading = jnp.max(jnp.where(starts[None, :] <= token[:, None], starts[None, :], 0), axis=1)
    indices = jnp.arange(HEAD_DIM // 2).astype(F32)
    frequency = 1.0 / THETA ** (2.0 * indices / HEAD_DIM)
    angles = (token - leading).astype(F32)[:, None] * frequency[None, :]
    cosine, sine = jnp.cos(angles), jnp.sin(angles)
    cosine = jnp.concatenate([cosine] * 4, axis=1)
    sine = jnp.concatenate([-sine, sine, -sine, sine], axis=1)
    return (cosine, sine, token[:, None], token[None, :], segment[:, None], segment[None, :])


def adamw(weight, gradient, moment, square, rate, decay):
    momentum = BETA_ONE * moment + (1.0 - BETA_ONE) * gradient
    variance = BETA_TWO * square + (1.0 - BETA_TWO) * gradient * gradient
    moment_hat = momentum / (1.0 - BETA_ONE**STEP)
    square_hat = variance / (1.0 - BETA_TWO**STEP)
    updated = weight - rate * (moment_hat / (jnp.sqrt(square_hat) + ADAM_EPS) + decay * weight)
    return (momentum, variance, updated)


def inverse_rms(v):
    return lax.rsqrt(jnp.mean(v * v, axis=-1, keepdims=True) + EPS)


def norm_backward(v, inverse, upstream):
    inner = jnp.mean(upstream * v, axis=-1, keepdims=True)
    return inverse * upstream - v * (inverse * inverse * inverse * inner)


def after(x, *others):
    return lax.optimization_barrier((x, *others))[0]


def on_device(
    residual, cotangent, document_lengths,
    norm_gains, query_weight, keyvalue_weight, output_weight, gateup_weight, down_weight,
    moment_gains, moment_query, moment_keyvalue, moment_output, moment_gateup, moment_down,
    square_gains, square_query, square_keyvalue, square_output, square_gateup, square_down,
):
    residual, cotangent = residual[0], cotangent[0]
    low_gains = norm_gains.astype(BF16).astype(F32)
    gain_one, gain_two = low_gains[0][:, None], low_gains[1][:, None]
    low_qkv = jnp.concatenate(
        (query_weight, keyvalue_weight[0], keyvalue_weight[1]), axis=1
    ).astype(BF16)
    low_gateup = jnp.concatenate((gateup_weight[0], gateup_weight[1]), axis=1).astype(BF16)
    low_output = output_weight.astype(BF16).T
    low_down = down_weight.astype(BF16).T

    scaled_qkv = (low_qkv.astype(F32) * gain_one).astype(BF16)
    scaled_gateup = (low_gateup.astype(F32) * gain_two).astype(BF16)

    ffn_full = lax.all_gather(
        jnp.concatenate((scaled_gateup, low_down), axis=1), "dp", axis=0, tiled=True
    )
    gateup_full = ffn_full[:, : 2 * HIDDEN]
    down_full = ffn_full[:, 2 * HIDDEN :]
    qkv_full = gather_dp(scaled_qkv, "x")
    output_full = gather_dp(low_output, "y")

    inverse_one = inverse_rms(residual)
    rows_one = gather_z((residual * inverse_one).astype(BF16))
    tables = attention_tables(document_lengths[0])
    attended, q, kv, lse = attend_forward(nn(rows_one, qkv_full), tables)
    attention = scatter_z(nt(attended, output_full))
    middle = residual + attention
    inverse_two = inverse_rms(middle)
    rows_two = gather_z((middle * inverse_two).astype(BF16))
    cot_rows = gather_z(after(cotangent.astype(BF16), rows_one))

    gate_up = nn(rows_two, gateup_full)
    gate, up = gate_up[:, :HIDDEN], gate_up[:, HIDDEN:]
    sigmoid = jax.nn.sigmoid(gate)
    activated = gate * sigmoid
    hidden = (activated * up).astype(BF16)
    grad_hidden = nn(cot_rows, down_full)
    slope = sigmoid * (1.0 + gate * (1.0 - sigmoid))
    grad_gate = (grad_hidden * up * slope).astype(BF16)
    grad_up = (grad_hidden * activated).astype(BF16)
    grad_gateup = jnp.concatenate((grad_gate, grad_up), axis=1)

    grad_normed_two = scatter_z(nt(grad_gateup, gateup_full))
    grad_down = lax.psum_scatter(
        tn(cot_rows, hidden).astype(BF16), "dp", scatter_dimension=0, tiled=True
    ).astype(F32)
    grad_ffn = lax.psum_scatter(
        tn(rows_two, grad_gateup).astype(BF16), "dp", scatter_dimension=0, tiled=True
    ).astype(F32)
    feedfwd = scatter_z(nt(hidden, down_full))
    block_output = middle + feedfwd

    grad_middle = cotangent + norm_backward(middle, inverse_two, grad_normed_two)
    attention_rows = gather_z(grad_middle.astype(BF16))
    grad_attended = nn(attention_rows, output_full).astype(BF16)
    grad_output = scatter_dp(tn(attention_rows, attended).astype(BF16), "y")
    grad_projected = attend_backward(q, kv, lse, grad_attended, tables)
    grad_qkv = scatter_dp(tn(rows_one, grad_projected).astype(BF16), "x")
    grad_normed_one = scatter_z(nt(grad_projected, qkv_full))
    input_gradient = grad_middle + norm_backward(residual, inverse_one, grad_normed_one)

    gain_parts = jnp.stack(
        (
            jnp.sum(low_qkv.astype(F32) * grad_qkv, axis=1),
            jnp.sum(low_gateup.astype(F32) * grad_ffn, axis=1),
        )
    )
    gains = gain_parts + shift_z(gain_parts, 1) + shift_z(gain_parts, -1) + shift_z(gain_parts, 2)
    grad_qkv = grad_qkv * gain_one
    grad_ffn = grad_ffn * gain_two
    reduced = (
        gains,
        grad_qkv[:, :QUERY_COLS],
        jnp.stack((grad_qkv[:, QUERY_COLS : QUERY_COLS + 64], grad_qkv[:, QUERY_COLS + 64 :])),
        grad_output.T,
        jnp.stack((grad_ffn[:, :HIDDEN], grad_ffn[:, HIDDEN:])),
        grad_down.T,
    )
    masters = (norm_gains, query_weight, keyvalue_weight, output_weight, gateup_weight, down_weight)
    moments = (
        moment_gains, moment_query, moment_keyvalue, moment_output, moment_gateup, moment_down,
    )
    squares = (
        square_gains, square_query, square_keyvalue, square_output, square_gateup, square_down,
    )
    results = [
        adamw(masters[i], reduced[i], moments[i], squares[i], RATES[i], DECAYS[i]) for i in range(6)
    ]
    return (
        block_output[None],
        input_gradient[None],
        *reduced,
        *(r[0] for r in results),
        *(r[1] for r in results),
        *(r[2] for r in results),
    )


def solution(mesh):
    rows = P("dp", "mp", None)
    weights = (
        P(None, "dp"),
        P("dp", "mp"),
        P(None, "dp", "mp"),
        P("mp", "dp"),
        P(None, "dp", "mp"),
        P("mp", "dp"),
    )
    return jax.shard_map(
        on_device,
        mesh=mesh,
        in_specs=(rows, rows, P("dp", None), *weights, *weights, *weights),
        out_specs=(rows, rows, *weights, *weights, *weights, *weights),
        check_vma=False,
    )
```

```python
import functools

import jax
import jax.numpy as jnp
from jax import lax
from jax.experimental import pallas as pl
from jax.experimental.pallas import tpu as pltpu
from jax.sharding import PartitionSpec as P

HEAD_DIM = 64
HEADS_LOCAL = 8
QUERY_COLS = 512
QKV_COLS = 640
HIDDEN = 1408
SEQ = 512
PART = 128
D = 2048
STEP = 10

EPS = 1e-05
THETA = 10000.0
BETA_ONE = 0.9
BETA_TWO = 0.95
ADAM_EPS = 1e-08
RATES = (1.0, 0.05, 0.05, 0.5, 0.05, 0.025)
DECAYS = (0.0, 0.1, 0.1, 0.1, 0.1, 0.1)
SIDE = 4
BF16 = jnp.bfloat16
F32 = jnp.float32
SPLIT = 768


def cost(us):
    return pl.CostEstimate(
        flops=int(us * 1.1e9), bytes_accessed=int(us * 3.0e6), transcendentals=0
    )


def pair_mask(core, step):
    return (1, 3)[step] if core == 0 else (3, 1)[step]


def dp_index(y, x, core):
    return (y * SIDE + x) * 2 + core


def chips():
    return [(y, x, c) for y in range(SIDE) for x in range(SIDE) for c in range(2)]


def pair_z(a, step):
    pairs = [
        (dp * SIDE + z, dp * SIDE + (z ^ pair_mask(dp % 2, step)))
        for dp in range(2 * SIDE * SIDE)
        for z in range(SIDE)
    ]
    return lax.ppermute(a, ("dp", "mp"), pairs)


def pair_x(a, step):
    pairs = [(dp_index(y, x, c), dp_index(y, x ^ pair_mask(c, step), c)) for y, x, c in chips()]
    return lax.ppermute(a, "dp", pairs)


def pair_y(a, step):
    pairs = [(dp_index(y, x, c), dp_index(y ^ pair_mask(c, step), x, c)) for y, x, c in chips()]
    return lax.ppermute(a, "dp", pairs)


def shift_z(x, by):
    return lax.ppermute(x, "mp", [(i, (i + by) % SIDE) for i in range(SIDE)])


def shift_first(a, by):
    pairs = [
        (dp_index(y, x, c), dp_index((y + by) % SIDE, x, c) if c else dp_index(y, (x + by) % SIDE, c))
        for y, x, c in chips()
    ]
    return lax.ppermute(a, "dp", pairs)


def shift_second(a, by):
    pairs = [
        (dp_index(y, x, c), dp_index(y, (x + by) % SIDE, c) if c else dp_index((y + by) % SIDE, x, c))
        for y, x, c in chips()
    ]
    return lax.ppermute(a, "dp", pairs)


def swap_core(a):
    return lax.ppermute(a, "dp", [(i, i ^ 1) for i in range(2 * SIDE * SIDE)])


def place():
    i = lax.axis_index("dp")
    return i // (2 * SIDE), (i // 2) % SIDE, i % 2


def here():
    return jnp.stack(place()).astype(jnp.int32)


def pick(k, values):
    out = jnp.int32(values[0])
    for i in range(1, len(values)):
        out = jnp.where(k == i, values[i], out)
    return out


def pair_steps(core):
    return jnp.where(core == 0, jnp.array([0, 1, 3, 2]), jnp.array([0, 3, 1, 2])).astype(jnp.int32)


def split_sum(near, got):
    k = near.shape[0] // 2
    keep = near[:k].astype(F32) + got[:k].astype(F32)
    return keep, (near[k:].astype(F32) + got[k:].astype(F32)).astype(BF16)


def place_kernel(here_ref, mine_ref, other_ref, qkv_ref, output_ref):
    y, x, core = here_ref[0], here_ref[1], here_ref[2]

    @pl.loop(0, SIDE * SIDE)
    def _(k):
        first, second = pick(k // SIDE, (0, 3, 1, 2)), pick(k % SIDE, (0, 3, 1, 2))
        for own, blocks_ref in ((True, mine_ref), (False, other_ref)):
            c = core if own else 1 - core
            along_x, along_y = jnp.where(c == 0, first, second), jnp.where(c == 0, second, first)
            chip = ((y + along_y) % SIDE) * SIDE + (x + along_x) % SIDE
            qkv_ref[chip, c] = blocks_ref[k, :, :QKV_COLS]
            output_ref[chip, c] = blocks_ref[k, :, QKV_COLS:]


def place_attention(mine, other):
    parts = pl.pallas_call(
        place_kernel,
        out_shape=[
            jax.ShapeDtypeStruct((SIDE * SIDE, 2, 64, n), mine.dtype)
            for n in (QKV_COLS, QUERY_COLS)
        ],
        in_specs=[pl.BlockSpec(memory_space=pltpu.SMEM)] + whole(2),
        out_specs=whole(2),
        compiler_params=pltpu.CompilerParams(vmem_limit_bytes=32 * 2**20),
        cost_estimate=cost(3),
    )(here(), mine, other)
    return [p.reshape(D, -1) for p in parts]


def fold_kernel(x_first, here_ref, mine_ref, got_ref, near_ref, far_ref):
    y, x, core = here_ref[0], here_ref[1], here_ref[2]
    steps = lambda k: pick(k, (0, jnp.where(core == 0, 1, 3), jnp.where(core == 0, 3, 1), 2))

    def chip(k):
        first, second = steps(k // SIDE), steps(k % SIDE)
        if x_first:
            return (y ^ second) * SIDE + (x ^ first)
        return (y ^ first) * SIDE + (x ^ second)

    @pl.loop(0, 2 * SIDE)
    def _(k):
        i, j = chip(k), chip(2 * SIDE + k)
        near_ref[k] = (mine_ref[i].astype(F32) + got_ref[i].astype(F32)).astype(BF16)
        far_ref[k] = (mine_ref[j].astype(F32) + got_ref[j].astype(F32)).astype(BF16)


def fold(mine, got, x_first, us):
    n = mine.shape[2]
    return pl.pallas_call(
        functools.partial(fold_kernel, x_first),
        out_shape=[jax.ShapeDtypeStruct((2 * SIDE, 64, n), BF16)] * 2,
        in_specs=[pl.BlockSpec(memory_space=pltpu.SMEM)] + whole(2),
        out_specs=whole(2),
        compiler_params=pltpu.CompilerParams(vmem_limit_bytes=32 * 2**20),
        cost_estimate=cost(us),
    )(here(), mine, got)


def pair_first(a, step, x_first):
    return (pair_x if x_first else pair_y)(a, step)


def pair_second(a, step, x_first):
    return (pair_y if x_first else pair_x)(a, step)


def scatter_second(line, x_first):
    keep, sent = split_sum(line[:2], pair_second(line[2:], 1, x_first))
    return keep[0] + pair_second(sent, 0, x_first)[0].astype(F32)


def nt(a, b):
    return lax.dot_general(a, b, (((1,), (1,)), ((), ())), preferred_element_type=F32)


def tn(a, b):
    return lax.dot_general(a, b, (((0,), (0,)), ((), ())), preferred_element_type=F32)


def nn(a, b):
    return lax.dot_general(a, b, (((1,), (0,)), ((), ())), preferred_element_type=F32)


def whole(n):
    return [pl.BlockSpec(memory_space=pltpu.VMEM)] * n


def prepare_kernel(
    gains_ref, query_ref, keyvalue_ref, output_ref, gateup_ref, down_ref, part_ref, ffn_ref
):
    gains = gains_ref[...].astype(BF16).astype(F32)
    scaled = lambda k, w: (w.astype(BF16).astype(F32) * gains[:, k : k + 1]).astype(BF16)
    part_ref[:, :QUERY_COLS] = scaled(0, query_ref[...])
    part_ref[:, QUERY_COLS:QKV_COLS] = scaled(
        0, jnp.concatenate([keyvalue_ref[0], keyvalue_ref[1]], axis=1)
    )
    part_ref[:, QKV_COLS:] = output_ref[...].astype(BF16)
    ffn_ref[:, :HIDDEN] = scaled(1, gateup_ref[0])
    ffn_ref[:, HIDDEN : 2 * HIDDEN] = scaled(1, gateup_ref[1])
    ffn_ref[:, 2 * HIDDEN :] = down_ref[...].astype(BF16)


def prepare(norm_gains, query, keyvalue, output, gateup, down):
    return pl.pallas_call(
        prepare_kernel,
        out_shape=[
            jax.ShapeDtypeStruct((64, QKV_COLS + QUERY_COLS), BF16),
            jax.ShapeDtypeStruct((64, 3 * HIDDEN), BF16),
        ],
        in_specs=whole(6),
        out_specs=whole(2),
        compiler_params=pltpu.CompilerParams(vmem_limit_bytes=16 * 2**20),
        cost_estimate=cost(2),
    )(norm_gains.T, query, keyvalue, output.T, gateup, down.T)


def back_kernel(gate_ref, up_ref, gate_w_ref, up_w_ref, near_ref, far_ref):
    out = nt(gate_ref[...], gate_w_ref[...]) + nt(up_ref[...], up_w_ref[...])
    near_ref[...] = out[: SEQ // 2]
    far_ref[...] = out[SEQ // 2 :].astype(BF16)


def back_to_rows(grad_gate, grad_up, weights):
    tile = 512
    grad = pl.BlockSpec((SEQ, HIDDEN), lambda i: (0, 0))
    weight = lambda at: pl.BlockSpec((tile, HIDDEN), lambda i: (i, at))
    out = pl.BlockSpec((SEQ // 2, tile), lambda i: (0, i))
    return pl.pallas_call(
        back_kernel,
        out_shape=[jax.ShapeDtypeStruct((SEQ // 2, D), t) for t in (F32, BF16)],
        grid=(D // tile,),
        in_specs=[grad, grad, weight(0), weight(1)],
        out_specs=[out, out],
        compiler_params=pltpu.CompilerParams(vmem_limit_bytes=32 * 2**20),
        cost_estimate=cost(10),
    )(grad_gate, grad_up, weights, weights)


def turn_kernel(a_ref, turned_ref):
    turned_ref[...] = a_ref[...].T


def turned(a):
    return pl.pallas_call(
        turn_kernel,
        out_shape=jax.ShapeDtypeStruct((D, SEQ), BF16),
        in_specs=whole(1),
        out_specs=whole(1)[0],
        compiler_params=pltpu.CompilerParams(vmem_limit_bytes=16 * 2**20),
        cost_estimate=cost(1),
    )(a)


def weights_kernel(at, core_ref, a_ref, b_ref, c_ref, d_ref, mine_ref, other_ref):
    first = core_ref[0] == 0
    n = b_ref.shape[1]

    @pl.loop(0, D // 256)
    def _(chunk):
        rows = pl.ds(pl.multiple_of(chunk * 256, 256), 256)
        out = nn(a_ref[rows, :], b_ref[...]).astype(BF16)
        more = nn(c_ref[rows, :], d_ref[:, at]).astype(BF16)
        for k in range(2):
            for cols, full in ((slice(0, n), out), (slice(n, None), more)):
                low, high = full[k * 128 : k * 128 + 64], full[k * 128 + 64 : k * 128 + 128]
                mine_ref[chunk * 2 + k, :, cols] = jnp.where(first, low, high)
                other_ref[chunk * 2 + k, :, cols] = jnp.where(first, high, low)


def weight_gradients(a, b, c, d, at):
    n = b.shape[1] + at.stop - at.start
    _, _, core = place()
    return pl.pallas_call(
        functools.partial(weights_kernel, at),
        out_shape=[jax.ShapeDtypeStruct((SIDE * SIDE, 64, n), BF16)] * 2,
        in_specs=[pl.BlockSpec(memory_space=pltpu.SMEM)] + whole(4),
        out_specs=whole(2),
        compiler_params=pltpu.CompilerParams(vmem_limit_bytes=40 * 2**20),
        cost_estimate=cost(8),
    )(core[None], a, b, c, d)


def by_chip(g):
    _, _, core = place()
    g = g.reshape(SIDE * SIDE, 2, 64, g.shape[1])
    pick = lambda c: lax.dynamic_index_in_dim(g, c, 1, keepdims=False)
    return pick(core), pick(1 - core)


def hidden_kernel(
    near_ref, far_ref, gate_w_ref, up_w_ref, grad_hidden_ref,
    hidden_ref, grad_gate_ref, grad_up_ref, rows_ref,
):
    @pl.when(pl.program_id(0) == 0)
    def _():
        rows_ref[: SEQ // 2, :] = near_ref[...]
        rows_ref[SEQ // 2 :, :] = far_ref[...]

    gate_up = nn(rows_ref[...], jnp.concatenate([gate_w_ref[...], up_w_ref[...]], axis=1))
    grad_hidden = grad_hidden_ref[...]
    gate, up = gate_up[:, :128], gate_up[:, 128:]
    sigmoid = 1.0 / (1.0 + jnp.exp(-gate))
    activated = gate * sigmoid
    slope = sigmoid * (1.0 + gate * (1.0 - sigmoid))
    hidden_ref[...] = (activated * up).astype(BF16)
    grad_gate_ref[...] = (grad_hidden * up * slope).astype(BF16)
    grad_up_ref[...] = (grad_hidden * activated).astype(BF16)


def hidden_units(near, far, grad_hidden, weights):
    steps = HIDDEN // 128
    weight = lambda at: pl.BlockSpec((D, 128), lambda j: (0, at * steps + j))
    return pl.pallas_call(
        hidden_kernel,
        out_shape=[jax.ShapeDtypeStruct((SEQ, HIDDEN), BF16)] * 3,
        grid=(steps,),
        in_specs=[pl.BlockSpec((SEQ // 2, D), lambda j: (0, 0))] * 2
        + [weight(0), weight(1), pl.BlockSpec((SEQ, 128), lambda j: (0, j))],
        out_specs=[pl.BlockSpec((SEQ, 128), lambda j: (0, j))] * 3,
        scratch_shapes=[pltpu.VMEM((SEQ, D), BF16)],
        compiler_params=pltpu.CompilerParams(vmem_limit_bytes=24 * 2**20),
        cost_estimate=cost(10),
    )(near, far, weights, weights, grad_hidden)


def turn(x, cosine, sine):
    lane = lax.broadcasted_iota(jnp.int32, x.shape, 1)
    ahead = pltpu.roll(x, 96, 1)
    behind = pltpu.roll(x, 32, 1)
    return x * cosine + jnp.where(lane % HEAD_DIM < HEAD_DIM // 2, ahead, behind) * sine


def mask_bias(ends_ref, block):
    shape = ((block + 1) * PART, PART)
    key = lax.broadcasted_iota(jnp.int32, shape, 0)
    query = lax.broadcasted_iota(jnp.int32, shape, 1) + block * PART
    key_segment = jnp.zeros(shape, jnp.int32)
    query_segment = jnp.zeros(shape, jnp.int32)
    for d in range(4):
        key_segment += (key >= ends_ref[d]).astype(jnp.int32)
        query_segment += (query >= ends_ref[d]).astype(jnp.int32)
    return jnp.where((key_segment == query_segment) & (key <= query), 0.0, -1e30)


def halves(x):
    none = jnp.zeros_like(x)
    return jnp.concatenate([x, none], axis=1), jnp.concatenate([none, x], axis=1)


def in_token_order(slot_ref, kv_ref, ordered_ref):
    for block in range(SIDE):
        rows = pl.ds(pl.multiple_of(slot_ref[block] * PART, PART), PART)
        ordered_ref[block * PART : (block + 1) * PART, :] = kv_ref[rows, :]


def forward_kernel(
    slot_ref, ends_ref, qkv_ref, cos_ref, sin_ref, att_ref, q_ref, kv_ref, lse_ref, ordered_ref
):
    cosine, sine = cos_ref[...], sin_ref[...]
    for pair in range(HEADS_LOCAL // 2):
        cols = slice(pair * 128, pair * 128 + 128)
        q_ref[:, cols] = (turn(qkv_ref[:, cols], cosine, sine).astype(BF16)) * BF16(0.125)
    kv = qkv_ref[:, QUERY_COLS:QKV_COLS]
    lane = lax.broadcasted_iota(jnp.int32, kv.shape, 1)
    kv_ref[...] = jnp.where(lane < HEAD_DIM, turn(kv, cosine, sine), kv).astype(BF16)
    in_token_order(slot_ref, kv_ref, ordered_ref)
    kv = ordered_ref[...]
    keys_both = halves(kv[:, :HEAD_DIM])
    values_turned = kv.astype(F32).T[HEAD_DIM:].astype(BF16)
    for block in range(SIDE):
        seen = (block + 1) * PART
        rows = pl.ds(pl.multiple_of(slot_ref[block] * PART, PART), PART)
        bias = mask_bias(ends_ref, block)
        for pair in range(HEADS_LOCAL // 2):
            cols = slice(pair * 128, pair * 128 + 128)
            q = q_ref[rows, cols]
            outs = []
            for h in range(2):
                s = nt(keys_both[h][:seen], q) + bias
                top = jnp.max(s, axis=0, keepdims=True)
                e = jnp.exp(s - top)
                total = jnp.sum(e, axis=0, keepdims=True)
                p = (e * (1.0 / total)).astype(BF16)
                outs.append(nn(values_turned[:, :seen], p))
                lse_ref[2 * pair + h : 2 * pair + h + 1, block * PART : seen] = top + jnp.log(total)
            att_ref[rows, cols] = jnp.concatenate(outs, axis=0).T.astype(BF16)


def backward_kernel(
    slot_ref, ends_ref, q_ref, kv_ref, lse_ref, up_ref, cos_ref, sin_ref,
    out_ref, ordered_ref, dk_ref, dv_ref,
):
    in_token_order(slot_ref, kv_ref, ordered_ref)
    kv = ordered_ref[...]
    keys_both, values_both = halves(kv[:, :HEAD_DIM]), halves(kv[:, HEAD_DIM:])
    keys_turned = kv.astype(F32).T[:HEAD_DIM].astype(BF16)
    dk_ref[...] = jnp.zeros_like(dk_ref)
    dv_ref[...] = jnp.zeros_like(dv_ref)
    lane = lax.broadcasted_iota(jnp.int32, (PART, 128), 1)
    for block in range(SIDE):
        seen = (block + 1) * PART
        rows = pl.ds(pl.multiple_of(slot_ref[block] * PART, PART), PART)
        bias = mask_bias(ends_ref, block)
        cosine, sine = cos_ref[rows, :], -sin_ref[rows, :]
        for pair in range(HEADS_LOCAL // 2):
            cols = slice(pair * 128, pair * 128 + 128)
            q, up = q_ref[rows, cols], up_ref[rows, cols]
            dqs, ps, dss = [], [], []
            for h in range(2):
                s = nt(keys_both[h][:seen], q) + bias
                p = jnp.exp(s - lse_ref[2 * pair + h : 2 * pair + h + 1, block * PART : seen])
                dp = nt(values_both[h][:seen], up)
                inner = jnp.sum(p * dp, axis=0, keepdims=True)
                ds = (p * (dp - inner)).astype(BF16)
                dqs.append(nn(keys_turned[:, :seen], ds))
                ps.append(p.astype(BF16))
                dss.append(ds)
            none = jnp.zeros_like(q)
            q_apart = jnp.concatenate(
                [jnp.where(lane < HEAD_DIM, q, none), jnp.where(lane < HEAD_DIM, none, q)], axis=0
            )
            up_apart = jnp.concatenate(
                [jnp.where(lane < HEAD_DIM, up, none), jnp.where(lane < HEAD_DIM, none, up)], axis=0
            )
            dk_ref[:seen, :] += nn(jnp.concatenate(dss, axis=1), q_apart)
            dv_ref[:seen, :] += nn(jnp.concatenate(ps, axis=1), up_apart)
            dq = jnp.concatenate(dqs, axis=0).T * 0.125
            out_ref[rows, cols] = turn(dq, cosine, sine).astype(BF16)
    lane = lax.broadcasted_iota(jnp.int32, (SEQ, 128), 1)
    dk, dv = dk_ref[...], dv_ref[...]
    dk, dv = dk + pltpu.roll(dk, HEAD_DIM, 1), dv + pltpu.roll(dv, HEAD_DIM, 1)
    dk_ref[...] = jnp.where(lane < HEAD_DIM, dk, dv)
    for block in range(SIDE):
        rows = pl.ds(pl.multiple_of(slot_ref[block] * PART, PART), PART)
        dkv = dk_ref[block * PART : (block + 1) * PART, :]
        turned = turn(dkv, cos_ref[rows, :], -sin_ref[rows, :])
        dkv = jnp.where(lane[:PART] < HEAD_DIM, turned, dkv)
        out_ref[rows, QUERY_COLS:QKV_COLS] = dkv.astype(BF16)


def small(n):
    return [pl.BlockSpec(memory_space=pltpu.SMEM)] * n


def attend_forward(qkv, tables):
    slot, ends, cosine, sine = tables
    return pl.pallas_call(
        forward_kernel,
        out_shape=(
            jax.ShapeDtypeStruct((SEQ, QUERY_COLS), BF16),
            jax.ShapeDtypeStruct((SEQ, QUERY_COLS), BF16),
            jax.ShapeDtypeStruct((SEQ, 128), BF16),
            jax.ShapeDtypeStruct((HEADS_LOCAL, SEQ), F32),
        ),
        in_specs=small(2) + whole(3),
        out_specs=whole(4),
        scratch_shapes=[pltpu.VMEM((SEQ, 128), BF16)],
        compiler_params=pltpu.CompilerParams(vmem_limit_bytes=24 * 2**20),
        cost_estimate=cost(8),
    )(slot, ends, qkv, cosine, sine)


def attend_backward(q, kv, lse, upstream, tables):
    slot, ends, cosine, sine = tables
    return pl.pallas_call(
        backward_kernel,
        out_shape=jax.ShapeDtypeStruct((SEQ, QKV_COLS), BF16),
        in_specs=small(2) + whole(6),
        out_specs=pl.BlockSpec(memory_space=pltpu.VMEM),
        scratch_shapes=[
            pltpu.VMEM((SEQ, 128), BF16),
            pltpu.VMEM((SEQ, 128), F32),
            pltpu.VMEM((SEQ, 128), F32),
        ],
        compiler_params=pltpu.CompilerParams(vmem_limit_bytes=24 * 2**20),
        cost_estimate=cost(10),
    )(slot, ends, q, kv, lse, upstream, cosine, sine)


def attention_tables(lengths):
    block = lax.axis_index("mp") ^ pair_steps(place()[2])
    slot = jnp.sum(
        jnp.where(block[None, :] == jnp.arange(SIDE)[:, None], jnp.arange(SIDE)[None, :], 0), axis=1
    ).astype(jnp.int32)
    token = (block[:, None] * PART + jnp.arange(PART)[None, :]).reshape(SEQ)
    ends = jnp.cumsum(lengths).astype(jnp.int32)
    starts = ends - lengths
    leading = jnp.max(jnp.where(starts[None, :] <= token[:, None], starts[None, :], 0), axis=1)
    indices = jnp.arange(HEAD_DIM // 2).astype(F32)
    frequency = 1.0 / THETA ** (2.0 * indices / HEAD_DIM)
    angles = (token - leading).astype(F32)[:, None] * frequency[None, :]
    cosine, sine = jnp.cos(angles), jnp.sin(angles)
    cosine = jnp.concatenate([cosine] * 4, axis=1)
    sine = jnp.concatenate([-sine, sine, -sine, sine], axis=1)
    return slot, ends, cosine, sine


def adamw(weight, gradient, moment, square, rate, decay):
    momentum = BETA_ONE * moment + (1.0 - BETA_ONE) * gradient
    variance = BETA_TWO * square + (1.0 - BETA_TWO) * gradient * gradient
    moment_hat = momentum / (1.0 - BETA_ONE**STEP)
    square_hat = variance / (1.0 - BETA_TWO**STEP)
    updated = weight - rate * (moment_hat / (jnp.sqrt(square_hat) + ADAM_EPS) + decay * weight)
    return (momentum, variance, updated)


def inverse_rms(v):
    return lax.rsqrt(jnp.mean(v * v, axis=-1, keepdims=True) + EPS)


def norm_backward(v, inverse, upstream):
    inner = jnp.mean(upstream * v, axis=-1, keepdims=True)
    return inverse * upstream - v * (inverse * inverse * inverse * inner)


def after(x, *others):
    return lax.optimization_barrier((x, *others))[0]


def on_device(
    residual, cotangent, document_lengths,
    norm_gains, query_weight, keyvalue_weight, output_weight, gateup_weight, down_weight,
    moment_gains, moment_query, moment_keyvalue, moment_output, moment_gateup, moment_down,
    square_gains, square_query, square_keyvalue, square_output, square_gateup, square_down,
):
    residual, cotangent = residual[0], cotangent[0]
    half = SEQ // 2

    inverse_one = inverse_rms(residual)
    normed_one = (residual * inverse_one).astype(BF16)
    one_near = jnp.concatenate([normed_one, pair_z(normed_one, 0)])
    part, ffn_part = prepare(
        norm_gains, after(query_weight, normed_one),
        keyvalue_weight, output_weight, gateup_weight, down_weight,
    )
    line = jnp.stack([part, shift_first(part, 1), shift_first(part, -1), shift_first(part, 2)])
    ffn_full = lax.all_gather(ffn_part, "dp", axis=0, tiled=True)
    tables = attention_tables(document_lengths[0])
    line = after(line, one_near, *tables)
    plane = [line, shift_second(line, 1), shift_second(line, -1), shift_second(line, 2)]
    one_far = pair_z(one_near, 1)
    low_cotangent = after(cotangent.astype(BF16), one_near)
    cot_near = jnp.concatenate([low_cotangent, pair_z(low_cotangent, 0)])
    mine = jnp.stack(plane, axis=1).reshape(SIDE * SIDE, *part.shape)
    mine = after(mine, one_far, cot_near)
    other = swap_core(mine)
    cot_far = pair_z(cot_near, 1)
    qkv_full, output_full = place_attention(mine, other)
    qkv = nn(one_near, qkv_full), nn(one_far, qkv_full)
    attended, q, kv, lse = attend_forward(jnp.concatenate(qkv), tables)

    far = nt(after(attended, cot_far)[half:], output_full).astype(BF16)
    got = pair_z(far, 1)
    near = nt(after(attended, far)[:half], output_full)
    cot_rows = jnp.concatenate([cot_near, cot_far])
    cot_turned = turned(after(cot_rows, near))
    keep, sent = split_sum(near, after(got, cot_turned))
    middle = residual + (keep + pair_z(sent, 0).astype(F32))
    inverse_two = inverse_rms(middle)
    normed_two = (middle * inverse_two).astype(BF16)
    got = pair_z(normed_two, 0)
    down_full = ffn_full[:, 2 * HIDDEN :]
    grad_hidden = nn(after(cot_rows, normed_two), down_full)
    two_near = jnp.concatenate([normed_two, after(got, grad_hidden)])
    two_far = pair_z(two_near, 1)

    hidden, grad_gate, grad_up = hidden_units(two_near, two_far, grad_hidden, ffn_full)
    near, far = back_to_rows(grad_gate, grad_up, ffn_full)
    got = pair_z(far, 1)
    rows_turned = turned(after(jnp.concatenate([two_near, two_far]), far))
    grad_a = weight_gradients(rows_turned, grad_gate, cot_turned, hidden, slice(0, SPLIT))
    grad_b = weight_gradients(
        rows_turned, after(grad_up, *grad_a), cot_turned, hidden, slice(SPLIT, HIDDEN)
    )
    keep, sent = split_sum(near, after(got, *grad_b))
    got = pair_z(sent, 0)
    got_a, got_b = swap_core(after(grad_a[1], sent)), swap_core(after(grad_b[1], sent))
    down = nt(after(hidden, sent), down_full)
    grad_normed_two = keep + after(got, down).astype(F32)

    grad_middle = cotangent + norm_backward(middle, inverse_two, grad_normed_two)
    low_grad = grad_middle.astype(BF16)
    got_low = pair_z(low_grad, 0)
    near_a, far_a = fold(after(grad_a[0], low_grad), got_a, True, 4)
    got_line_a = pair_first(far_a, 1, True)
    near_b, far_b = fold(after(grad_b[0], near_a), got_b, False, 4)
    got_line_b = pair_first(far_b, 1, False)
    rows_near = jnp.concatenate([low_grad, after(got_low, near_b)])
    rows_far = pair_z(rows_near, 1)
    rows_middle = jnp.concatenate([rows_near, rows_far])
    grad_attended = nn(rows_middle, output_full).astype(BF16)
    down_far = after(down[half:].astype(BF16), rows_middle)
    got_down = pair_z(down_far, 1)
    grad_output = by_chip(tn(rows_middle, after(attended, grad_attended)).astype(BF16))
    got_output = swap_core(grad_output[1])
    grad_projected = attend_backward(q, kv, lse, after(grad_attended, *grad_output), tables)

    grad = nt(grad_projected, qkv_full)
    near, far = grad[:half], after(grad[half:].astype(BF16), got_down)
    got = pair_z(far, 1)
    rows_one = jnp.concatenate([one_near, one_far])
    grad_qkv = by_chip(tn(rows_one, after(grad_projected, far)).astype(BF16))
    got_qkv = swap_core(grad_qkv[1])
    keep_a, sent_a = split_sum(near_a, after(got_line_a, *grad_qkv))
    got_a = pair_first(sent_a, 0, True)
    keep_b, sent_b = split_sum(near_b, after(got_line_b, *grad_qkv))
    got_b = pair_first(sent_b, 0, False)
    near_output, far_output = fold(after(grad_output[0], sent_a, sent_b), got_output, False, 20)
    got_line_output = pair_first(far_output, 1, False)
    near_qkv, far_qkv = fold(after(grad_qkv[0], near_output), got_qkv, True, 1)
    got_line_qkv = pair_first(far_qkv, 1, True)
    keep, sent = split_sum(near, after(got, near_qkv))
    got = pair_z(sent, 0)

    keep_down, sent_down = split_sum(down[:half], after(got_down, sent))
    got_down = pair_z(sent_down, 0)
    grad_normed_one = keep + got.astype(F32)
    line_a = (keep_a + after(got_a, sent).astype(F32)).astype(BF16)
    line_b = (keep_b + after(got_b, sent).astype(F32)).astype(BF16)
    keep_qkv, sent_qkv = split_sum(near_qkv, after(got_line_qkv, line_a, line_b))
    got_line_qkv = pair_first(sent_qkv, 0, True)
    keep_output, sent_output = split_sum(near_output, after(got_line_output, sent_qkv))
    got_line_output = pair_first(sent_output, 0, False)
    input_gradient = grad_middle + norm_backward(residual, inverse_one, grad_normed_one)
    block_output = middle + (keep_down + got_down.astype(F32))
    grad_ffn_a = scatter_second(line_a, True)
    grad_ffn_b = scatter_second(line_b, False)
    line_qkv = (keep_qkv + got_line_qkv.astype(F32)).astype(BF16)
    line_output = (keep_output + got_line_output.astype(F32)).astype(BF16)
    grad_qkv = scatter_second(line_qkv, True)
    grad_output = scatter_second(line_output, False)

    low_gains = norm_gains.astype(BF16).astype(F32)
    gain_one, gain_two = low_gains[0][:, None], low_gains[1][:, None]
    low_qkv = jnp.concatenate(
        (query_weight, keyvalue_weight[0], keyvalue_weight[1]), axis=1
    ).astype(BF16)
    low_gate, low_up = (w.astype(BF16).astype(F32) for w in (gateup_weight[0], gateup_weight[1]))
    gain_parts = jnp.stack(
        (
            jnp.sum(low_qkv.astype(F32) * grad_qkv, axis=1),
            jnp.sum(low_gate * grad_ffn_a[:, :HIDDEN], axis=1)
            + jnp.sum(low_up * grad_ffn_b[:, :HIDDEN], axis=1),
        )
    )
    gains = gain_parts + shift_z(gain_parts, 1) + shift_z(gain_parts, -1) + shift_z(gain_parts, 2)
    grad_qkv = grad_qkv * gain_one
    reduced = (
        gains,
        grad_qkv[:, :QUERY_COLS],
        jnp.stack((grad_qkv[:, QUERY_COLS : QUERY_COLS + 64], grad_qkv[:, QUERY_COLS + 64 :])),
        grad_output.T,
        jnp.stack((grad_ffn_a[:, :HIDDEN] * gain_two, grad_ffn_b[:, :HIDDEN] * gain_two)),
        jnp.concatenate((grad_ffn_a[:, HIDDEN:], grad_ffn_b[:, HIDDEN:]), axis=1).T,
    )
    masters = (norm_gains, query_weight, keyvalue_weight, output_weight, gateup_weight, down_weight)
    moments = (
        moment_gains, moment_query, moment_keyvalue, moment_output, moment_gateup, moment_down,
    )
    squares = (
        square_gains, square_query, square_keyvalue, square_output, square_gateup, square_down,
    )
    results = [
        adamw(masters[i], reduced[i], moments[i], squares[i], RATES[i], DECAYS[i]) for i in range(6)
    ]
    return (
        block_output[None],
        input_gradient[None],
        *reduced,
        *(r[0] for r in results),
        *(r[1] for r in results),
        *(r[2] for r in results),
    )


def solution(mesh):
    rows = P("dp", "mp", None)
    weights = (
        P(None, "dp"),
        P("dp", "mp"),
        P(None, "dp", "mp"),
        P("mp", "dp"),
        P(None, "dp", "mp"),
        P("mp", "dp"),
    )
    return jax.shard_map(
        on_device,
        mesh=mesh,
        in_specs=(rows, rows, P("dp", None), *weights, *weights, *weights),
        out_specs=(rows, rows, *weights, *weights, *weights, *weights),
        check_vma=False,
    )
```

```python
import functools

import jax
import jax.numpy as jnp
from jax import lax
from jax.experimental import pallas as pl
from jax.experimental.pallas import tpu as pltpu
from jax.sharding import PartitionSpec as P

HEAD_DIM = 64
HEADS_LOCAL = 8
QUERY_COLS = 512
QKV_COLS = 640
HIDDEN = 1408
SEQ = 512
PART = 128
D = 2048
STEP = 10

EPS = 1e-05
THETA = 10000.0
BETA_ONE = 0.9
BETA_TWO = 0.95
ADAM_EPS = 1e-08
RATES = (1.0, 0.05, 0.05, 0.5, 0.05, 0.025)
DECAYS = (0.0, 0.1, 0.1, 0.1, 0.1, 0.1)
SIDE = 4
BF16 = jnp.bfloat16
F32 = jnp.float32
SPLIT = 768


def cost(us):
    return pl.CostEstimate(
        flops=int(us * 1.1e9), bytes_accessed=int(us * 3.0e6), transcendentals=0
    )


def pair_mask(core, step):
    return (1, 3)[step] if core == 0 else (3, 1)[step]


def dp_index(y, x, core):
    return (y * SIDE + x) * 2 + core


def chips():
    return [(y, x, c) for y in range(SIDE) for x in range(SIDE) for c in range(2)]


def pair_z(a, step):
    pairs = [
        (dp * SIDE + z, dp * SIDE + (z ^ pair_mask(dp % 2, step)))
        for dp in range(2 * SIDE * SIDE)
        for z in range(SIDE)
    ]
    return lax.ppermute(a, ("dp", "mp"), pairs)


def pair_x(a, step):
    pairs = [(dp_index(y, x, c), dp_index(y, x ^ pair_mask(c, step), c)) for y, x, c in chips()]
    return lax.ppermute(a, "dp", pairs)


def pair_y(a, step):
    pairs = [(dp_index(y, x, c), dp_index(y ^ pair_mask(c, step), x, c)) for y, x, c in chips()]
    return lax.ppermute(a, "dp", pairs)


def shift_z(x, by):
    return lax.ppermute(x, "mp", [(i, (i + by) % SIDE) for i in range(SIDE)])


def shift_first(a, by):
    pairs = [
        (dp_index(y, x, c), dp_index((y + by) % SIDE, x, c) if c else dp_index(y, (x + by) % SIDE, c))
        for y, x, c in chips()
    ]
    return lax.ppermute(a, "dp", pairs)


def shift_second(a, by):
    pairs = [
        (dp_index(y, x, c), dp_index(y, (x + by) % SIDE, c) if c else dp_index((y + by) % SIDE, x, c))
        for y, x, c in chips()
    ]
    return lax.ppermute(a, "dp", pairs)


def swap_core(a):
    return lax.ppermute(a, "dp", [(i, i ^ 1) for i in range(2 * SIDE * SIDE)])


def place():
    i = lax.axis_index("dp")
    return i // (2 * SIDE), (i // 2) % SIDE, i % 2


def here():
    return jnp.stack(place()).astype(jnp.int32)


def pick(k, values):
    out = jnp.int32(values[0])
    for i in range(1, len(values)):
        out = jnp.where(k == i, values[i], out)
    return out


def pair_steps(core):
    return jnp.where(core == 0, jnp.array([0, 1, 3, 2]), jnp.array([0, 3, 1, 2])).astype(jnp.int32)


def send_sum(near, got):
    return (near[PART:] + got[PART:].astype(F32)).astype(BF16)


def split_sum(near, got):
    k = near.shape[0] // 2
    keep = near[:k].astype(F32) + got[:k].astype(F32)
    return keep, (near[k:].astype(F32) + got[k:].astype(F32)).astype(BF16)


def place_kernel(here_ref, mine_ref, other_ref, qkv_ref, output_ref):
    y, x, core = here_ref[0], here_ref[1], here_ref[2]

    @pl.loop(0, SIDE * SIDE)
    def _(k):
        first, second = pick(k // SIDE, (0, 3, 1, 2)), pick(k % SIDE, (0, 3, 1, 2))
        for own, blocks_ref in ((True, mine_ref), (False, other_ref)):
            c = core if own else 1 - core
            along_x, along_y = jnp.where(c == 0, first, second), jnp.where(c == 0, second, first)
            chip = ((y + along_y) % SIDE) * SIDE + (x + along_x) % SIDE
            qkv_ref[chip, c] = blocks_ref[k, :, :QKV_COLS]
            output_ref[chip, c] = blocks_ref[k, :, QKV_COLS:]


def place_attention(mine, other):
    parts = pl.pallas_call(
        place_kernel,
        out_shape=[
            jax.ShapeDtypeStruct((SIDE * SIDE, 2, 64, n), mine.dtype)
            for n in (QKV_COLS, QUERY_COLS)
        ],
        in_specs=[pl.BlockSpec(memory_space=pltpu.SMEM)] + whole(2),
        out_specs=whole(2),
        compiler_params=pltpu.CompilerParams(vmem_limit_bytes=32 * 2**20),
        cost_estimate=cost(3),
    )(here(), mine, other)
    return [p.reshape(D, -1) for p in parts]


def pair_first(a, step, x_first):
    return (pair_x if x_first else pair_y)(a, step)


def pair_second(a, step, x_first):
    return (pair_y if x_first else pair_x)(a, step)


def nt(a, b):
    return lax.dot_general(a, b, (((1,), (1,)), ((), ())), preferred_element_type=F32)


def tn(a, b):
    return lax.dot_general(a, b, (((0,), (0,)), ((), ())), preferred_element_type=F32)


def nn(a, b):
    return lax.dot_general(a, b, (((1,), (0,)), ((), ())), preferred_element_type=F32)


def whole(n):
    return [pl.BlockSpec(memory_space=pltpu.VMEM)] * n


def prepare_kernel(
    gains_ref, query_ref, keyvalue_ref, output_ref, gateup_ref, down_ref, part_ref, ffn_ref
):
    gains = gains_ref[...].astype(BF16).astype(F32)
    scaled = lambda k, w: (w.astype(BF16).astype(F32) * gains[:, k : k + 1]).astype(BF16)
    part_ref[:, :QUERY_COLS] = scaled(0, query_ref[...])
    part_ref[:, QUERY_COLS:QKV_COLS] = scaled(
        0, jnp.concatenate([keyvalue_ref[0], keyvalue_ref[1]], axis=1)
    )
    part_ref[:, QKV_COLS:] = output_ref[...].astype(BF16)
    ffn_ref[:, :HIDDEN] = scaled(1, gateup_ref[0])
    ffn_ref[:, HIDDEN : 2 * HIDDEN] = scaled(1, gateup_ref[1])
    ffn_ref[:, 2 * HIDDEN :] = down_ref[...].astype(BF16)


def prepare(norm_gains, query, keyvalue, output, gateup, down):
    full = lambda v: pl.BlockSpec(v.shape, lambda i: (0,) * len(v.shape))
    arrays = (norm_gains.T, query, keyvalue, output.T, gateup, down.T)
    outs = [jax.ShapeDtypeStruct((64, n), BF16) for n in (QKV_COLS + QUERY_COLS, 3 * HIDDEN)]
    return pl.pallas_call(
        prepare_kernel,
        out_shape=outs,
        grid=(1,),
        in_specs=[full(v) for v in arrays],
        out_specs=[full(v) for v in outs],
        compiler_params=pltpu.CompilerParams(vmem_limit_bytes=16 * 2**20),
        cost_estimate=cost(2),
    )(*arrays)


def back_kernel(gate_ref, up_ref, gate_w_ref, up_w_ref, near_ref, far_ref):
    out = nt(gate_ref[...], gate_w_ref[...]) + nt(up_ref[...], up_w_ref[...])
    near_ref[...] = out[: SEQ // 2]
    far_ref[...] = out[SEQ // 2 :].astype(BF16)


def back_to_rows(grad_gate, grad_up, weights):
    tile = 512
    grad = pl.BlockSpec((SEQ, HIDDEN), lambda i: (0, 0))
    weight = lambda at: pl.BlockSpec((tile, HIDDEN), lambda i: (i, at))
    out = pl.BlockSpec((SEQ // 2, tile), lambda i: (0, i))
    return pl.pallas_call(
        back_kernel,
        out_shape=[jax.ShapeDtypeStruct((SEQ // 2, D), t) for t in (F32, BF16)],
        grid=(D // tile,),
        in_specs=[grad, grad, weight(0), weight(1)],
        out_specs=[out, out],
        compiler_params=pltpu.CompilerParams(vmem_limit_bytes=32 * 2**20),
        cost_estimate=cost(10),
    )(grad_gate, grad_up, weights, weights)


def turn_kernel(near_ref, far_ref, turned_ref):
    turned_ref[:, : SEQ // 2] = near_ref[...].T
    turned_ref[:, SEQ // 2 :] = far_ref[...].T


def turned(near, far, us=1):
    return pl.pallas_call(
        turn_kernel,
        out_shape=jax.ShapeDtypeStruct((D, SEQ), BF16),
        in_specs=whole(2),
        out_specs=whole(1)[0],
        compiler_params=pltpu.CompilerParams(vmem_limit_bytes=16 * 2**20),
        cost_estimate=cost(us),
    )(near, far)


def rows_kernel(a_ref, w_ref, near_ref, far_ref):
    out = nt(a_ref[...], w_ref[...])
    near_ref[...] = out[: SEQ // 2]
    far_ref[...] = out[SEQ // 2 :].astype(BF16)


def product_rows(a, w, at, us):
    k, tile = a.shape[1], 512
    out = pl.BlockSpec((SEQ // 2, tile), lambda i: (0, i))
    return pl.pallas_call(
        rows_kernel,
        out_shape=[jax.ShapeDtypeStruct((SEQ // 2, D), t) for t in (F32, BF16)],
        grid=(D // tile,),
        in_specs=[
            pl.BlockSpec((SEQ, k), lambda i: (0, 0)),
            pl.BlockSpec((tile, k), lambda i: (i, at)),
        ],
        out_specs=[out, out],
        compiler_params=pltpu.CompilerParams(vmem_limit_bytes=24 * 2**20),
        cost_estimate=cost(us),
    )(a, w)


def chip_at(k, here_ref, x_first):
    y, x, core = here_ref[0], here_ref[1], here_ref[2]
    steps = lambda i: pick(i, (0, jnp.where(core == 0, 1, 3), jnp.where(core == 0, 3, 1), 2))
    first, second = steps(k // SIDE), steps(k % SIDE)
    if x_first:
        return (y ^ second) * SIDE + (x ^ first)
    return (y ^ first) * SIDE + (x ^ second)


def chip_products(cuts, refs, row):
    outs = []
    for i, cut in enumerate(cuts):
        a_ref, b_ref = refs[2 * i], refs[2 * i + 1]
        rows = [a_ref[pl.ds(pl.multiple_of(row(j), 64), 64), :] for j in range(SIDE)]
        outs.append(nn(jnp.concatenate(rows, axis=0), b_ref[:, cut]))
    return outs


def other_kernel(cuts, here_ref, *refs):
    step, core = pl.program_id(0), here_ref[2]
    at = 0
    for out in chip_products(cuts, refs, lambda j: (step * SIDE + j) * 128 + (1 - core) * 64):
        for j in range(SIDE):
            refs[-1][j, :, at : at + out.shape[1]] = out[j * 64 : j * 64 + 64].astype(BF16)
        at += out.shape[1]


def mine_kernel(cuts, x_first, here_ref, *refs):
    step, core = pl.program_id(0), here_ref[2]
    got = refs[2 * len(cuts) : 2 * len(cuts) + SIDE]
    row = lambda j: chip_at(step * SIDE + j, here_ref, x_first) * 128 + core * 64
    outs = chip_products(cuts, refs, row)
    for half, out_ref in enumerate(refs[-2:]):

        @pl.when(step // 2 == half)
        def _():
            at = 0
            for out in outs:
                cols = slice(at, at + out.shape[1])
                for j in range(SIDE):
                    sums = out[j * 64 : j * 64 + 64] + got[j][0, :, cols].astype(F32)
                    out_ref[j, :, cols] = sums.astype(BF16)
                at = cols.stop


def weight_products(pairs, got, x_first, us):
    cuts = [c for _, _, c in pairs]
    arrays = [v for a, b, _ in pairs for v in (a, b)]
    n = sum(c.stop - c.start for c in cuts)
    full = lambda v: pl.BlockSpec(v.shape, lambda i, h: (0, 0))
    block = (SIDE, 64, n)
    if got is None:
        kernel = functools.partial(other_kernel, cuts)
        specs = [full(v) for v in arrays]
        outs = jax.ShapeDtypeStruct((SIDE * SIDE, 64, n), BF16)
        out_specs = pl.BlockSpec(block, lambda i, h: (i, 0, 0))
    else:
        kernel = functools.partial(mine_kernel, cuts, x_first)
        chips = [
            pl.BlockSpec((1, 64, n), lambda i, h, j=j: (chip_at(i * SIDE + j, h, x_first), 0, 0))
            for j in range(SIDE)
        ]
        specs = [full(v) for v in arrays] + chips
        arrays = arrays + [got] * SIDE
        outs = [jax.ShapeDtypeStruct((2 * SIDE, 64, n), BF16)] * 2
        out_specs = [
            pl.BlockSpec(block, lambda i, h: (jnp.minimum(i, 1), 0, 0)),
            pl.BlockSpec(block, lambda i, h: (jnp.maximum(i - 2, 0), 0, 0)),
        ]
    return pl.pallas_call(
        kernel,
        out_shape=outs,
        grid_spec=pltpu.PrefetchScalarGridSpec(
            num_scalar_prefetch=1, grid=(SIDE,), in_specs=specs, out_specs=out_specs
        ),
        compiler_params=pltpu.CompilerParams(vmem_limit_bytes=32 * 2**20),
        cost_estimate=cost(us),
    )(here(), *arrays)


def norm_kernel(near_ref, got_ref, got_own_ref, residual_ref, middle_ref, low_ref):
    got = got_ref[...].astype(F32) + got_own_ref[...].astype(F32)
    v = residual_ref[...] + near_ref[...] + got
    inverse = lax.rsqrt(jnp.mean(v * v, axis=-1, keepdims=True) + EPS)
    middle_ref[...] = v
    low_ref[...] = (v * inverse).astype(BF16)


def norm_back_kernel(near_ref, got_ref, got_own_ref, v_ref, base_ref, out_ref, low_ref):
    u = near_ref[...] + (got_ref[...].astype(F32) + got_own_ref[...].astype(F32))
    v = v_ref[...]
    inverse = lax.rsqrt(jnp.mean(v * v, axis=-1, keepdims=True) + EPS)
    inner = jnp.mean(u * v, axis=-1, keepdims=True)
    out = base_ref[...] + (inverse * u - v * (inverse * inverse * inverse * inner))
    out_ref[...] = out
    low_ref[...] = out.astype(BF16)


def by_rows(kernel, *arrays):
    block = pl.BlockSpec((32, D), lambda i: (i, 0))
    return pl.pallas_call(
        kernel,
        out_shape=[jax.ShapeDtypeStruct((PART, D), t) for t in (F32, BF16)],
        grid=(PART // 32,),
        in_specs=[block] * len(arrays),
        out_specs=[block, block],
        compiler_params=pltpu.CompilerParams(vmem_limit_bytes=12 * 2**20),
        cost_estimate=cost(1.5),
    )(*arrays)


def hidden_kernel(
    near_ref, far_ref, gate_w_ref, up_w_ref, grad_hidden_ref,
    hidden_ref, grad_gate_ref, grad_up_ref, rows_ref,
):
    @pl.when(pl.program_id(0) == 0)
    def _():
        rows_ref[: SEQ // 2, :] = near_ref[...]
        rows_ref[SEQ // 2 :, :] = far_ref[...]

    gate_up = nn(rows_ref[...], jnp.concatenate([gate_w_ref[...], up_w_ref[...]], axis=1))
    grad_hidden = grad_hidden_ref[...]
    gate, up = gate_up[:, :128], gate_up[:, 128:]
    sigmoid = 1.0 / (1.0 + jnp.exp(-gate))
    activated = gate * sigmoid
    slope = sigmoid * (1.0 + gate * (1.0 - sigmoid))
    hidden_ref[...] = (activated * up).astype(BF16)
    grad_gate_ref[...] = (grad_hidden * up * slope).astype(BF16)
    grad_up_ref[...] = (grad_hidden * activated).astype(BF16)


def hidden_units(near, far, grad_hidden, weights):
    steps = HIDDEN // 128
    weight = lambda at: pl.BlockSpec((D, 128), lambda j: (0, at * steps + j))
    return pl.pallas_call(
        hidden_kernel,
        out_shape=[jax.ShapeDtypeStruct((SEQ, HIDDEN), BF16)] * 3,
        grid=(steps,),
        in_specs=[pl.BlockSpec((SEQ // 2, D), lambda j: (0, 0))] * 2
        + [weight(0), weight(1), pl.BlockSpec((SEQ, 128), lambda j: (0, j))],
        out_specs=[pl.BlockSpec((SEQ, 128), lambda j: (0, j))] * 3,
        scratch_shapes=[pltpu.VMEM((SEQ, D), BF16)],
        compiler_params=pltpu.CompilerParams(vmem_limit_bytes=24 * 2**20),
        cost_estimate=cost(10),
    )(near, far, weights, weights, grad_hidden)


def turn(x, cosine, sine):
    lane = lax.broadcasted_iota(jnp.int32, x.shape, 1)
    ahead = pltpu.roll(x, 96, 1)
    behind = pltpu.roll(x, 32, 1)
    return x * cosine + jnp.where(lane % HEAD_DIM < HEAD_DIM // 2, ahead, behind) * sine


def mask_bias(ends_ref, block):
    shape = ((block + 1) * PART, PART)
    key = lax.broadcasted_iota(jnp.int32, shape, 0)
    query = lax.broadcasted_iota(jnp.int32, shape, 1) + block * PART
    key_segment = jnp.zeros(shape, jnp.int32)
    query_segment = jnp.zeros(shape, jnp.int32)
    for d in range(4):
        key_segment += (key >= ends_ref[d]).astype(jnp.int32)
        query_segment += (query >= ends_ref[d]).astype(jnp.int32)
    return jnp.where((key_segment == query_segment) & (key <= query), 0.0, -1e30)


def halves(x):
    none = jnp.zeros_like(x)
    return jnp.concatenate([x, none], axis=1), jnp.concatenate([none, x], axis=1)


def in_token_order(slot_ref, kv_ref, ordered_ref):
    for block in range(SIDE):
        rows = pl.ds(pl.multiple_of(slot_ref[block] * PART, PART), PART)
        ordered_ref[block * PART : (block + 1) * PART, :] = kv_ref[rows, :]


def forward_kernel(
    slot_ref, ends_ref, qkv_ref, cos_ref, sin_ref, att_ref, q_ref, kv_ref, lse_ref, ordered_ref
):
    cosine, sine = cos_ref[...], sin_ref[...]
    for pair in range(HEADS_LOCAL // 2):
        cols = slice(pair * 128, pair * 128 + 128)
        q_ref[:, cols] = (turn(qkv_ref[:, cols], cosine, sine).astype(BF16)) * BF16(0.125)
    kv = qkv_ref[:, QUERY_COLS:QKV_COLS]
    lane = lax.broadcasted_iota(jnp.int32, kv.shape, 1)
    kv_ref[...] = jnp.where(lane < HEAD_DIM, turn(kv, cosine, sine), kv).astype(BF16)
    in_token_order(slot_ref, kv_ref, ordered_ref)
    kv = ordered_ref[...]
    keys_both = halves(kv[:, :HEAD_DIM])
    values_turned = kv.astype(F32).T[HEAD_DIM:].astype(BF16)
    heads = range(HEADS_LOCAL)
    for block in range(SIDE):
        seen = (block + 1) * PART
        rows = pl.ds(pl.multiple_of(slot_ref[block] * PART, PART), PART)
        bias = mask_bias(ends_ref, block)
        q = [q_ref[rows, k * 128 : (k + 1) * 128] for k in range(HEADS_LOCAL // 2)]
        s = [nt(keys_both[h % 2][:seen], q[h // 2]) + bias for h in heads]
        top = [jnp.max(v, axis=0, keepdims=True) for v in s]
        e = [jnp.exp(v - t) for v, t in zip(s, top)]
        total = [jnp.sum(v, axis=0, keepdims=True) for v in e]
        p = [(v * (1.0 / t)).astype(BF16) for v, t in zip(e, total)]
        out = [nn(values_turned[:, :seen], v) for v in p]
        for h in heads:
            lse_ref[h : h + 1, block * PART : seen] = top[h] + jnp.log(total[h])
        for k in range(HEADS_LOCAL // 2):
            both = jnp.concatenate(out[2 * k : 2 * k + 2], axis=0)
            att_ref[rows, k * 128 : (k + 1) * 128] = both.T.astype(BF16)


def apart(x):
    lane = lax.broadcasted_iota(jnp.int32, x.shape, 1)
    none = jnp.zeros_like(x)
    first = lane < HEAD_DIM
    return jnp.concatenate([jnp.where(first, x, none), jnp.where(first, none, x)], axis=0)


def backward_kernel(
    slot_ref, ends_ref, q_ref, kv_ref, lse_ref, up_ref, cos_ref, sin_ref,
    out_ref, ordered_ref, dk_ref, dv_ref,
):
    in_token_order(slot_ref, kv_ref, ordered_ref)
    kv = ordered_ref[...]
    keys_both, values_both = halves(kv[:, :HEAD_DIM]), halves(kv[:, HEAD_DIM:])
    keys_turned = kv.astype(F32).T[:HEAD_DIM].astype(BF16)
    dk_ref[...] = jnp.zeros_like(dk_ref)
    dv_ref[...] = jnp.zeros_like(dv_ref)
    heads, pairs = range(HEADS_LOCAL), range(HEADS_LOCAL // 2)
    for block in range(SIDE):
        seen = (block + 1) * PART
        rows = pl.ds(pl.multiple_of(slot_ref[block] * PART, PART), PART)
        bias = mask_bias(ends_ref, block)
        cosine, sine = cos_ref[rows, :], -sin_ref[rows, :]
        q = [q_ref[rows, k * 128 : (k + 1) * 128] for k in pairs]
        up = [up_ref[rows, k * 128 : (k + 1) * 128] for k in pairs]
        s = [nt(keys_both[h % 2][:seen], q[h // 2]) + bias for h in heads]
        dp = [nt(values_both[h % 2][:seen], up[h // 2]) for h in heads]
        p = [jnp.exp(s[h] - lse_ref[h : h + 1, block * PART : seen]) for h in heads]
        inner = [jnp.sum(p[h] * dp[h], axis=0, keepdims=True) for h in heads]
        ds = [(p[h] * (dp[h] - inner[h])).astype(BF16) for h in heads]
        p = [v.astype(BF16) for v in p]
        dq = [nn(keys_turned[:, :seen], v) for v in ds]
        q_apart = jnp.concatenate([apart(v) for v in q], axis=0)
        up_apart = jnp.concatenate([apart(v) for v in up], axis=0)
        dk_ref[:seen, :] += nn(jnp.concatenate(ds, axis=1), q_apart)
        dv_ref[:seen, :] += nn(jnp.concatenate(p, axis=1), up_apart)
        for k in pairs:
            both = jnp.concatenate(dq[2 * k : 2 * k + 2], axis=0).T * 0.125
            out_ref[rows, k * 128 : (k + 1) * 128] = turn(both, cosine, sine).astype(BF16)
    lane = lax.broadcasted_iota(jnp.int32, (SEQ, 128), 1)
    dk, dv = dk_ref[...], dv_ref[...]
    dk, dv = dk + pltpu.roll(dk, HEAD_DIM, 1), dv + pltpu.roll(dv, HEAD_DIM, 1)
    dk_ref[...] = jnp.where(lane < HEAD_DIM, dk, dv)
    for block in range(SIDE):
        rows = pl.ds(pl.multiple_of(slot_ref[block] * PART, PART), PART)
        dkv = dk_ref[block * PART : (block + 1) * PART, :]
        turned = turn(dkv, cos_ref[rows, :], -sin_ref[rows, :])
        dkv = jnp.where(lane[:PART] < HEAD_DIM, turned, dkv)
        out_ref[rows, QUERY_COLS:QKV_COLS] = dkv.astype(BF16)


def small(n):
    return [pl.BlockSpec(memory_space=pltpu.SMEM)] * n


def attend_forward(qkv, tables):
    slot, ends, cosine, sine = tables
    return pl.pallas_call(
        forward_kernel,
        out_shape=(
            jax.ShapeDtypeStruct((SEQ, QUERY_COLS), BF16),
            jax.ShapeDtypeStruct((SEQ, QUERY_COLS), BF16),
            jax.ShapeDtypeStruct((SEQ, 128), BF16),
            jax.ShapeDtypeStruct((HEADS_LOCAL, SEQ), F32),
        ),
        in_specs=small(2) + whole(3),
        out_specs=whole(4),
        scratch_shapes=[pltpu.VMEM((SEQ, 128), BF16)],
        compiler_params=pltpu.CompilerParams(vmem_limit_bytes=24 * 2**20),
        cost_estimate=cost(5),
    )(slot, ends, qkv, cosine, sine)


def attend_backward(q, kv, lse, upstream, tables):
    slot, ends, cosine, sine = tables
    return pl.pallas_call(
        backward_kernel,
        out_shape=jax.ShapeDtypeStruct((SEQ, QKV_COLS), BF16),
        in_specs=small(2) + whole(6),
        out_specs=pl.BlockSpec(memory_space=pltpu.VMEM),
        scratch_shapes=[
            pltpu.VMEM((SEQ, 128), BF16),
            pltpu.VMEM((SEQ, 128), F32),
            pltpu.VMEM((SEQ, 128), F32),
        ],
        compiler_params=pltpu.CompilerParams(vmem_limit_bytes=24 * 2**20),
        cost_estimate=cost(6),
    )(slot, ends, q, kv, lse, upstream, cosine, sine)


def attention_tables(lengths):
    block = lax.axis_index("mp") ^ pair_steps(place()[2])
    slot = jnp.sum(
        jnp.where(block[None, :] == jnp.arange(SIDE)[:, None], jnp.arange(SIDE)[None, :], 0), axis=1
    ).astype(jnp.int32)
    token = (block[:, None] * PART + jnp.arange(PART)[None, :]).reshape(SEQ)
    ends = jnp.cumsum(lengths).astype(jnp.int32)
    starts = ends - lengths
    leading = jnp.max(jnp.where(starts[None, :] <= token[:, None], starts[None, :], 0), axis=1)
    indices = jnp.arange(HEAD_DIM // 2).astype(F32)
    frequency = 1.0 / THETA ** (2.0 * indices / HEAD_DIM)
    angles = (token - leading).astype(F32)[:, None] * frequency[None, :]
    cosine, sine = jnp.cos(angles), jnp.sin(angles)
    cosine = jnp.concatenate([cosine] * 4, axis=1)
    sine = jnp.concatenate([-sine, sine, -sine, sine], axis=1)
    return slot, ends, cosine, sine


def adamw(weight, gradient, moment, square, rate, decay):
    momentum = BETA_ONE * moment + (1.0 - BETA_ONE) * gradient
    variance = BETA_TWO * square + (1.0 - BETA_TWO) * gradient * gradient
    moment_hat = momentum / (1.0 - BETA_ONE**STEP)
    square_hat = variance / (1.0 - BETA_TWO**STEP)
    updated = weight - rate * (moment_hat / (jnp.sqrt(square_hat) + ADAM_EPS) + decay * weight)
    return (momentum, variance, updated)


def inverse_rms(v):
    return lax.rsqrt(jnp.mean(v * v, axis=-1, keepdims=True) + EPS)


def after(x, *others):
    return lax.optimization_barrier((x, *others))[0]


def on_device(
    residual, cotangent, document_lengths,
    norm_gains, query_weight, keyvalue_weight, output_weight, gateup_weight, down_weight,
    moment_gains, moment_query, moment_keyvalue, moment_output, moment_gateup, moment_down,
    square_gains, square_query, square_keyvalue, square_output, square_gateup, square_down,
):
    residual, cotangent = residual[0], cotangent[0]
    half = SEQ // 2

    inverse_one = inverse_rms(residual)
    normed_one = (residual * inverse_one).astype(BF16)
    got_one = pair_z(normed_one, 0)
    part, ffn_part = prepare(
        norm_gains, after(query_weight, normed_one),
        keyvalue_weight, output_weight, gateup_weight, down_weight,
    )
    line = jnp.stack([part, shift_first(part, 1), shift_first(part, -1), shift_first(part, 2)])
    ffn_full = lax.all_gather(ffn_part, "dp", axis=0, tiled=True)
    tables = attention_tables(document_lengths[0])
    line = after(line, *tables)
    plane = [line, shift_second(line, 1), shift_second(line, -1), shift_second(line, 2)]
    one_near = after(jnp.concatenate([normed_one, got_one]), line)
    one_far = pair_z(one_near, 1)
    low_cotangent = after(cotangent.astype(BF16), one_near)
    cot_near = jnp.concatenate([low_cotangent, pair_z(low_cotangent, 0)])
    mine = jnp.stack(plane, axis=1).reshape(SIDE * SIDE, *part.shape)
    mine = after(mine, one_far, cot_near)
    other = swap_core(mine)
    cot_far = pair_z(cot_near, 1)
    qkv_full, output_full = place_attention(mine, other)
    qkv = nn(one_near, qkv_full), nn(one_far, qkv_full)
    attended, q, kv, lse = attend_forward(jnp.concatenate(qkv), tables)

    far = nt(after(attended, cot_far)[half:], output_full).astype(BF16)
    got = pair_z(far, 1)
    near = nt(after(attended, far)[:half], output_full)
    cot_turned = turned(after(cot_near, near), cot_far)
    got = after(got, cot_turned)
    middle, normed_two = by_rows(norm_kernel, near, got, pair_z(send_sum(near, got), 0), residual)
    got = pair_z(normed_two, 0)
    cot_rows = jnp.concatenate([cot_near, cot_far])
    down_full = ffn_full[:, 2 * HIDDEN :]
    grad_hidden = nn(after(cot_rows, normed_two), down_full)
    two_near = jnp.concatenate([normed_two, after(got, grad_hidden)])
    two_far = pair_z(two_near, 1)
    one_turned = turned(after(one_near, two_near), one_far)
    two_far = after(two_far, one_turned)

    hidden, grad_gate, grad_up = hidden_units(two_near, two_far, grad_hidden, ffn_full)
    near, far = back_to_rows(grad_gate, grad_up, ffn_full)
    got = pair_z(far, 1)
    rows_turned = turned(after(two_near, far), two_far)
    all_columns = slice(0, HIDDEN)
    pairs_a = (
        (rows_turned, grad_gate, all_columns), (cot_turned, hidden, slice(0, SPLIT))
    )
    pairs_b = (
        (rows_turned, grad_up, all_columns), (cot_turned, hidden, slice(SPLIT, HIDDEN))
    )
    other_a = weight_products(pairs_a, None, True, 4)
    other_b = weight_products(pairs_b, None, False, 4)
    got = after(got, other_a, other_b)
    sent = send_sum(near, got)
    got_own = pair_z(sent, 0)
    got_a = swap_core(after(other_a, sent))
    got_b = swap_core(after(other_b, sent))
    down_near, down_far = product_rows(after(hidden, sent), ffn_full, 2, 5)
    got_own = after(got_own, down_near)

    grad_middle, low_grad = by_rows(norm_back_kernel, near, got, got_own, middle, cotangent)
    got_low = pair_z(low_grad, 0)
    near_a, far_a = weight_products(pairs_a, after(got_a, low_grad), True, 4)
    got_a = pair_first(far_a, 1, True)
    rows_near = jnp.concatenate([low_grad, after(got_low, near_a)])
    rows_far = pair_z(rows_near, 1)
    near_b, far_b = weight_products(pairs_b, after(got_b, rows_near), False, 0.001)
    got_b = pair_first(far_b, 1, False)
    grad_attended = nn(after(rows_near, near_b), output_full).astype(BF16)
    rows_far = after(rows_far, grad_attended)
    grad_attended = jnp.concatenate([grad_attended, nn(rows_far, output_full).astype(BF16)])
    grad_projected = attend_backward(q, kv, lse, grad_attended, tables)
    pairs_qkv = ((one_turned, grad_projected, slice(0, QKV_COLS)),)
    other_qkv = weight_products(pairs_qkv, None, True, 1)
    got_qkv = swap_core(other_qkv)
    near, far = product_rows(after(grad_projected, other_qkv), qkv_full, 0, 2)
    got = pair_z(far, 1)
    keep_a, sent_a = split_sum(near_a, after(got_a, far))
    got_a = pair_first(sent_a, 0, True)
    middle_turned = turned(after(rows_near, sent_a), rows_far, 0.001)
    pairs_output = ((middle_turned, attended, slice(0, QUERY_COLS)),)
    other_output = weight_products(pairs_output, None, False, 0.001)
    got_output = swap_core(other_output)
    keep_b, sent_b = split_sum(near_b, after(got_b, other_output))
    got_b = pair_first(sent_b, 0, False)
    near_qkv, far_qkv = weight_products(pairs_qkv, after(got_qkv, sent_b), True, 0.001)
    got_qkv = pair_first(far_qkv, 1, True)
    near_output, far_output = weight_products(
        pairs_output, after(got_output, near_qkv), False, 0.001
    )
    got_output = pair_first(far_output, 1, False)
    got = after(got, near_output)
    sent = send_sum(near, got)
    got_own = pair_z(sent, 0)

    keep_qkv, sent_qkv = split_sum(near_qkv, after(got_qkv, sent))
    got_qkv = pair_first(sent_qkv, 0, True)
    line_a = (keep_a + after(got_a, sent_qkv).astype(F32)).astype(BF16)
    got_a = pair_second(line_a[2:], 1, True)
    keep_output, sent_output = split_sum(near_output, after(got_output, line_a))
    got_output = pair_first(sent_output, 0, False)
    got_own = after(got_own, sent_output)
    input_gradient, _ = by_rows(norm_back_kernel, near, got, got_own, residual, grad_middle)
    got_down = pair_z(after(down_far, got_own), 1)
    line_b = (keep_b + after(got_b, got_own).astype(F32)).astype(BF16)
    got_b = pair_second(line_b[2:], 1, False)
    line_qkv = (keep_qkv + after(got_qkv, line_b).astype(F32)).astype(BF16)
    got_qkv = pair_second(line_qkv[2:], 1, True)
    line_output = (keep_output + after(got_output, line_qkv).astype(F32)).astype(BF16)
    got_output = pair_second(line_output[2:], 1, False)
    keep_a, sent_a = split_sum(line_a[:2], after(got_a, line_output))
    got_a = pair_second(sent_a, 0, True)
    keep_qkv, sent_qkv = split_sum(line_qkv[:2], after(got_qkv, sent_a))
    got_qkv = pair_second(sent_qkv, 0, True)
    got_down = after(got_down, sent_qkv)
    sent_down = send_sum(down_near, got_down)
    got_down_own = pair_z(sent_down, 0)
    keep_b, sent_b = split_sum(line_b[:2], after(got_b, sent_down))
    got_b = pair_second(sent_b, 0, False)
    keep_output, sent_output = split_sum(line_output[:2], after(got_output, sent_b))
    got_output = pair_second(sent_output, 0, False)
    grad_ffn_a = keep_a[0] + got_a[0].astype(F32)
    grad_qkv = keep_qkv[0] + got_qkv[0].astype(F32)
    grad_ffn_b = keep_b[0] + got_b[0].astype(F32)
    grad_output = keep_output[0] + got_output[0].astype(F32)
    block_output = middle + (
        down_near[:PART] + (got_down[:PART].astype(F32) + got_down_own.astype(F32))
    )

    low_gains = norm_gains.astype(BF16).astype(F32)
    gain_one, gain_two = low_gains[0][:, None], low_gains[1][:, None]
    low_qkv = jnp.concatenate(
        (query_weight, keyvalue_weight[0], keyvalue_weight[1]), axis=1
    ).astype(BF16)
    low_gate, low_up = (w.astype(BF16).astype(F32) for w in (gateup_weight[0], gateup_weight[1]))
    gain_parts = jnp.stack(
        (
            jnp.sum(low_qkv.astype(F32) * grad_qkv, axis=1),
            jnp.sum(low_gate * grad_ffn_a[:, :HIDDEN], axis=1)
            + jnp.sum(low_up * grad_ffn_b[:, :HIDDEN], axis=1),
        )
    )
    gains = gain_parts + shift_z(gain_parts, 1) + shift_z(gain_parts, -1) + shift_z(gain_parts, 2)
    grad_qkv = grad_qkv * gain_one
    reduced = (
        gains,
        grad_qkv[:, :QUERY_COLS],
        jnp.stack((grad_qkv[:, QUERY_COLS : QUERY_COLS + 64], grad_qkv[:, QUERY_COLS + 64 :])),
        grad_output.T,
        jnp.stack((grad_ffn_a[:, :HIDDEN] * gain_two, grad_ffn_b[:, :HIDDEN] * gain_two)),
        jnp.concatenate((grad_ffn_a[:, HIDDEN:], grad_ffn_b[:, HIDDEN:]), axis=1).T,
    )
    masters = (norm_gains, query_weight, keyvalue_weight, output_weight, gateup_weight, down_weight)
    moments = (
        moment_gains, moment_query, moment_keyvalue, moment_output, moment_gateup, moment_down,
    )
    squares = (
        square_gains, square_query, square_keyvalue, square_output, square_gateup, square_down,
    )
    results = [
        adamw(masters[i], reduced[i], moments[i], squares[i], RATES[i], DECAYS[i]) for i in range(6)
    ]
    return (
        block_output[None],
        input_gradient[None],
        *reduced,
        *(r[0] for r in results),
        *(r[1] for r in results),
        *(r[2] for r in results),
    )


def solution(mesh):
    rows = P("dp", "mp", None)
    weights = (
        P(None, "dp"),
        P("dp", "mp"),
        P(None, "dp", "mp"),
        P("mp", "dp"),
        P(None, "dp", "mp"),
        P("mp", "dp"),
    )
    return jax.shard_map(
        on_device,
        mesh=mesh,
        in_specs=(rows, rows, P("dp", None), *weights, *weights, *weights),
        out_specs=(rows, rows, *weights, *weights, *weights, *weights),
        check_vma=False,
    )
```

```python
import functools

import jax
import jax.numpy as jnp
from jax import lax
from jax.experimental import pallas as pl
from jax.experimental.pallas import tpu as pltpu
from jax.sharding import PartitionSpec as P

HEAD_DIM = 64
HEADS_LOCAL = 8
QUERY_COLS = 512
QKV_COLS = 640
HIDDEN = 1408
SEQ = 512
PART = 128
D = 2048
STEP = 10

EPS = 1e-05
THETA = 10000.0
BETA_ONE = 0.9
BETA_TWO = 0.95
ADAM_EPS = 1e-08
RATES = (1.0, 0.05, 0.05, 0.5, 0.05, 0.025)
DECAYS = (0.0, 0.1, 0.1, 0.1, 0.1, 0.1)
SIDE = 4
BF16 = jnp.bfloat16
F32 = jnp.float32
SPLIT = 768


def cost(us):
    return pl.CostEstimate(
        flops=int(us * 1.1e9), bytes_accessed=int(us * 3.0e6), transcendentals=0
    )


def pair_mask(core, step):
    return (1, 3)[step] if core == 0 else (3, 1)[step]


def dp_index(y, x, core):
    return (y * SIDE + x) * 2 + core


def chips():
    return [(y, x, c) for y in range(SIDE) for x in range(SIDE) for c in range(2)]


def pair_z(a, step):
    pairs = [
        (dp * SIDE + z, dp * SIDE + (z ^ pair_mask(dp % 2, step)))
        for dp in range(2 * SIDE * SIDE)
        for z in range(SIDE)
    ]
    return lax.ppermute(a, ("dp", "mp"), pairs)


def pair_x(a, step):
    pairs = [(dp_index(y, x, c), dp_index(y, x ^ pair_mask(c, step), c)) for y, x, c in chips()]
    return lax.ppermute(a, "dp", pairs)


def pair_y(a, step):
    pairs = [(dp_index(y, x, c), dp_index(y ^ pair_mask(c, step), x, c)) for y, x, c in chips()]
    return lax.ppermute(a, "dp", pairs)


def shift_z(x, by):
    return lax.ppermute(x, "mp", [(i, (i + by) % SIDE) for i in range(SIDE)])


def shift_first(a, by):
    pairs = [
        (dp_index(y, x, c), dp_index((y + by) % SIDE, x, c) if c else dp_index(y, (x + by) % SIDE, c))
        for y, x, c in chips()
    ]
    return lax.ppermute(a, "dp", pairs)


def shift_second(a, by):
    pairs = [
        (dp_index(y, x, c), dp_index(y, (x + by) % SIDE, c) if c else dp_index((y + by) % SIDE, x, c))
        for y, x, c in chips()
    ]
    return lax.ppermute(a, "dp", pairs)


def swap_core(a):
    return lax.ppermute(a, "dp", [(i, i ^ 1) for i in range(2 * SIDE * SIDE)])


def place():
    i = lax.axis_index("dp")
    return i // (2 * SIDE), (i // 2) % SIDE, i % 2


def here():
    return jnp.stack(place()).astype(jnp.int32)


def pick(k, values):
    out = jnp.int32(values[0])
    for i in range(1, len(values)):
        out = jnp.where(k == i, values[i], out)
    return out


def pair_steps(core):
    return jnp.where(core == 0, jnp.array([0, 1, 3, 2]), jnp.array([0, 3, 1, 2])).astype(jnp.int32)


def add_low(near, got):
    return (near + got.astype(F32)).astype(BF16)


def send_sum(near, got):
    return (near[PART:] + got[PART:].astype(F32)).astype(BF16)


def split_sum(near, got):
    k = near.shape[0] // 2
    keep = near[:k].astype(F32) + got[:k].astype(F32)
    return keep, (near[k:].astype(F32) + got[k:].astype(F32)).astype(BF16)


def place_kernel(here_ref, mine_ref, other_ref, qkv_ref, output_ref):
    y, x, core = here_ref[0], here_ref[1], here_ref[2]

    @pl.loop(0, SIDE * SIDE)
    def _(k):
        first, second = pick(k // SIDE, (0, 3, 1, 2)), pick(k % SIDE, (0, 3, 1, 2))
        for own, blocks_ref in ((True, mine_ref), (False, other_ref)):
            c = core if own else 1 - core
            along_x, along_y = jnp.where(c == 0, first, second), jnp.where(c == 0, second, first)
            chip = ((y + along_y) % SIDE) * SIDE + (x + along_x) % SIDE
            qkv_ref[chip, c] = blocks_ref[k, :, :QKV_COLS]
            output_ref[chip, c] = blocks_ref[k, :, QKV_COLS:]


def place_attention(mine, other):
    parts = pl.pallas_call(
        place_kernel,
        out_shape=[
            jax.ShapeDtypeStruct((SIDE * SIDE, 2, 64, n), mine.dtype)
            for n in (QKV_COLS, QUERY_COLS)
        ],
        in_specs=[pl.BlockSpec(memory_space=pltpu.SMEM)] + whole(2),
        out_specs=whole(2),
        compiler_params=pltpu.CompilerParams(vmem_limit_bytes=32 * 2**20),
        cost_estimate=cost(3),
    )(here(), mine, other)
    return [p.reshape(D, -1) for p in parts]


def pair_first(a, step, x_first):
    return (pair_x if x_first else pair_y)(a, step)


def pair_second(a, step, x_first):
    return (pair_y if x_first else pair_x)(a, step)


def nt(a, b):
    return lax.dot_general(a, b, (((1,), (1,)), ((), ())), preferred_element_type=F32)


def tn(a, b):
    return lax.dot_general(a, b, (((0,), (0,)), ((), ())), preferred_element_type=F32)


def nn(a, b):
    return lax.dot_general(a, b, (((1,), (0,)), ((), ())), preferred_element_type=F32)


def whole(n):
    return [pl.BlockSpec(memory_space=pltpu.VMEM)] * n


def prepare_kernel(
    gains_ref, query_ref, keyvalue_ref, output_ref, gateup_ref, down_ref, part_ref, ffn_ref
):
    gains = gains_ref[...].astype(BF16).astype(F32).T
    scaled = lambda k, w: (w.astype(BF16).astype(F32) * gains[:, k : k + 1]).astype(BF16)
    part_ref[:, :QUERY_COLS] = scaled(0, query_ref[...])
    part_ref[:, QUERY_COLS:QKV_COLS] = scaled(
        0, jnp.concatenate([keyvalue_ref[0], keyvalue_ref[1]], axis=1)
    )
    part_ref[:, QKV_COLS:] = output_ref[...].astype(BF16)
    ffn_ref[:, :HIDDEN] = scaled(1, gateup_ref[0])
    ffn_ref[:, HIDDEN : 2 * HIDDEN] = scaled(1, gateup_ref[1])
    ffn_ref[:, 2 * HIDDEN :] = down_ref[...].astype(BF16)


def prepare(norm_gains, query, keyvalue, output, gateup, down):
    full = lambda v: pl.BlockSpec(v.shape, lambda i: (0,) * len(v.shape))
    arrays = (norm_gains, query, keyvalue, output.T, gateup, down.T)
    outs = [jax.ShapeDtypeStruct((64, n), BF16) for n in (QKV_COLS + QUERY_COLS, 3 * HIDDEN)]
    return pl.pallas_call(
        prepare_kernel,
        out_shape=outs,
        grid=(1,),
        in_specs=[full(v) for v in arrays],
        out_specs=[full(v) for v in outs],
        compiler_params=pltpu.CompilerParams(vmem_limit_bytes=60 * 2**20),
        cost_estimate=cost(2),
    )(*arrays)


def back_kernel(gate_ref, up_ref, gate_w_ref, up_w_ref, near_ref, far_ref):
    out = nt(gate_ref[...], gate_w_ref[...]) + nt(up_ref[...], up_w_ref[...])
    near_ref[...] = out[: SEQ // 2]
    far_ref[...] = out[SEQ // 2 :].astype(BF16)


def back_to_rows(grad_gate, grad_up, weights):
    tile = 512
    grad = pl.BlockSpec((SEQ, HIDDEN), lambda i: (0, 0))
    weight = lambda at: pl.BlockSpec((tile, HIDDEN), lambda i: (i, at))
    out = pl.BlockSpec((SEQ // 2, tile), lambda i: (0, i))
    return pl.pallas_call(
        back_kernel,
        out_shape=[jax.ShapeDtypeStruct((SEQ // 2, D), t) for t in (F32, BF16)],
        grid=(D // tile,),
        in_specs=[grad, grad, weight(0), weight(1)],
        out_specs=[out, out],
        compiler_params=pltpu.CompilerParams(vmem_limit_bytes=32 * 2**20),
        cost_estimate=cost(10),
    )(grad_gate, grad_up, weights, weights)


def turn_kernel(near_ref, far_ref, turned_ref):
    turned_ref[:, : SEQ // 2] = near_ref[...].T
    turned_ref[:, SEQ // 2 :] = far_ref[...].T


def turned(near, far, us=1):
    return pl.pallas_call(
        turn_kernel,
        out_shape=jax.ShapeDtypeStruct((D, SEQ), BF16),
        in_specs=whole(2),
        out_specs=whole(1)[0],
        compiler_params=pltpu.CompilerParams(vmem_limit_bytes=16 * 2**20),
        cost_estimate=cost(us),
    )(near, far)


def rows_kernel(a_ref, w_ref, near_ref, far_ref):
    out = nt(a_ref[...], w_ref[...])
    near_ref[...] = out[: SEQ // 2]
    far_ref[...] = out[SEQ // 2 :].astype(BF16)


def product_rows(a, w, at, us):
    k, tile = a.shape[1], 512
    out = pl.BlockSpec((SEQ // 2, tile), lambda i: (0, i))
    return pl.pallas_call(
        rows_kernel,
        out_shape=[jax.ShapeDtypeStruct((SEQ // 2, D), t) for t in (F32, BF16)],
        grid=(D // tile,),
        in_specs=[
            pl.BlockSpec((SEQ, k), lambda i: (0, 0)),
            pl.BlockSpec((tile, k), lambda i: (i, at)),
        ],
        out_specs=[out, out],
        compiler_params=pltpu.CompilerParams(vmem_limit_bytes=24 * 2**20),
        cost_estimate=cost(us),
    )(a, w)


def chip_at(k, here_ref, x_first):
    y, x, core = here_ref[0], here_ref[1], here_ref[2]
    steps = lambda i: pick(i, (0, jnp.where(core == 0, 1, 3), jnp.where(core == 0, 3, 1), 2))
    first, second = steps(k // SIDE), steps(k % SIDE)
    if x_first:
        return (y ^ second) * SIDE + (x ^ first)
    return (y ^ first) * SIDE + (x ^ second)


def chip_products(cuts, refs, row):
    outs = []
    for i, cut in enumerate(cuts):
        a_ref, b_ref = refs[2 * i], refs[2 * i + 1]
        rows = [a_ref[pl.ds(pl.multiple_of(row(j), 64), 64), :] for j in range(SIDE)]
        outs.append(nn(jnp.concatenate(rows, axis=0), b_ref[:, cut]))
    return outs


def other_kernel(cuts, here_ref, *refs):
    step, core = pl.program_id(0), here_ref[2]
    at = 0
    for out in chip_products(cuts, refs, lambda j: (step * SIDE + j) * 128 + (1 - core) * 64):
        for j in range(SIDE):
            refs[-1][j, :, at : at + out.shape[1]] = out[j * 64 : j * 64 + 64].astype(BF16)
        at += out.shape[1]


def mine_kernel(cuts, x_first, here_ref, *refs):
    step, core = pl.program_id(0), here_ref[2]
    got = refs[2 * len(cuts) : 2 * len(cuts) + SIDE]
    row = lambda j: chip_at(step * SIDE + j, here_ref, x_first) * 128 + core * 64
    outs = chip_products(cuts, refs, row)
    for half, out_ref in enumerate(refs[-2:]):

        @pl.when(step // 2 == half)
        def _():
            at = 0
            for out in outs:
                cols = slice(at, at + out.shape[1])
                for j in range(SIDE):
                    sums = out[j * 64 : j * 64 + 64] + got[j][0, :, cols].astype(F32)
                    out_ref[j, :, cols] = sums.astype(BF16)
                at = cols.stop


def weight_products(pairs, got, x_first, us):
    cuts = [c for _, _, c in pairs]
    arrays = [v for a, b, _ in pairs for v in (a, b)]
    n = sum(c.stop - c.start for c in cuts)
    full = lambda v: pl.BlockSpec(v.shape, lambda i, h: (0, 0))
    block = (SIDE, 64, n)
    if got is None:
        kernel = functools.partial(other_kernel, cuts)
        specs = [full(v) for v in arrays]
        outs = jax.ShapeDtypeStruct((SIDE * SIDE, 64, n), BF16)
        out_specs = pl.BlockSpec(block, lambda i, h: (i, 0, 0))
    else:
        kernel = functools.partial(mine_kernel, cuts, x_first)
        chips = [
            pl.BlockSpec((1, 64, n), lambda i, h, j=j: (chip_at(i * SIDE + j, h, x_first), 0, 0))
            for j in range(SIDE)
        ]
        specs = [full(v) for v in arrays] + chips
        arrays = arrays + [got] * SIDE
        outs = [jax.ShapeDtypeStruct((2 * SIDE, 64, n), BF16)] * 2
        out_specs = [
            pl.BlockSpec(block, lambda i, h: (jnp.minimum(i, 1), 0, 0)),
            pl.BlockSpec(block, lambda i, h: (jnp.maximum(i - 2, 0), 0, 0)),
        ]
    return pl.pallas_call(
        kernel,
        out_shape=outs,
        grid_spec=pltpu.PrefetchScalarGridSpec(
            num_scalar_prefetch=1, grid=(SIDE,), in_specs=specs, out_specs=out_specs
        ),
        compiler_params=pltpu.CompilerParams(vmem_limit_bytes=32 * 2**20),
        cost_estimate=cost(us),
    )(here(), *arrays)


def first_norm_kernel(v_ref, _, low_ref, size_ref):
    v = v_ref[...]
    square = jnp.mean(v * v, axis=-1, keepdims=True) + EPS
    low_ref[...] = (v * lax.rsqrt(square)).astype(BF16)
    size_ref[...] = jnp.broadcast_to(jnp.sqrt(square), size_ref.shape)


def first_norm(residual, part):
    block = pl.BlockSpec((32, D), lambda i: (i, 0))
    return pl.pallas_call(
        first_norm_kernel,
        out_shape=[
            jax.ShapeDtypeStruct((PART, D), BF16), jax.ShapeDtypeStruct((PART, 128), F32)
        ],
        grid=(PART // 32,),
        in_specs=[block, pl.BlockSpec(memory_space=pl.ANY)],
        out_specs=[block, pl.BlockSpec((32, 128), lambda i: (i, 0))],
        compiler_params=pltpu.CompilerParams(vmem_limit_bytes=12 * 2**20),
        cost_estimate=cost(1),
    )(residual, part)


def pair_norm_kernel(
    sum_ref, got_ref, residual_ref, normed_ref, size_ref, own_ref, partner_ref, low_ref
):
    own = pl.program_id(0) < PART // 64
    base = jnp.where(own, residual_ref[...], normed_ref[...].astype(F32) * size_ref[:, :1])
    v = base + (sum_ref[...].astype(F32) + got_ref[...].astype(F32))
    inverse = lax.rsqrt(jnp.mean(v * v, axis=-1, keepdims=True) + EPS)
    low_ref[...] = (v * inverse).astype(BF16)

    @pl.when(own)
    def _():
        own_ref[...] = v

    @pl.when(jnp.logical_not(own))
    def _():
        partner_ref[...] = v.astype(BF16)


def pair_norm_back_kernel(
    sum_ref, got_ref, v_ref, partner_ref, cotangent_ref, low_cotangent_ref, out_ref, low_ref
):
    own = pl.program_id(0) < PART // 64
    base = jnp.where(own, cotangent_ref[...], low_cotangent_ref[...].astype(F32))
    v = jnp.where(own, v_ref[...], partner_ref[...].astype(F32))
    u = sum_ref[...].astype(F32) + got_ref[...].astype(F32)
    inverse = lax.rsqrt(jnp.mean(v * v, axis=-1, keepdims=True) + EPS)
    inner = jnp.mean(u * v, axis=-1, keepdims=True)
    out = base + (inverse * u - v * (inverse * inverse * inverse * inner))
    low_ref[...] = out.astype(BF16)

    @pl.when(own)
    def _():
        out_ref[...] = out


HALF = PART // 64
EACH, ACROSS = (lambda i: i), (lambda i: (i + HALF) % (2 * HALF))
OWN, PARTNER = (lambda i: jnp.minimum(i, HALF - 1)), (lambda i: jnp.maximum(i - HALF, 0))


def by_pair_rows(kernel, ins, outs):
    block = lambda n, at: pl.BlockSpec((64, n), lambda i: (at(i), 0))
    rows = lambda at: 2 * PART if at is EACH else PART
    return pl.pallas_call(
        kernel,
        out_shape=[jax.ShapeDtypeStruct((rows(at), D), t) for t, at in outs],
        grid=(2 * HALF,),
        in_specs=[block(a.shape[1], at) for a, at in ins],
        out_specs=[block(D, at) for _, at in outs],
        compiler_params=pltpu.CompilerParams(vmem_limit_bytes=24 * 2**20),
        cost_estimate=cost(2),
    )(*[a for a, _ in ins])


def norm_back_kernel(near_ref, got_ref, got_own_ref, v_ref, base_ref, out_ref, low_ref):
    u = near_ref[...] + (got_ref[...].astype(F32) + got_own_ref[...].astype(F32))
    v = v_ref[...]
    inverse = lax.rsqrt(jnp.mean(v * v, axis=-1, keepdims=True) + EPS)
    inner = jnp.mean(u * v, axis=-1, keepdims=True)
    out = base_ref[...] + (inverse * u - v * (inverse * inverse * inverse * inner))
    out_ref[...] = out
    low_ref[...] = out.astype(BF16)


def by_rows(kernel, *arrays):
    block = pl.BlockSpec((32, D), lambda i: (i, 0))
    return pl.pallas_call(
        kernel,
        out_shape=[jax.ShapeDtypeStruct((PART, D), t) for t in (F32, BF16)],
        grid=(PART // 32,),
        in_specs=[block] * len(arrays),
        out_specs=[block, block],
        compiler_params=pltpu.CompilerParams(vmem_limit_bytes=12 * 2**20),
        cost_estimate=cost(1.5),
    )(*arrays)


def hidden_kernel(
    near_ref, far_ref, gate_w_ref, up_w_ref, grad_hidden_ref,
    hidden_ref, grad_gate_ref, grad_up_ref, rows_ref,
):
    @pl.when(pl.program_id(0) == 0)
    def _():
        rows_ref[: SEQ // 2, :] = near_ref[...]
        rows_ref[SEQ // 2 :, :] = far_ref[...]

    gate_up = nn(rows_ref[...], jnp.concatenate([gate_w_ref[...], up_w_ref[...]], axis=1))
    grad_hidden = grad_hidden_ref[...]
    gate, up = gate_up[:, :128], gate_up[:, 128:]
    sigmoid = 1.0 / (1.0 + jnp.exp(-gate))
    activated = gate * sigmoid
    slope = sigmoid * (1.0 + gate * (1.0 - sigmoid))
    hidden_ref[...] = (activated * up).astype(BF16)
    grad_gate_ref[...] = (grad_hidden * up * slope).astype(BF16)
    grad_up_ref[...] = (grad_hidden * activated).astype(BF16)


def hidden_units(near, far, grad_hidden, weights):
    steps = HIDDEN // 128
    weight = lambda at: pl.BlockSpec((D, 128), lambda j: (0, at * steps + j))
    return pl.pallas_call(
        hidden_kernel,
        out_shape=[jax.ShapeDtypeStruct((SEQ, HIDDEN), BF16)] * 3,
        grid=(steps,),
        in_specs=[pl.BlockSpec((SEQ // 2, D), lambda j: (0, 0))] * 2
        + [weight(0), weight(1), pl.BlockSpec((SEQ, 128), lambda j: (0, j))],
        out_specs=[pl.BlockSpec((SEQ, 128), lambda j: (0, j))] * 3,
        scratch_shapes=[pltpu.VMEM((SEQ, D), BF16)],
        compiler_params=pltpu.CompilerParams(vmem_limit_bytes=24 * 2**20),
        cost_estimate=cost(10),
    )(near, far, weights, weights, grad_hidden)


def turn(x, cosine, sine):
    lane = lax.broadcasted_iota(jnp.int32, x.shape, 1)
    ahead = pltpu.roll(x, 96, 1)
    behind = pltpu.roll(x, 32, 1)
    return x * cosine + jnp.where(lane % HEAD_DIM < HEAD_DIM // 2, ahead, behind) * sine


def mask_bias(ends_ref, block):
    shape = ((block + 1) * PART, PART)
    key = lax.broadcasted_iota(jnp.int32, shape, 0)
    query = lax.broadcasted_iota(jnp.int32, shape, 1) + block * PART
    key_segment = jnp.zeros(shape, jnp.int32)
    query_segment = jnp.zeros(shape, jnp.int32)
    for d in range(4):
        key_segment += (key >= ends_ref[d]).astype(jnp.int32)
        query_segment += (query >= ends_ref[d]).astype(jnp.int32)
    return jnp.where((key_segment == query_segment) & (key <= query), 0.0, -1e30)


def halves(x):
    none = jnp.zeros_like(x)
    return jnp.concatenate([x, none], axis=1), jnp.concatenate([none, x], axis=1)


def in_token_order(slot_ref, kv_ref, ordered_ref):
    for block in range(SIDE):
        rows = pl.ds(pl.multiple_of(slot_ref[block] * PART, PART), PART)
        ordered_ref[block * PART : (block + 1) * PART, :] = kv_ref[rows, :]


def forward_kernel(
    slot_ref, ends_ref, qkv_ref, cos_ref, sin_ref, att_ref, q_ref, kv_ref, lse_ref, ordered_ref
):
    cosine, sine = cos_ref[...], sin_ref[...]
    for pair in range(HEADS_LOCAL // 2):
        cols = slice(pair * 128, pair * 128 + 128)
        q_ref[:, cols] = (turn(qkv_ref[:, cols], cosine, sine).astype(BF16)) * BF16(0.125)
    kv = qkv_ref[:, QUERY_COLS:QKV_COLS]
    lane = lax.broadcasted_iota(jnp.int32, kv.shape, 1)
    kv_ref[...] = jnp.where(lane < HEAD_DIM, turn(kv, cosine, sine), kv).astype(BF16)
    in_token_order(slot_ref, kv_ref, ordered_ref)
    kv = ordered_ref[...]
    keys_both = halves(kv[:, :HEAD_DIM])
    values_turned = kv.astype(F32).T[HEAD_DIM:].astype(BF16)
    heads = range(HEADS_LOCAL)
    for block in range(SIDE):
        seen = (block + 1) * PART
        rows = pl.ds(pl.multiple_of(slot_ref[block] * PART, PART), PART)
        bias = mask_bias(ends_ref, block)
        q = [q_ref[rows, k * 128 : (k + 1) * 128] for k in range(HEADS_LOCAL // 2)]
        s = [nt(keys_both[h % 2][:seen], q[h // 2]) + bias for h in heads]
        top = [jnp.max(v, axis=0, keepdims=True) for v in s]
        e = [jnp.exp(v - t) for v, t in zip(s, top)]
        total = [jnp.sum(v, axis=0, keepdims=True) for v in e]
        p = [(v * (1.0 / t)).astype(BF16) for v, t in zip(e, total)]
        out = [nn(values_turned[:, :seen], v) for v in p]
        for h in heads:
            lse_ref[h : h + 1, block * PART : seen] = top[h] + jnp.log(total[h])
        for k in range(HEADS_LOCAL // 2):
            both = jnp.concatenate(out[2 * k : 2 * k + 2], axis=0)
            att_ref[rows, k * 128 : (k + 1) * 128] = both.T.astype(BF16)


def apart(x):
    lane = lax.broadcasted_iota(jnp.int32, x.shape, 1)
    none = jnp.zeros_like(x)
    first = lane < HEAD_DIM
    return jnp.concatenate([jnp.where(first, x, none), jnp.where(first, none, x)], axis=0)


def backward_kernel(
    slot_ref, ends_ref, q_ref, kv_ref, lse_ref, up_ref, cos_ref, sin_ref,
    out_ref, ordered_ref, dk_ref, dv_ref,
):
    in_token_order(slot_ref, kv_ref, ordered_ref)
    kv = ordered_ref[...]
    keys_both, values_both = halves(kv[:, :HEAD_DIM]), halves(kv[:, HEAD_DIM:])
    keys_turned = kv.astype(F32).T[:HEAD_DIM].astype(BF16)
    dk_ref[...] = jnp.zeros_like(dk_ref)
    dv_ref[...] = jnp.zeros_like(dv_ref)
    heads, pairs = range(HEADS_LOCAL), range(HEADS_LOCAL // 2)
    for block in range(SIDE):
        seen = (block + 1) * PART
        rows = pl.ds(pl.multiple_of(slot_ref[block] * PART, PART), PART)
        bias = mask_bias(ends_ref, block)
        cosine, sine = cos_ref[rows, :], -sin_ref[rows, :]
        q = [q_ref[rows, k * 128 : (k + 1) * 128] for k in pairs]
        up = [up_ref[rows, k * 128 : (k + 1) * 128] for k in pairs]
        s = [nt(keys_both[h % 2][:seen], q[h // 2]) + bias for h in heads]
        dp = [nt(values_both[h % 2][:seen], up[h // 2]) for h in heads]
        p = [jnp.exp(s[h] - lse_ref[h : h + 1, block * PART : seen]) for h in heads]
        inner = [jnp.sum(p[h] * dp[h], axis=0, keepdims=True) for h in heads]
        ds = [(p[h] * (dp[h] - inner[h])).astype(BF16) for h in heads]
        p = [v.astype(BF16) for v in p]
        dq = [nn(keys_turned[:, :seen], v) for v in ds]
        q_apart = jnp.concatenate([apart(v) for v in q], axis=0)
        up_apart = jnp.concatenate([apart(v) for v in up], axis=0)
        dk_ref[:seen, :] += nn(jnp.concatenate(ds, axis=1), q_apart)
        dv_ref[:seen, :] += nn(jnp.concatenate(p, axis=1), up_apart)
        for k in pairs:
            both = jnp.concatenate(dq[2 * k : 2 * k + 2], axis=0).T * 0.125
            out_ref[rows, k * 128 : (k + 1) * 128] = turn(both, cosine, sine).astype(BF16)
    lane = lax.broadcasted_iota(jnp.int32, (SEQ, 128), 1)
    dk, dv = dk_ref[...], dv_ref[...]
    dk, dv = dk + pltpu.roll(dk, HEAD_DIM, 1), dv + pltpu.roll(dv, HEAD_DIM, 1)
    dk_ref[...] = jnp.where(lane < HEAD_DIM, dk, dv)
    for block in range(SIDE):
        rows = pl.ds(pl.multiple_of(slot_ref[block] * PART, PART), PART)
        dkv = dk_ref[block * PART : (block + 1) * PART, :]
        turned = turn(dkv, cos_ref[rows, :], -sin_ref[rows, :])
        dkv = jnp.where(lane[:PART] < HEAD_DIM, turned, dkv)
        out_ref[rows, QUERY_COLS:QKV_COLS] = dkv.astype(BF16)


def small(n):
    return [pl.BlockSpec(memory_space=pltpu.SMEM)] * n


def attend_forward(qkv, tables):
    slot, ends, cosine, sine = tables
    return pl.pallas_call(
        forward_kernel,
        out_shape=(
            jax.ShapeDtypeStruct((SEQ, QUERY_COLS), BF16),
            jax.ShapeDtypeStruct((SEQ, QUERY_COLS), BF16),
            jax.ShapeDtypeStruct((SEQ, 128), BF16),
            jax.ShapeDtypeStruct((HEADS_LOCAL, SEQ), F32),
        ),
        in_specs=small(2) + whole(3),
        out_specs=whole(4),
        scratch_shapes=[pltpu.VMEM((SEQ, 128), BF16)],
        compiler_params=pltpu.CompilerParams(vmem_limit_bytes=24 * 2**20),
        cost_estimate=cost(5),
    )(slot, ends, qkv, cosine, sine)


def attend_backward(q, kv, lse, upstream, tables):
    slot, ends, cosine, sine = tables
    return pl.pallas_call(
        backward_kernel,
        out_shape=jax.ShapeDtypeStruct((SEQ, QKV_COLS), BF16),
        in_specs=small(2) + whole(6),
        out_specs=pl.BlockSpec(memory_space=pltpu.VMEM),
        scratch_shapes=[
            pltpu.VMEM((SEQ, 128), BF16),
            pltpu.VMEM((SEQ, 128), F32),
            pltpu.VMEM((SEQ, 128), F32),
        ],
        compiler_params=pltpu.CompilerParams(vmem_limit_bytes=24 * 2**20),
        cost_estimate=cost(6),
    )(slot, ends, q, kv, lse, upstream, cosine, sine)


def attention_tables(lengths):
    block = lax.axis_index("mp") ^ pair_steps(place()[2])
    slot = jnp.sum(
        jnp.where(block[None, :] == jnp.arange(SIDE)[:, None], jnp.arange(SIDE)[None, :], 0), axis=1
    ).astype(jnp.int32)
    token = (block[:, None] * PART + jnp.arange(PART)[None, :]).reshape(SEQ)
    ends = jnp.cumsum(lengths).astype(jnp.int32)
    starts = ends - lengths
    leading = jnp.max(jnp.where(starts[None, :] <= token[:, None], starts[None, :], 0), axis=1)
    indices = jnp.arange(HEAD_DIM // 2).astype(F32)
    frequency = 1.0 / THETA ** (2.0 * indices / HEAD_DIM)
    angles = (token - leading).astype(F32)[:, None] * frequency[None, :]
    cosine, sine = jnp.cos(angles), jnp.sin(angles)
    cosine = jnp.concatenate([cosine] * 4, axis=1)
    sine = jnp.concatenate([-sine, sine, -sine, sine], axis=1)
    return slot, ends, cosine, sine


def adamw(weight, gradient, moment, square, rate, decay):
    momentum = BETA_ONE * moment + (1.0 - BETA_ONE) * gradient
    variance = BETA_TWO * square + (1.0 - BETA_TWO) * gradient * gradient
    moment_hat = momentum / (1.0 - BETA_ONE**STEP)
    square_hat = variance / (1.0 - BETA_TWO**STEP)
    updated = weight - rate * (moment_hat / (jnp.sqrt(square_hat) + ADAM_EPS) + decay * weight)
    return (momentum, variance, updated)


def after(x, *others):
    return lax.optimization_barrier((x, *others))[0]


def on_device(
    residual, cotangent, document_lengths,
    norm_gains, query_weight, keyvalue_weight, output_weight, gateup_weight, down_weight,
    moment_gains, moment_query, moment_keyvalue, moment_output, moment_gateup, moment_down,
    square_gains, square_query, square_keyvalue, square_output, square_gateup, square_down,
):
    residual, cotangent = residual[0], cotangent[0]
    half = SEQ // 2

    part, ffn_part = prepare(
        norm_gains, query_weight, keyvalue_weight, output_weight, gateup_weight, down_weight
    )
    normed_one, size = first_norm(residual, part)
    got_one = pair_z(normed_one, 0)
    got_size = pair_z(size, 0)
    line = jnp.stack([part, shift_first(part, 1), shift_first(part, -1), shift_first(part, 2)])
    ffn_full = lax.all_gather(ffn_part, "dp", axis=0, tiled=True)
    tables = attention_tables(document_lengths[0])
    line = after(line, *tables)
    plane = [line, shift_second(line, 1), shift_second(line, -1), shift_second(line, 2)]
    one_near = after(jnp.concatenate([normed_one, got_one]), line)
    one_far = pair_z(one_near, 1)
    low_cotangent = after(cotangent.astype(BF16), one_near)
    cot_near = jnp.concatenate([low_cotangent, pair_z(low_cotangent, 0)])
    mine = jnp.stack(plane, axis=1).reshape(SIDE * SIDE, *part.shape)
    mine = after(mine, one_far, cot_near)
    other = swap_core(mine)
    cot_far = pair_z(cot_near, 1)
    qkv_full, output_full = place_attention(mine, other)
    qkv = nn(one_near, qkv_full), nn(one_far, qkv_full)
    attended, q, kv, lse = attend_forward(after(jnp.concatenate(qkv), got_size), tables)

    far = nt(after(attended, cot_far)[half:], output_full).astype(BF16)
    got = pair_z(far, 1)
    near = nt(after(attended, far)[:half], output_full)
    cot_turned = turned(after(cot_near, near), cot_far)
    got = after(got, cot_turned)
    sent = add_low(near, got)
    got_pair = pair_z(sent, 0)
    cot_rows = jnp.concatenate([cot_near, cot_far])
    got_pair = after(got_pair, cot_rows)
    middle, partner_middle, two_near = by_pair_rows(
        pair_norm_kernel,
        ((sent, EACH), (got_pair, ACROSS), (residual, OWN), (one_near, EACH), (got_size, PARTNER)),
        ((F32, OWN), (BF16, PARTNER), (BF16, EACH)),
    )
    two_far = pair_z(two_near, 1)
    down_full = ffn_full[:, 2 * HIDDEN :]
    one_turned = turned(after(one_near, two_near), one_far)
    grad_hidden = nn(after(cot_rows, one_turned), down_full)
    two_far = after(two_far, grad_hidden)

    hidden, grad_gate, grad_up = hidden_units(two_near, two_far, grad_hidden, ffn_full)
    near, far = back_to_rows(grad_gate, grad_up, ffn_full)
    got = pair_z(far, 1)
    rows_turned = turned(after(two_near, far), two_far)
    all_columns = slice(0, HIDDEN)
    pairs_a = (
        (rows_turned, grad_gate, all_columns), (cot_turned, hidden, slice(0, SPLIT))
    )
    pairs_b = (
        (rows_turned, grad_up, all_columns), (cot_turned, hidden, slice(SPLIT, HIDDEN))
    )
    other_a = weight_products(pairs_a, None, True, 4)
    other_b = weight_products(pairs_b, None, False, 4)
    got = after(got, other_a, other_b)
    sent = add_low(near, got)
    got_pair = pair_z(sent, 0)
    got_a = swap_core(after(other_a, sent))
    got_b = swap_core(after(other_b, sent))
    down = nt(after(hidden, sent), down_full)
    down_near, down_far = down[:half], down[half:].astype(BF16)
    near_a, far_a = weight_products(pairs_a, after(got_a, down), True, 4)
    got_a = pair_first(far_a, 1, True)
    got_pair = after(got_pair, near_a)

    grad_middle, rows_near = by_pair_rows(
        pair_norm_back_kernel,
        (
            (sent, EACH), (got_pair, ACROSS), (middle, OWN), (partner_middle, PARTNER),
            (cotangent, OWN), (cot_near, EACH),
        ),
        ((F32, OWN), (BF16, EACH)),
    )
    rows_far = pair_z(rows_near, 1)
    near_b, far_b = weight_products(pairs_b, after(got_b, rows_near), False, 0.001)
    got_b = pair_first(far_b, 1, False)
    grad_attended = nn(after(rows_near, near_b), output_full).astype(BF16)
    rows_far = after(rows_far, grad_attended)
    grad_attended = jnp.concatenate([grad_attended, nn(rows_far, output_full).astype(BF16)])
    grad_projected = attend_backward(q, kv, lse, grad_attended, tables)
    pairs_qkv = ((one_turned, grad_projected, slice(0, QKV_COLS)),)
    other_qkv = weight_products(pairs_qkv, None, True, 1)
    got_qkv = swap_core(other_qkv)
    near, far = product_rows(after(grad_projected, other_qkv), qkv_full, 0, 2)
    got = pair_z(far, 1)
    keep_a, sent_a = split_sum(near_a, after(got_a, far))
    got_a = pair_first(sent_a, 0, True)
    middle_turned = turned(after(rows_near, sent_a), rows_far, 0.001)
    pairs_output = ((middle_turned, attended, slice(0, QUERY_COLS)),)
    other_output = weight_products(pairs_output, None, False, 0.001)
    got_output = swap_core(other_output)
    keep_b, sent_b = split_sum(near_b, after(got_b, other_output))
    got_b = pair_first(sent_b, 0, False)
    near_qkv, far_qkv = weight_products(pairs_qkv, after(got_qkv, sent_b), True, 0.001)
    got_qkv = pair_first(far_qkv, 1, True)
    near_output, far_output = weight_products(
        pairs_output, after(got_output, near_qkv), False, 0.001
    )
    got_output = pair_first(far_output, 1, False)
    got = after(got, near_output)
    sent = send_sum(near, got)
    got_own = pair_z(sent, 0)

    keep_qkv, sent_qkv = split_sum(near_qkv, after(got_qkv, sent))
    got_qkv = pair_first(sent_qkv, 0, True)
    line_a = (keep_a + after(got_a, sent_qkv).astype(F32)).astype(BF16)
    got_a = pair_second(line_a[2:], 1, True)
    keep_output, sent_output = split_sum(near_output, after(got_output, line_a))
    got_output = pair_first(sent_output, 0, False)
    got_own = after(got_own, sent_output)
    input_gradient, _ = by_rows(norm_back_kernel, near, got, got_own, residual, grad_middle)
    got_down = pair_z(after(down_far, got_own), 1)
    line_b = (keep_b + after(got_b, got_own).astype(F32)).astype(BF16)
    got_b = pair_second(line_b[2:], 1, False)
    line_qkv = (keep_qkv + after(got_qkv, line_b).astype(F32)).astype(BF16)
    got_qkv = pair_second(line_qkv[2:], 1, True)
    line_output = (keep_output + after(got_output, line_qkv).astype(F32)).astype(BF16)
    got_output = pair_second(line_output[2:], 1, False)
    keep_a, sent_a = split_sum(line_a[:2], after(got_a, line_output))
    got_a = pair_second(sent_a, 0, True)
    keep_qkv, sent_qkv = split_sum(line_qkv[:2], after(got_qkv, sent_a))
    got_qkv = pair_second(sent_qkv, 0, True)
    got_down = after(got_down, sent_qkv)
    sent_down = send_sum(down_near, got_down)
    got_down_own = pair_z(sent_down, 0)
    keep_b, sent_b = split_sum(line_b[:2], after(got_b, sent_down))
    got_b = pair_second(sent_b, 0, False)
    keep_output, sent_output = split_sum(line_output[:2], after(got_output, sent_b))
    got_output = pair_second(sent_output, 0, False)
    grad_ffn_a = keep_a[0] + got_a[0].astype(F32)
    grad_qkv = keep_qkv[0] + got_qkv[0].astype(F32)
    grad_ffn_b = keep_b[0] + got_b[0].astype(F32)
    block_output = middle + (
        down_near[:PART] + (got_down[:PART].astype(F32) + got_down_own.astype(F32))
    )

    low_gains = norm_gains.astype(BF16).astype(F32)
    gain_one, gain_two = low_gains[0][:, None], low_gains[1][:, None]
    low_qkv = jnp.concatenate(
        (query_weight, keyvalue_weight[0], keyvalue_weight[1]), axis=1
    ).astype(BF16)
    low_gate, low_up = (w.astype(BF16).astype(F32) for w in (gateup_weight[0], gateup_weight[1]))
    gain_parts = jnp.stack(
        (
            jnp.sum(low_qkv.astype(F32) * grad_qkv, axis=1),
            jnp.sum(low_gate * grad_ffn_a[:, :HIDDEN], axis=1)
            + jnp.sum(low_up * grad_ffn_b[:, :HIDDEN], axis=1),
        )
    )
    grad_output = keep_output[0] + after(got_output, gain_parts)[0].astype(F32)
    gains = gain_parts + shift_z(gain_parts, 1) + shift_z(gain_parts, -1) + shift_z(gain_parts, 2)
    grad_qkv = grad_qkv * gain_one
    reduced = (
        gains,
        grad_qkv[:, :QUERY_COLS],
        jnp.stack((grad_qkv[:, QUERY_COLS : QUERY_COLS + 64], grad_qkv[:, QUERY_COLS + 64 :])),
        grad_output.T,
        jnp.stack((grad_ffn_a[:, :HIDDEN] * gain_two, grad_ffn_b[:, :HIDDEN] * gain_two)),
        jnp.concatenate((grad_ffn_a[:, HIDDEN:], grad_ffn_b[:, HIDDEN:]), axis=1).T,
    )
    masters = (norm_gains, query_weight, keyvalue_weight, output_weight, gateup_weight, down_weight)
    moments = (
        moment_gains, moment_query, moment_keyvalue, moment_output, moment_gateup, moment_down,
    )
    squares = (
        square_gains, square_query, square_keyvalue, square_output, square_gateup, square_down,
    )
    results = [
        adamw(masters[i], reduced[i], moments[i], squares[i], RATES[i], DECAYS[i]) for i in range(6)
    ]
    return (
        block_output[None],
        input_gradient[None],
        *reduced,
        *(r[0] for r in results),
        *(r[1] for r in results),
        *(r[2] for r in results),
    )


def solution(mesh):
    rows = P("dp", "mp", None)
    weights = (
        P(None, "dp"),
        P("dp", "mp"),
        P(None, "dp", "mp"),
        P("mp", "dp"),
        P(None, "dp", "mp"),
        P("mp", "dp"),
    )
    return jax.shard_map(
        on_device,
        mesh=mesh,
        in_specs=(rows, rows, P("dp", None), *weights, *weights, *weights),
        out_specs=(rows, rows, *weights, *weights, *weights, *weights),
        check_vma=False,
    )
```

```python
import functools

import jax
import jax.numpy as jnp
from jax import lax
from jax.experimental import pallas as pl
from jax.experimental.pallas import tpu as pltpu
from jax.sharding import PartitionSpec as P

HEAD_DIM = 64
HEADS_LOCAL = 8
QUERY_COLS = 512
QKV_COLS = 640
HIDDEN = 1408
SEQ = 512
PART = 128
D = 2048
STEP = 10

EPS = 1e-05
THETA = 10000.0
BETA_ONE = 0.9
BETA_TWO = 0.95
ADAM_EPS = 1e-08
RATES = (1.0, 0.05, 0.05, 0.5, 0.05, 0.025)
DECAYS = (0.0, 0.1, 0.1, 0.1, 0.1, 0.1)
SIDE = 4
BF16 = jnp.bfloat16
F32 = jnp.float32
SPLIT = 768


def cost(us):
    return pl.CostEstimate(
        flops=int(us * 1.1e9), bytes_accessed=int(us * 3.0e6), transcendentals=0
    )


def pair_mask(core, step):
    return (1, 3)[step] if core == 0 else (3, 1)[step]


def dp_index(y, x, core):
    return (y * SIDE + x) * 2 + core


def chips():
    return [(y, x, c) for y in range(SIDE) for x in range(SIDE) for c in range(2)]


def pair_z(a, step):
    pairs = [
        (dp * SIDE + z, dp * SIDE + (z ^ pair_mask(dp % 2, step)))
        for dp in range(2 * SIDE * SIDE)
        for z in range(SIDE)
    ]
    return lax.ppermute(a, ("dp", "mp"), pairs)


def pair_x(a, step):
    pairs = [(dp_index(y, x, c), dp_index(y, x ^ pair_mask(c, step), c)) for y, x, c in chips()]
    return lax.ppermute(a, "dp", pairs)


def pair_y(a, step):
    pairs = [(dp_index(y, x, c), dp_index(y ^ pair_mask(c, step), x, c)) for y, x, c in chips()]
    return lax.ppermute(a, "dp", pairs)


def shift_z(x, by):
    return lax.ppermute(x, "mp", [(i, (i + by) % SIDE) for i in range(SIDE)])


def shift_first(a, by):
    pairs = [
        (dp_index(y, x, c), dp_index((y + by) % SIDE, x, c) if c else dp_index(y, (x + by) % SIDE, c))
        for y, x, c in chips()
    ]
    return lax.ppermute(a, "dp", pairs)


def shift_second(a, by):
    pairs = [
        (dp_index(y, x, c), dp_index(y, (x + by) % SIDE, c) if c else dp_index((y + by) % SIDE, x, c))
        for y, x, c in chips()
    ]
    return lax.ppermute(a, "dp", pairs)


def swap_core(a):
    return lax.ppermute(a, "dp", [(i, i ^ 1) for i in range(2 * SIDE * SIDE)])


def place():
    i = lax.axis_index("dp")
    return i // (2 * SIDE), (i // 2) % SIDE, i % 2


def here():
    return jnp.stack(place()).astype(jnp.int32)


def pick(k, values):
    out = jnp.int32(values[0])
    for i in range(1, len(values)):
        out = jnp.where(k == i, values[i], out)
    return out


def pair_steps(core):
    return jnp.where(core == 0, jnp.array([0, 1, 3, 2]), jnp.array([0, 3, 1, 2])).astype(jnp.int32)


def add_low(near, got):
    return (near + got.astype(F32)).astype(BF16)


def send_sum(near, got):
    return (near[PART:] + got[PART:].astype(F32)).astype(BF16)


def split_sum(near, got):
    k = near.shape[0] // 2
    keep = near[:k].astype(F32) + got[:k].astype(F32)
    return keep, (near[k:].astype(F32) + got[k:].astype(F32)).astype(BF16)


def place_kernel(here_ref, mine_ref, other_ref, qkv_ref, output_ref):
    y, x, core = here_ref[0], here_ref[1], here_ref[2]

    @pl.loop(0, SIDE * SIDE)
    def _(k):
        first, second = pick(k // SIDE, (0, 3, 1, 2)), pick(k % SIDE, (0, 3, 1, 2))
        for own, blocks_ref in ((True, mine_ref), (False, other_ref)):
            c = core if own else 1 - core
            along_x, along_y = jnp.where(c == 0, first, second), jnp.where(c == 0, second, first)
            chip = ((y + along_y) % SIDE) * SIDE + (x + along_x) % SIDE
            qkv_ref[chip, c] = blocks_ref[k, :, :QKV_COLS]
            output_ref[chip, c] = blocks_ref[k, :, QKV_COLS:]


def place_attention(mine, other):
    parts = pl.pallas_call(
        place_kernel,
        out_shape=[
            jax.ShapeDtypeStruct((SIDE * SIDE, 2, 64, n), mine.dtype)
            for n in (QKV_COLS, QUERY_COLS)
        ],
        in_specs=[pl.BlockSpec(memory_space=pltpu.SMEM)] + whole(2),
        out_specs=whole(2),
        compiler_params=pltpu.CompilerParams(vmem_limit_bytes=32 * 2**20),
        cost_estimate=cost(3),
    )(here(), mine, other)
    return [p.reshape(D, -1) for p in parts]


def pair_first(a, step, x_first):
    return (pair_x if x_first else pair_y)(a, step)


def pair_second(a, step, x_first):
    return (pair_y if x_first else pair_x)(a, step)


def nt(a, b):
    return lax.dot_general(a, b, (((1,), (1,)), ((), ())), preferred_element_type=F32)


def tn(a, b):
    return lax.dot_general(a, b, (((0,), (0,)), ((), ())), preferred_element_type=F32)


def nn(a, b):
    return lax.dot_general(a, b, (((1,), (0,)), ((), ())), preferred_element_type=F32)


def whole(n):
    return [pl.BlockSpec(memory_space=pltpu.VMEM)] * n


def prepare_kernel(
    gains_ref, query_ref, keyvalue_ref, output_ref, gateup_ref, down_ref, part_ref, ffn_ref
):
    gains = gains_ref[...].astype(BF16).astype(F32).T
    scaled = lambda k, w: (w.astype(BF16).astype(F32) * gains[:, k : k + 1]).astype(BF16)
    part_ref[:, :QUERY_COLS] = scaled(0, query_ref[...])
    part_ref[:, QUERY_COLS:QKV_COLS] = scaled(
        0, jnp.concatenate([keyvalue_ref[0], keyvalue_ref[1]], axis=1)
    )
    part_ref[:, QKV_COLS:] = output_ref[...].astype(BF16)
    ffn_ref[:, :HIDDEN] = scaled(1, gateup_ref[0])
    ffn_ref[:, HIDDEN : 2 * HIDDEN] = scaled(1, gateup_ref[1])
    ffn_ref[:, 2 * HIDDEN :] = down_ref[...].astype(BF16)


def prepare(norm_gains, query, keyvalue, output, gateup, down):
    full = lambda v: pl.BlockSpec(v.shape, lambda i: (0,) * len(v.shape))
    arrays = (norm_gains, query, keyvalue, output.T, gateup, down.T)
    outs = [jax.ShapeDtypeStruct((64, n), BF16) for n in (QKV_COLS + QUERY_COLS, 3 * HIDDEN)]
    return pl.pallas_call(
        prepare_kernel,
        out_shape=outs,
        grid=(1,),
        in_specs=[full(v) for v in arrays],
        out_specs=[full(v) for v in outs],
        compiler_params=pltpu.CompilerParams(vmem_limit_bytes=60 * 2**20),
        cost_estimate=cost(2),
    )(*arrays)


def back_kernel(gate_ref, up_ref, gate_w_ref, up_w_ref, near_ref, far_ref):
    out = nt(gate_ref[...], gate_w_ref[...]) + nt(up_ref[...], up_w_ref[...])
    near_ref[...] = out[: SEQ // 2]
    far_ref[...] = out[SEQ // 2 :].astype(BF16)


def back_to_rows(grad_gate, grad_up, weights):
    tile = 512
    grad = pl.BlockSpec((SEQ, HIDDEN), lambda i: (0, 0))
    weight = lambda at: pl.BlockSpec((tile, HIDDEN), lambda i: (i, at))
    out = pl.BlockSpec((SEQ // 2, tile), lambda i: (0, i))
    return pl.pallas_call(
        back_kernel,
        out_shape=[jax.ShapeDtypeStruct((SEQ // 2, D), t) for t in (F32, BF16)],
        grid=(D // tile,),
        in_specs=[grad, grad, weight(0), weight(1)],
        out_specs=[out, out],
        compiler_params=pltpu.CompilerParams(vmem_limit_bytes=32 * 2**20),
        cost_estimate=cost(10),
    )(grad_gate, grad_up, weights, weights)


def turn_kernel(near_ref, far_ref, turned_ref):
    turned_ref[:, : SEQ // 2] = near_ref[...].T
    turned_ref[:, SEQ // 2 :] = far_ref[...].T


def turned(near, far, us=1):
    return pl.pallas_call(
        turn_kernel,
        out_shape=jax.ShapeDtypeStruct((D, SEQ), BF16),
        in_specs=whole(2),
        out_specs=whole(1)[0],
        compiler_params=pltpu.CompilerParams(vmem_limit_bytes=16 * 2**20),
        cost_estimate=cost(us),
    )(near, far)


def rows_kernel(a_ref, w_ref, near_ref, far_ref):
    out = nt(a_ref[...], w_ref[...])
    near_ref[...] = out[: SEQ // 2]
    far_ref[...] = out[SEQ // 2 :].astype(BF16)


def product_rows(a, w, at, us):
    k, tile = a.shape[1], 512
    out = pl.BlockSpec((SEQ // 2, tile), lambda i: (0, i))
    return pl.pallas_call(
        rows_kernel,
        out_shape=[jax.ShapeDtypeStruct((SEQ // 2, D), t) for t in (F32, BF16)],
        grid=(D // tile,),
        in_specs=[
            pl.BlockSpec((SEQ, k), lambda i: (0, 0)),
            pl.BlockSpec((tile, k), lambda i: (i, at)),
        ],
        out_specs=[out, out],
        compiler_params=pltpu.CompilerParams(vmem_limit_bytes=24 * 2**20),
        cost_estimate=cost(us),
    )(a, w)


def chip_at(k, here_ref, x_first):
    y, x, core = here_ref[0], here_ref[1], here_ref[2]
    steps = lambda i: pick(i, (0, jnp.where(core == 0, 1, 3), jnp.where(core == 0, 3, 1), 2))
    first, second = steps(k // SIDE), steps(k % SIDE)
    if x_first:
        return (y ^ second) * SIDE + (x ^ first)
    return (y ^ first) * SIDE + (x ^ second)


def chip_products(cuts, refs, row):
    outs = []
    for i, cut in enumerate(cuts):
        a_ref, b_ref = refs[2 * i], refs[2 * i + 1]
        rows = [a_ref[pl.ds(pl.multiple_of(row(j), 64), 64), :] for j in range(SIDE)]
        outs.append(nn(jnp.concatenate(rows, axis=0), b_ref[:, cut]))
    return outs


def other_kernel(cuts, here_ref, *refs):
    step, core = pl.program_id(0), here_ref[2]
    at = 0
    for out in chip_products(cuts, refs, lambda j: (step * SIDE + j) * 128 + (1 - core) * 64):
        for j in range(SIDE):
            refs[-1][j, :, at : at + out.shape[1]] = out[j * 64 : j * 64 + 64].astype(BF16)
        at += out.shape[1]


def mine_kernel(cuts, x_first, here_ref, *refs):
    step, core = pl.program_id(0), here_ref[2]
    got = refs[2 * len(cuts) : 2 * len(cuts) + SIDE]
    row = lambda j: chip_at(step * SIDE + j, here_ref, x_first) * 128 + core * 64
    outs = chip_products(cuts, refs, row)
    for half, out_ref in enumerate(refs[-2:]):

        @pl.when(step // 2 == half)
        def _():
            at = 0
            for out in outs:
                cols = slice(at, at + out.shape[1])
                for j in range(SIDE):
                    sums = out[j * 64 : j * 64 + 64] + got[j][0, :, cols].astype(F32)
                    out_ref[j, :, cols] = sums.astype(BF16)
                at = cols.stop


def weight_products(pairs, got, x_first, us):
    cuts = [c for _, _, c in pairs]
    arrays = [v for a, b, _ in pairs for v in (a, b)]
    n = sum(c.stop - c.start for c in cuts)
    full = lambda v: pl.BlockSpec(v.shape, lambda i, h: (0, 0))
    block = (SIDE, 64, n)
    if got is None:
        kernel = functools.partial(other_kernel, cuts)
        specs = [full(v) for v in arrays]
        outs = jax.ShapeDtypeStruct((SIDE * SIDE, 64, n), BF16)
        out_specs = pl.BlockSpec(block, lambda i, h: (i, 0, 0))
    else:
        kernel = functools.partial(mine_kernel, cuts, x_first)
        chips = [
            pl.BlockSpec((1, 64, n), lambda i, h, j=j: (chip_at(i * SIDE + j, h, x_first), 0, 0))
            for j in range(SIDE)
        ]
        specs = [full(v) for v in arrays] + chips
        arrays = arrays + [got] * SIDE
        outs = [jax.ShapeDtypeStruct((2 * SIDE, 64, n), BF16)] * 2
        out_specs = [
            pl.BlockSpec(block, lambda i, h: (jnp.minimum(i, 1), 0, 0)),
            pl.BlockSpec(block, lambda i, h: (jnp.maximum(i - 2, 0), 0, 0)),
        ]
    return pl.pallas_call(
        kernel,
        out_shape=outs,
        grid_spec=pltpu.PrefetchScalarGridSpec(
            num_scalar_prefetch=1, grid=(SIDE,), in_specs=specs, out_specs=out_specs
        ),
        compiler_params=pltpu.CompilerParams(vmem_limit_bytes=24 * 2**20),
        cost_estimate=cost(us),
    )(here(), *arrays)


def first_norm_kernel(v_ref, _, low_ref, size_ref):
    v = v_ref[...]
    square = jnp.mean(v * v, axis=-1, keepdims=True) + EPS
    low_ref[...] = (v * lax.rsqrt(square)).astype(BF16)
    size_ref[...] = jnp.broadcast_to(jnp.sqrt(square), size_ref.shape)


def first_norm(residual, part):
    block = pl.BlockSpec((32, D), lambda i: (i, 0))
    return pl.pallas_call(
        first_norm_kernel,
        out_shape=[
            jax.ShapeDtypeStruct((PART, D), BF16), jax.ShapeDtypeStruct((PART, 128), F32)
        ],
        grid=(PART // 32,),
        in_specs=[block, pl.BlockSpec(memory_space=pl.ANY)],
        out_specs=[block, pl.BlockSpec((32, 128), lambda i: (i, 0))],
        compiler_params=pltpu.CompilerParams(vmem_limit_bytes=12 * 2**20),
        cost_estimate=cost(1),
    )(residual, part)


def pair_norm_kernel(
    sum_ref, got_ref, residual_ref, normed_ref, size_ref, own_ref, partner_ref, low_ref
):
    own = pl.program_id(0) < PART // 64
    base = jnp.where(own, residual_ref[...], normed_ref[...].astype(F32) * size_ref[:, :1])
    v = base + (sum_ref[...].astype(F32) + got_ref[...].astype(F32))
    inverse = lax.rsqrt(jnp.mean(v * v, axis=-1, keepdims=True) + EPS)
    low_ref[...] = (v * inverse).astype(BF16)

    @pl.when(own)
    def _():
        own_ref[...] = v

    @pl.when(jnp.logical_not(own))
    def _():
        partner_ref[...] = v.astype(BF16)


def pair_norm_back_kernel(
    sum_ref, got_ref, v_ref, partner_ref, cotangent_ref, low_cotangent_ref, out_ref, low_ref
):
    own = pl.program_id(0) < PART // 64
    base = jnp.where(own, cotangent_ref[...], low_cotangent_ref[...].astype(F32))
    v = jnp.where(own, v_ref[...], partner_ref[...].astype(F32))
    u = sum_ref[...].astype(F32) + got_ref[...].astype(F32)
    inverse = lax.rsqrt(jnp.mean(v * v, axis=-1, keepdims=True) + EPS)
    inner = jnp.mean(u * v, axis=-1, keepdims=True)
    out = base + (inverse * u - v * (inverse * inverse * inverse * inner))
    low_ref[...] = out.astype(BF16)

    @pl.when(own)
    def _():
        out_ref[...] = out


HALF = PART // 64
EACH, ACROSS = (lambda i: i), (lambda i: (i + HALF) % (2 * HALF))
OWN, PARTNER = (lambda i: jnp.minimum(i, HALF - 1)), (lambda i: jnp.maximum(i - HALF, 0))


def by_pair_rows(kernel, ins, outs):
    block = lambda n, at: pl.BlockSpec((64, n), lambda i: (at(i), 0))
    rows = lambda at: 2 * PART if at is EACH else PART
    return pl.pallas_call(
        kernel,
        out_shape=[jax.ShapeDtypeStruct((rows(at), D), t) for t, at in outs],
        grid=(2 * HALF,),
        in_specs=[block(a.shape[1], at) for a, at in ins],
        out_specs=[block(D, at) for _, at in outs],
        compiler_params=pltpu.CompilerParams(vmem_limit_bytes=24 * 2**20),
        cost_estimate=cost(2),
    )(*[a for a, _ in ins])


def norm_back_kernel(near_ref, got_ref, got_own_ref, v_ref, base_ref, out_ref, low_ref):
    u = near_ref[...] + (got_ref[...].astype(F32) + got_own_ref[...].astype(F32))
    v = v_ref[...]
    inverse = lax.rsqrt(jnp.mean(v * v, axis=-1, keepdims=True) + EPS)
    inner = jnp.mean(u * v, axis=-1, keepdims=True)
    out = base_ref[...] + (inverse * u - v * (inverse * inverse * inverse * inner))
    out_ref[...] = out
    low_ref[...] = out.astype(BF16)


def by_rows(kernel, *arrays):
    block = pl.BlockSpec((32, D), lambda i: (i, 0))
    return pl.pallas_call(
        kernel,
        out_shape=[jax.ShapeDtypeStruct((PART, D), t) for t in (F32, BF16)],
        grid=(PART // 32,),
        in_specs=[block] * len(arrays),
        out_specs=[block, block],
        compiler_params=pltpu.CompilerParams(vmem_limit_bytes=12 * 2**20),
        cost_estimate=cost(1.5),
    )(*arrays)


def hidden_kernel(
    near_ref, far_ref, gate_w_ref, up_w_ref, grad_hidden_ref,
    hidden_ref, grad_gate_ref, grad_up_ref, rows_ref,
):
    @pl.when(pl.program_id(0) == 0)
    def _():
        rows_ref[: SEQ // 2, :] = near_ref[...]
        rows_ref[SEQ // 2 :, :] = far_ref[...]

    gate_up = nn(rows_ref[...], jnp.concatenate([gate_w_ref[...], up_w_ref[...]], axis=1))
    grad_hidden = grad_hidden_ref[...]
    gate, up = gate_up[:, :128], gate_up[:, 128:]
    sigmoid = 1.0 / (1.0 + jnp.exp(-gate))
    activated = gate * sigmoid
    slope = sigmoid * (1.0 + gate * (1.0 - sigmoid))
    hidden_ref[...] = (activated * up).astype(BF16)
    grad_gate_ref[...] = (grad_hidden * up * slope).astype(BF16)
    grad_up_ref[...] = (grad_hidden * activated).astype(BF16)


def hidden_units(near, far, grad_hidden, weights):
    steps = HIDDEN // 128
    weight = lambda at: pl.BlockSpec((D, 128), lambda j: (0, at * steps + j))
    return pl.pallas_call(
        hidden_kernel,
        out_shape=[jax.ShapeDtypeStruct((SEQ, HIDDEN), BF16)] * 3,
        grid=(steps,),
        in_specs=whole(2)
        + [weight(0), weight(1), pl.BlockSpec((SEQ, 128), lambda j: (0, j))],
        out_specs=[pl.BlockSpec((SEQ, 128), lambda j: (0, j))] * 3,
        scratch_shapes=[pltpu.VMEM((SEQ, D), BF16)],
        compiler_params=pltpu.CompilerParams(vmem_limit_bytes=24 * 2**20),
        cost_estimate=cost(10),
    )(near, far, weights, weights, grad_hidden)


def turn(x, cosine, sine):
    lane = lax.broadcasted_iota(jnp.int32, x.shape, 1)
    ahead = pltpu.roll(x, 96, 1)
    behind = pltpu.roll(x, 32, 1)
    return x * cosine + jnp.where(lane % HEAD_DIM < HEAD_DIM // 2, ahead, behind) * sine


def mask_bias(ends_ref, block):
    shape = ((block + 1) * PART, PART)
    key = lax.broadcasted_iota(jnp.int32, shape, 0)
    query = lax.broadcasted_iota(jnp.int32, shape, 1) + block * PART
    key_segment = jnp.zeros(shape, jnp.int32)
    query_segment = jnp.zeros(shape, jnp.int32)
    for d in range(4):
        key_segment += (key >= ends_ref[d]).astype(jnp.int32)
        query_segment += (query >= ends_ref[d]).astype(jnp.int32)
    return jnp.where((key_segment == query_segment) & (key <= query), 0.0, -1e30)


def halves(x):
    none = jnp.zeros_like(x)
    return jnp.concatenate([x, none], axis=1), jnp.concatenate([none, x], axis=1)


def in_token_order(slot_ref, kv_ref, ordered_ref):
    for block in range(SIDE):
        rows = pl.ds(pl.multiple_of(slot_ref[block] * PART, PART), PART)
        ordered_ref[block * PART : (block + 1) * PART, :] = kv_ref[rows, :]


def forward_kernel(
    slot_ref, ends_ref, qkv_ref, cos_ref, sin_ref, att_ref, q_ref, kv_ref, lse_ref, ordered_ref
):
    cosine, sine = cos_ref[...], sin_ref[...]
    for pair in range(HEADS_LOCAL // 2):
        cols = slice(pair * 128, pair * 128 + 128)
        q_ref[:, cols] = (turn(qkv_ref[:, cols], cosine, sine).astype(BF16)) * BF16(0.125)
    kv = qkv_ref[:, QUERY_COLS:QKV_COLS]
    lane = lax.broadcasted_iota(jnp.int32, kv.shape, 1)
    kv_ref[...] = jnp.where(lane < HEAD_DIM, turn(kv, cosine, sine), kv).astype(BF16)
    in_token_order(slot_ref, kv_ref, ordered_ref)
    kv = ordered_ref[...]
    keys_both = halves(kv[:, :HEAD_DIM])
    values_turned = kv.astype(F32).T[HEAD_DIM:].astype(BF16)
    heads = range(HEADS_LOCAL)
    for block in range(SIDE):
        seen = (block + 1) * PART
        rows = pl.ds(pl.multiple_of(slot_ref[block] * PART, PART), PART)
        bias = mask_bias(ends_ref, block)
        q = [q_ref[rows, k * 128 : (k + 1) * 128] for k in range(HEADS_LOCAL // 2)]
        s = [nt(keys_both[h % 2][:seen], q[h // 2]) + bias for h in heads]
        top = [jnp.max(v, axis=0, keepdims=True) for v in s]
        e = [jnp.exp(v - t) for v, t in zip(s, top)]
        total = [jnp.sum(v, axis=0, keepdims=True) for v in e]
        p = [(v * (1.0 / t)).astype(BF16) for v, t in zip(e, total)]
        out = [nn(values_turned[:, :seen], v) for v in p]
        for h in heads:
            lse_ref[h : h + 1, block * PART : seen] = top[h] + jnp.log(total[h])
        for k in range(HEADS_LOCAL // 2):
            both = jnp.concatenate(out[2 * k : 2 * k + 2], axis=0)
            att_ref[rows, k * 128 : (k + 1) * 128] = both.T.astype(BF16)


def apart(x):
    lane = lax.broadcasted_iota(jnp.int32, x.shape, 1)
    none = jnp.zeros_like(x)
    first = lane < HEAD_DIM
    return jnp.concatenate([jnp.where(first, x, none), jnp.where(first, none, x)], axis=0)


def backward_kernel(
    slot_ref, ends_ref, q_ref, kv_ref, lse_ref, up_ref, cos_ref, sin_ref,
    out_ref, ordered_ref, dk_ref, dv_ref,
):
    in_token_order(slot_ref, kv_ref, ordered_ref)
    kv = ordered_ref[...]
    keys_both, values_both = halves(kv[:, :HEAD_DIM]), halves(kv[:, HEAD_DIM:])
    keys_turned = kv.astype(F32).T[:HEAD_DIM].astype(BF16)
    dk_ref[...] = jnp.zeros_like(dk_ref)
    dv_ref[...] = jnp.zeros_like(dv_ref)
    heads, pairs = range(HEADS_LOCAL), range(HEADS_LOCAL // 2)
    for block in range(SIDE):
        seen = (block + 1) * PART
        rows = pl.ds(pl.multiple_of(slot_ref[block] * PART, PART), PART)
        bias = mask_bias(ends_ref, block)
        cosine, sine = cos_ref[rows, :], -sin_ref[rows, :]
        q = [q_ref[rows, k * 128 : (k + 1) * 128] for k in pairs]
        up = [up_ref[rows, k * 128 : (k + 1) * 128] for k in pairs]
        s = [nt(keys_both[h % 2][:seen], q[h // 2]) + bias for h in heads]
        dp = [nt(values_both[h % 2][:seen], up[h // 2]) for h in heads]
        p = [jnp.exp(s[h] - lse_ref[h : h + 1, block * PART : seen]) for h in heads]
        inner = [jnp.sum(p[h] * dp[h], axis=0, keepdims=True) for h in heads]
        ds = [(p[h] * (dp[h] - inner[h])).astype(BF16) for h in heads]
        p = [v.astype(BF16) for v in p]
        dq = [nn(keys_turned[:, :seen], v) for v in ds]
        q_apart = jnp.concatenate([apart(v) for v in q], axis=0)
        up_apart = jnp.concatenate([apart(v) for v in up], axis=0)
        dk_ref[:seen, :] += nn(jnp.concatenate(ds, axis=1), q_apart)
        dv_ref[:seen, :] += nn(jnp.concatenate(p, axis=1), up_apart)
        for k in pairs:
            both = jnp.concatenate(dq[2 * k : 2 * k + 2], axis=0).T * 0.125
            out_ref[rows, k * 128 : (k + 1) * 128] = turn(both, cosine, sine).astype(BF16)
    lane = lax.broadcasted_iota(jnp.int32, (SEQ, 128), 1)
    dk, dv = dk_ref[...], dv_ref[...]
    dk, dv = dk + pltpu.roll(dk, HEAD_DIM, 1), dv + pltpu.roll(dv, HEAD_DIM, 1)
    dk_ref[...] = jnp.where(lane < HEAD_DIM, dk, dv)
    for block in range(SIDE):
        rows = pl.ds(pl.multiple_of(slot_ref[block] * PART, PART), PART)
        dkv = dk_ref[block * PART : (block + 1) * PART, :]
        turned = turn(dkv, cos_ref[rows, :], -sin_ref[rows, :])
        dkv = jnp.where(lane[:PART] < HEAD_DIM, turned, dkv)
        out_ref[rows, QUERY_COLS:QKV_COLS] = dkv.astype(BF16)


def small(n):
    return [pl.BlockSpec(memory_space=pltpu.SMEM)] * n


def attend_forward(qkv, tables):
    slot, ends, cosine, sine = tables
    return pl.pallas_call(
        forward_kernel,
        out_shape=(
            jax.ShapeDtypeStruct((SEQ, QUERY_COLS), BF16),
            jax.ShapeDtypeStruct((SEQ, QUERY_COLS), BF16),
            jax.ShapeDtypeStruct((SEQ, 128), BF16),
            jax.ShapeDtypeStruct((HEADS_LOCAL, SEQ), F32),
        ),
        in_specs=small(2) + whole(3),
        out_specs=whole(4),
        scratch_shapes=[pltpu.VMEM((SEQ, 128), BF16)],
        compiler_params=pltpu.CompilerParams(vmem_limit_bytes=24 * 2**20),
        cost_estimate=cost(5),
    )(slot, ends, qkv, cosine, sine)


def attend_backward(q, kv, lse, upstream, tables):
    slot, ends, cosine, sine = tables
    return pl.pallas_call(
        backward_kernel,
        out_shape=jax.ShapeDtypeStruct((SEQ, QKV_COLS), BF16),
        in_specs=small(2) + whole(6),
        out_specs=pl.BlockSpec(memory_space=pltpu.VMEM),
        scratch_shapes=[
            pltpu.VMEM((SEQ, 128), BF16),
            pltpu.VMEM((SEQ, 128), F32),
            pltpu.VMEM((SEQ, 128), F32),
        ],
        compiler_params=pltpu.CompilerParams(vmem_limit_bytes=24 * 2**20),
        cost_estimate=cost(6),
    )(slot, ends, q, kv, lse, upstream, cosine, sine)


def attention_tables(lengths):
    block = lax.axis_index("mp") ^ pair_steps(place()[2])
    slot = jnp.sum(
        jnp.where(block[None, :] == jnp.arange(SIDE)[:, None], jnp.arange(SIDE)[None, :], 0), axis=1
    ).astype(jnp.int32)
    token = (block[:, None] * PART + jnp.arange(PART)[None, :]).reshape(SEQ)
    ends = jnp.cumsum(lengths).astype(jnp.int32)
    starts = ends - lengths
    leading = jnp.max(jnp.where(starts[None, :] <= token[:, None], starts[None, :], 0), axis=1)
    indices = jnp.arange(HEAD_DIM // 2).astype(F32)
    frequency = 1.0 / THETA ** (2.0 * indices / HEAD_DIM)
    angles = (token - leading).astype(F32)[:, None] * frequency[None, :]
    cosine, sine = jnp.cos(angles), jnp.sin(angles)
    cosine = jnp.concatenate([cosine] * 4, axis=1)
    sine = jnp.concatenate([-sine, sine, -sine, sine], axis=1)
    return slot, ends, cosine, sine


def adamw(weight, gradient, moment, square, rate, decay):
    momentum = BETA_ONE * moment + (1.0 - BETA_ONE) * gradient
    variance = BETA_TWO * square + (1.0 - BETA_TWO) * gradient * gradient
    moment_hat = momentum / (1.0 - BETA_ONE**STEP)
    square_hat = variance / (1.0 - BETA_TWO**STEP)
    updated = weight - rate * (moment_hat / (jnp.sqrt(square_hat) + ADAM_EPS) + decay * weight)
    return (momentum, variance, updated)


def after(x, *others):
    return lax.optimization_barrier((x, *others))[0]


def on_device(
    residual, cotangent, document_lengths,
    norm_gains, query_weight, keyvalue_weight, output_weight, gateup_weight, down_weight,
    moment_gains, moment_query, moment_keyvalue, moment_output, moment_gateup, moment_down,
    square_gains, square_query, square_keyvalue, square_output, square_gateup, square_down,
):
    residual, cotangent = residual[0], cotangent[0]
    half = SEQ // 2

    part, ffn_part = prepare(
        norm_gains, query_weight, keyvalue_weight, output_weight, gateup_weight, down_weight
    )
    normed_one, size = first_norm(residual, part)
    got_one = pair_z(normed_one, 0)
    got_size = pair_z(size, 0)
    line = jnp.stack([part, shift_first(part, 1), shift_first(part, -1), shift_first(part, 2)])
    ffn_full = lax.all_gather(ffn_part, "dp", axis=0, tiled=True)
    tables = attention_tables(document_lengths[0])
    line = after(line, *tables)
    plane = [line, shift_second(line, 1), shift_second(line, -1), shift_second(line, 2)]
    one_near = after(jnp.concatenate([normed_one, got_one]), line)
    one_far = pair_z(one_near, 1)
    low_cotangent = after(cotangent.astype(BF16), one_near)
    cot_near = jnp.concatenate([low_cotangent, pair_z(low_cotangent, 0)])
    mine = jnp.stack(plane, axis=1).reshape(SIDE * SIDE, *part.shape)
    mine = after(mine, one_far, cot_near)
    other = swap_core(mine)
    cot_far = pair_z(cot_near, 1)
    qkv_full, output_full = place_attention(mine, other)
    qkv = nn(one_near, qkv_full), nn(one_far, qkv_full)
    attended, q, kv, lse = attend_forward(after(jnp.concatenate(qkv), got_size), tables)

    far = nt(after(attended, cot_far)[half:], output_full).astype(BF16)
    got = pair_z(far, 1)
    near = nt(after(attended, far)[:half], output_full)
    cot_turned = turned(after(cot_near, near), cot_far)
    got = after(got, cot_turned)
    sent = add_low(near, got)
    got_pair = pair_z(sent, 0)
    cot_rows = jnp.concatenate([cot_near, cot_far])
    got_pair = after(got_pair, cot_rows)
    middle, partner_middle, two_near = by_pair_rows(
        pair_norm_kernel,
        ((sent, EACH), (got_pair, ACROSS), (residual, OWN), (one_near, EACH), (got_size, PARTNER)),
        ((F32, OWN), (BF16, PARTNER), (BF16, EACH)),
    )
    two_far = pair_z(two_near, 1)
    down_full = ffn_full[:, 2 * HIDDEN :]
    one_turned = turned(after(one_near, two_near), one_far)
    grad_hidden = nn(after(cot_rows, one_turned), down_full)
    two_far = after(two_far, grad_hidden)

    hidden, grad_gate, grad_up = hidden_units(two_near, two_far, grad_hidden, ffn_full)
    near, far = back_to_rows(grad_gate, grad_up, ffn_full)
    got = pair_z(far, 1)
    rows_turned = turned(after(two_near, far), two_far)
    all_columns = slice(0, HIDDEN)
    pairs_a = (
        (rows_turned, grad_gate, all_columns), (cot_turned, hidden, slice(0, SPLIT))
    )
    pairs_b = (
        (rows_turned, grad_up, all_columns), (cot_turned, hidden, slice(SPLIT, HIDDEN))
    )
    other_a = weight_products(pairs_a, None, True, 4)
    other_b = weight_products(pairs_b, None, False, 4)
    got = after(got, other_a, other_b)
    sent = add_low(near, got)
    got_pair = pair_z(sent, 0)
    got_a = swap_core(after(other_a, sent))
    got_b = swap_core(after(other_b, sent))
    down = nt(after(hidden, sent), down_full)
    down_near, down_far = down[:half], down[half:].astype(BF16)
    near_a, far_a = weight_products(pairs_a, after(got_a, down), True, 4)
    got_a = pair_first(far_a, 1, True)
    got_pair = after(got_pair, near_a)

    grad_middle, rows_near = by_pair_rows(
        pair_norm_back_kernel,
        (
            (sent, EACH), (got_pair, ACROSS), (middle, OWN), (partner_middle, PARTNER),
            (cotangent, OWN), (cot_near, EACH),
        ),
        ((F32, OWN), (BF16, EACH)),
    )
    rows_far = pair_z(rows_near, 1)
    near_b, far_b = weight_products(pairs_b, after(got_b, rows_near), False, 0.001)
    got_b = pair_first(far_b, 1, False)
    grad_attended = nn(after(rows_near, near_b), output_full).astype(BF16)
    rows_far = after(rows_far, grad_attended)
    grad_attended = jnp.concatenate([grad_attended, nn(rows_far, output_full).astype(BF16)])
    grad_projected = attend_backward(q, kv, lse, grad_attended, tables)
    pairs_qkv = ((one_turned, grad_projected, slice(0, QKV_COLS)),)
    other_qkv = weight_products(pairs_qkv, None, True, 1)
    got_qkv = swap_core(other_qkv)
    near, far = product_rows(after(grad_projected, other_qkv), qkv_full, 0, 2)
    got = pair_z(far, 1)
    keep_a, sent_a = split_sum(near_a, after(got_a, far))
    got_a = pair_first(sent_a, 0, True)
    middle_turned = turned(after(rows_near, sent_a), rows_far, 0.001)
    pairs_output = ((middle_turned, attended, slice(0, QUERY_COLS)),)
    other_output = weight_products(pairs_output, None, False, 0.001)
    got_output = swap_core(other_output)
    keep_b, sent_b = split_sum(near_b, after(got_b, other_output))
    got_b = pair_first(sent_b, 0, False)
    near_qkv, far_qkv = weight_products(pairs_qkv, after(got_qkv, sent_b), True, 0.001)
    got_qkv = pair_first(far_qkv, 1, True)
    near_output, far_output = weight_products(
        pairs_output, after(got_output, near_qkv), False, 0.001
    )
    got_output = pair_first(far_output, 1, False)
    got = after(got, near_output)
    sent = send_sum(near, got)
    got_own = pair_z(sent, 0)

    keep_qkv, sent_qkv = split_sum(near_qkv, after(got_qkv, sent))
    got_qkv = pair_first(sent_qkv, 0, True)
    line_a = (keep_a + after(got_a, sent_qkv).astype(F32)).astype(BF16)
    got_a = pair_second(line_a[2:], 1, True)
    keep_output, sent_output = split_sum(near_output, after(got_output, line_a))
    got_output = pair_first(sent_output, 0, False)
    got_own = after(got_own, sent_output)
    input_gradient, _ = by_rows(norm_back_kernel, near, got, got_own, residual, grad_middle)
    got_down = pair_z(after(down_far, got_own), 1)
    line_b = (keep_b + after(got_b, got_own).astype(F32)).astype(BF16)
    got_b = pair_second(line_b[2:], 1, False)
    line_qkv = (keep_qkv + after(got_qkv, line_b).astype(F32)).astype(BF16)
    got_qkv = pair_second(line_qkv[2:], 1, True)
    line_output = (keep_output + after(got_output, line_qkv).astype(F32)).astype(BF16)
    got_output = pair_second(line_output[2:], 1, False)
    keep_a, sent_a = split_sum(line_a[:2], after(got_a, line_output))
    got_a = pair_second(sent_a, 0, True)
    keep_qkv, sent_qkv = split_sum(line_qkv[:2], after(got_qkv, sent_a))
    got_qkv = pair_second(sent_qkv, 0, True)
    got_down = after(got_down, sent_qkv)
    sent_down = send_sum(down_near, got_down)
    got_down_own = pair_z(sent_down, 0)
    keep_b, sent_b = split_sum(line_b[:2], after(got_b, sent_down))
    got_b = pair_second(sent_b, 0, False)
    keep_output, sent_output = split_sum(line_output[:2], after(got_output, sent_b))
    got_output = pair_second(sent_output, 0, False)
    grad_ffn_a = keep_a[0] + got_a[0].astype(F32)
    grad_qkv = keep_qkv[0] + got_qkv[0].astype(F32)
    grad_ffn_b = keep_b[0] + got_b[0].astype(F32)
    block_output = middle + (
        down_near[:PART] + (got_down[:PART].astype(F32) + got_down_own.astype(F32))
    )

    low_gains = norm_gains.astype(BF16).astype(F32)
    gain_one, gain_two = low_gains[0][:, None], low_gains[1][:, None]
    low_qkv = jnp.concatenate(
        (query_weight, keyvalue_weight[0], keyvalue_weight[1]), axis=1
    ).astype(BF16)
    low_gate, low_up = (w.astype(BF16).astype(F32) for w in (gateup_weight[0], gateup_weight[1]))
    gain_parts = jnp.stack(
        (
            jnp.sum(low_qkv.astype(F32) * grad_qkv, axis=1),
            jnp.sum(low_gate * grad_ffn_a[:, :HIDDEN], axis=1)
            + jnp.sum(low_up * grad_ffn_b[:, :HIDDEN], axis=1),
        )
    )
    grad_output = keep_output[0] + after(got_output, gain_parts)[0].astype(F32)
    gains = gain_parts + shift_z(gain_parts, 1) + shift_z(gain_parts, -1) + shift_z(gain_parts, 2)
    grad_qkv = grad_qkv * gain_one
    reduced = (
        gains,
        grad_qkv[:, :QUERY_COLS],
        jnp.stack((grad_qkv[:, QUERY_COLS : QUERY_COLS + 64], grad_qkv[:, QUERY_COLS + 64 :])),
        grad_output.T,
        jnp.stack((grad_ffn_a[:, :HIDDEN] * gain_two, grad_ffn_b[:, :HIDDEN] * gain_two)),
        jnp.concatenate((grad_ffn_a[:, HIDDEN:], grad_ffn_b[:, HIDDEN:]), axis=1).T,
    )
    masters = (norm_gains, query_weight, keyvalue_weight, output_weight, gateup_weight, down_weight)
    moments = (
        moment_gains, moment_query, moment_keyvalue, moment_output, moment_gateup, moment_down,
    )
    squares = (
        square_gains, square_query, square_keyvalue, square_output, square_gateup, square_down,
    )
    results = [
        adamw(masters[i], reduced[i], moments[i], squares[i], RATES[i], DECAYS[i]) for i in range(6)
    ]
    return (
        block_output[None],
        input_gradient[None],
        *reduced,
        *(r[0] for r in results),
        *(r[1] for r in results),
        *(r[2] for r in results),
    )


def solution(mesh):
    rows = P("dp", "mp", None)
    weights = (
        P(None, "dp"),
        P("dp", "mp"),
        P(None, "dp", "mp"),
        P("mp", "dp"),
        P(None, "dp", "mp"),
        P("mp", "dp"),
    )
    return jax.shard_map(
        on_device,
        mesh=mesh,
        in_specs=(rows, rows, P("dp", None), *weights, *weights, *weights),
        out_specs=(rows, rows, *weights, *weights, *weights, *weights),
        check_vma=False,
    )
```

```python
import functools

import jax
import jax.numpy as jnp
from jax import lax
from jax.experimental import pallas as pl
from jax.experimental.pallas import tpu as pltpu
from jax.sharding import PartitionSpec as P

HEAD_DIM = 64
HEADS_LOCAL = 8
QUERY_COLS = 512
QKV_COLS = 640
HIDDEN = 1408
SEQ = 512
PART = 128
D = 2048
STEP = 10

EPS = 1e-05
THETA = 10000.0
BETA_ONE = 0.9
BETA_TWO = 0.95
ADAM_EPS = 1e-08
RATES = (1.0, 0.05, 0.05, 0.5, 0.05, 0.025)
DECAYS = (0.0, 0.1, 0.1, 0.1, 0.1, 0.1)
SIDE = 4
BF16 = jnp.bfloat16
F32 = jnp.float32
SPLIT = 768


def cost(us):
    return pl.CostEstimate(
        flops=int(us * 1.1e9), bytes_accessed=int(us * 3.0e6), transcendentals=0
    )


def pair_mask(core, step):
    return (1, 3)[step] if core == 0 else (3, 1)[step]


def dp_index(y, x, core):
    return (y * SIDE + x) * 2 + core


def chips():
    return [(y, x, c) for y in range(SIDE) for x in range(SIDE) for c in range(2)]


def pair_z(a, step):
    pairs = [
        (dp * SIDE + z, dp * SIDE + (z ^ pair_mask(dp % 2, step)))
        for dp in range(2 * SIDE * SIDE)
        for z in range(SIDE)
    ]
    return lax.ppermute(a, ("dp", "mp"), pairs)


def pair_x(a, step):
    pairs = [(dp_index(y, x, c), dp_index(y, x ^ pair_mask(c, step), c)) for y, x, c in chips()]
    return lax.ppermute(a, "dp", pairs)


def pair_y(a, step):
    pairs = [(dp_index(y, x, c), dp_index(y ^ pair_mask(c, step), x, c)) for y, x, c in chips()]
    return lax.ppermute(a, "dp", pairs)


def shift_z(x, by):
    return lax.ppermute(x, "mp", [(i, (i + by) % SIDE) for i in range(SIDE)])


def shift_first(a, by):
    pairs = [
        (dp_index(y, x, c), dp_index((y + by) % SIDE, x, c) if c else dp_index(y, (x + by) % SIDE, c))
        for y, x, c in chips()
    ]
    return lax.ppermute(a, "dp", pairs)


def shift_second(a, by):
    pairs = [
        (dp_index(y, x, c), dp_index(y, (x + by) % SIDE, c) if c else dp_index((y + by) % SIDE, x, c))
        for y, x, c in chips()
    ]
    return lax.ppermute(a, "dp", pairs)


def swap_core(a):
    return lax.ppermute(a, "dp", [(i, i ^ 1) for i in range(2 * SIDE * SIDE)])


def place():
    i = lax.axis_index("dp")
    return i // (2 * SIDE), (i // 2) % SIDE, i % 2


def here():
    return jnp.stack(place()).astype(jnp.int32)


def pick(k, values):
    out = jnp.int32(values[0])
    for i in range(1, len(values)):
        out = jnp.where(k == i, values[i], out)
    return out


def pair_steps(core):
    return jnp.where(core == 0, jnp.array([0, 1, 3, 2]), jnp.array([0, 3, 1, 2])).astype(jnp.int32)


def add_low(near, got):
    return (near + got.astype(F32)).astype(BF16)


def send_sum(near, got):
    return (near[PART:] + got[PART:].astype(F32)).astype(BF16)


def split_sum(near, got):
    k = near.shape[0] // 2
    keep = near[:k].astype(F32) + got[:k].astype(F32)
    return keep, (near[k:].astype(F32) + got[k:].astype(F32)).astype(BF16)


def place_kernel(here_ref, mine_ref, other_ref, qkv_ref, output_ref):
    y, x, core = here_ref[0], here_ref[1], here_ref[2]

    @pl.loop(0, SIDE * SIDE)
    def _(k):
        first, second = pick(k // SIDE, (0, 3, 1, 2)), pick(k % SIDE, (0, 3, 1, 2))
        for own, blocks_ref in ((True, mine_ref), (False, other_ref)):
            c = core if own else 1 - core
            along_x, along_y = jnp.where(c == 0, first, second), jnp.where(c == 0, second, first)
            chip = ((y + along_y) % SIDE) * SIDE + (x + along_x) % SIDE
            qkv_ref[chip, c] = blocks_ref[k, :, :QKV_COLS]
            output_ref[chip, c] = blocks_ref[k, :, QKV_COLS:]


def place_attention(mine, other):
    parts = pl.pallas_call(
        place_kernel,
        out_shape=[
            jax.ShapeDtypeStruct((SIDE * SIDE, 2, 64, n), mine.dtype)
            for n in (QKV_COLS, QUERY_COLS)
        ],
        in_specs=[pl.BlockSpec(memory_space=pltpu.SMEM)] + whole(2),
        out_specs=whole(2),
        compiler_params=pltpu.CompilerParams(vmem_limit_bytes=32 * 2**20),
        cost_estimate=cost(3),
    )(here(), mine, other)
    return [p.reshape(D, -1) for p in parts]


def pair_first(a, step, x_first):
    return (pair_x if x_first else pair_y)(a, step)


def pair_second(a, step, x_first):
    return (pair_y if x_first else pair_x)(a, step)


def nt(a, b):
    return lax.dot_general(a, b, (((1,), (1,)), ((), ())), preferred_element_type=F32)


def tn(a, b):
    return lax.dot_general(a, b, (((0,), (0,)), ((), ())), preferred_element_type=F32)


def nn(a, b):
    return lax.dot_general(a, b, (((1,), (0,)), ((), ())), preferred_element_type=F32)


def whole(n):
    return [pl.BlockSpec(memory_space=pltpu.VMEM)] * n


def prepare_kernel(
    gains_ref, query_ref, keyvalue_ref, output_ref, gateup_ref, down_ref, part_ref, ffn_ref
):
    gains = gains_ref[...].astype(BF16).astype(F32).T
    scaled = lambda k, w: (w.astype(BF16).astype(F32) * gains[:, k : k + 1]).astype(BF16)
    part_ref[:, :QUERY_COLS] = scaled(0, query_ref[...])
    part_ref[:, QUERY_COLS:QKV_COLS] = scaled(
        0, jnp.concatenate([keyvalue_ref[0], keyvalue_ref[1]], axis=1)
    )
    part_ref[:, QKV_COLS:] = output_ref[...].astype(BF16)
    ffn_ref[:, :HIDDEN] = scaled(1, gateup_ref[0])
    ffn_ref[:, HIDDEN : 2 * HIDDEN] = scaled(1, gateup_ref[1])
    ffn_ref[:, 2 * HIDDEN :] = down_ref[...].astype(BF16)


def prepare(norm_gains, query, keyvalue, output, gateup, down):
    full = lambda v: pl.BlockSpec(v.shape, lambda i: (0,) * len(v.shape))
    arrays = (norm_gains, query, keyvalue, output.T, gateup, down.T)
    outs = [jax.ShapeDtypeStruct((64, n), BF16) for n in (QKV_COLS + QUERY_COLS, 3 * HIDDEN)]
    return pl.pallas_call(
        prepare_kernel,
        out_shape=outs,
        grid=(1,),
        in_specs=[full(v) for v in arrays],
        out_specs=[full(v) for v in outs],
        compiler_params=pltpu.CompilerParams(vmem_limit_bytes=60 * 2**20),
        cost_estimate=cost(2),
    )(*arrays)


def back_kernel(gate_ref, up_ref, gate_w_ref, up_w_ref, near_ref, far_ref):
    out = nt(gate_ref[...], gate_w_ref[...]) + nt(up_ref[...], up_w_ref[...])
    near_ref[...] = out[: SEQ // 2]
    far_ref[...] = out[SEQ // 2 :].astype(BF16)


def back_to_rows(grad_gate, grad_up, weights):
    tile = 512
    grad = pl.BlockSpec((SEQ, HIDDEN), lambda i: (0, 0))
    weight = lambda at: pl.BlockSpec((tile, HIDDEN), lambda i: (i, at))
    out = pl.BlockSpec((SEQ // 2, tile), lambda i: (0, i))
    return pl.pallas_call(
        back_kernel,
        out_shape=[jax.ShapeDtypeStruct((SEQ // 2, D), t) for t in (F32, BF16)],
        grid=(D // tile,),
        in_specs=[grad, grad, weight(0), weight(1)],
        out_specs=[out, out],
        compiler_params=pltpu.CompilerParams(vmem_limit_bytes=24 * 2**20),
        cost_estimate=cost(10),
    )(grad_gate, grad_up, weights, weights)


def turn_kernel(near_ref, far_ref, turned_ref):
    turned_ref[:, : SEQ // 2] = near_ref[...].T
    turned_ref[:, SEQ // 2 :] = far_ref[...].T


def turned(near, far, us=1):
    return pl.pallas_call(
        turn_kernel,
        out_shape=jax.ShapeDtypeStruct((D, SEQ), BF16),
        in_specs=whole(2),
        out_specs=whole(1)[0],
        compiler_params=pltpu.CompilerParams(vmem_limit_bytes=16 * 2**20),
        cost_estimate=cost(us),
    )(near, far)


def rows_kernel(a_ref, w_ref, near_ref, far_ref):
    out = nt(a_ref[...], w_ref[...])
    near_ref[...] = out[: SEQ // 2]
    far_ref[...] = out[SEQ // 2 :].astype(BF16)


def product_rows(a, w, at, us):
    k, tile = a.shape[1], 512
    out = pl.BlockSpec((SEQ // 2, tile), lambda i: (0, i))
    return pl.pallas_call(
        rows_kernel,
        out_shape=[jax.ShapeDtypeStruct((SEQ // 2, D), t) for t in (F32, BF16)],
        grid=(D // tile,),
        in_specs=[
            pl.BlockSpec((SEQ, k), lambda i: (0, 0)),
            pl.BlockSpec((tile, k), lambda i: (i, at)),
        ],
        out_specs=[out, out],
        compiler_params=pltpu.CompilerParams(vmem_limit_bytes=16 * 2**20),
        cost_estimate=cost(us),
    )(a, w)


def chip_at(k, here_ref, x_first):
    y, x, core = here_ref[0], here_ref[1], here_ref[2]
    steps = lambda i: pick(i, (0, jnp.where(core == 0, 1, 3), jnp.where(core == 0, 3, 1), 2))
    first, second = steps(k // SIDE), steps(k % SIDE)
    if x_first:
        return (y ^ second) * SIDE + (x ^ first)
    return (y ^ first) * SIDE + (x ^ second)


def chip_products(cuts, refs, row):
    outs = []
    for i, cut in enumerate(cuts):
        a_ref, b_ref = refs[2 * i], refs[2 * i + 1]
        rows = [a_ref[pl.ds(pl.multiple_of(row(j), 64), 64), :] for j in range(SIDE)]
        outs.append(nn(jnp.concatenate(rows, axis=0), b_ref[:, cut]))
    return outs


def other_kernel(cuts, here_ref, *refs):
    step, core = pl.program_id(0), here_ref[2]
    at = 0
    for out in chip_products(cuts, refs, lambda j: (step * SIDE + j) * 128 + (1 - core) * 64):
        for j in range(SIDE):
            refs[-1][j, :, at : at + out.shape[1]] = out[j * 64 : j * 64 + 64].astype(BF16)
        at += out.shape[1]


def mine_kernel(cuts, x_first, here_ref, *refs):
    step, core = pl.program_id(0), here_ref[2]
    got = refs[2 * len(cuts) : 2 * len(cuts) + SIDE]
    row = lambda j: chip_at(step * SIDE + j, here_ref, x_first) * 128 + core * 64
    outs = chip_products(cuts, refs, row)
    for half, out_ref in enumerate(refs[-2:]):

        @pl.when(step // 2 == half)
        def _():
            at = 0
            for out in outs:
                cols = slice(at, at + out.shape[1])
                for j in range(SIDE):
                    sums = out[j * 64 : j * 64 + 64] + got[j][0, :, cols].astype(F32)
                    out_ref[j, :, cols] = sums.astype(BF16)
                at = cols.stop


def weight_products(pairs, got, x_first, us):
    cuts = [c for _, _, c in pairs]
    arrays = [v for a, b, _ in pairs for v in (a, b)]
    n = sum(c.stop - c.start for c in cuts)
    full = lambda v: pl.BlockSpec(v.shape, lambda i, h: (0, 0))
    block = (SIDE, 64, n)
    if got is None:
        kernel = functools.partial(other_kernel, cuts)
        specs = [full(v) for v in arrays]
        outs = jax.ShapeDtypeStruct((SIDE * SIDE, 64, n), BF16)
        out_specs = pl.BlockSpec(block, lambda i, h: (i, 0, 0))
    else:
        kernel = functools.partial(mine_kernel, cuts, x_first)
        chips = [
            pl.BlockSpec((1, 64, n), lambda i, h, j=j: (chip_at(i * SIDE + j, h, x_first), 0, 0))
            for j in range(SIDE)
        ]
        specs = [full(v) for v in arrays] + chips
        arrays = arrays + [got] * SIDE
        outs = [jax.ShapeDtypeStruct((2 * SIDE, 64, n), BF16)] * 2
        out_specs = [
            pl.BlockSpec(block, lambda i, h: (jnp.minimum(i, 1), 0, 0)),
            pl.BlockSpec(block, lambda i, h: (jnp.maximum(i - 2, 0), 0, 0)),
        ]
    return pl.pallas_call(
        kernel,
        out_shape=outs,
        grid_spec=pltpu.PrefetchScalarGridSpec(
            num_scalar_prefetch=1, grid=(SIDE,), in_specs=specs, out_specs=out_specs
        ),
        compiler_params=pltpu.CompilerParams(vmem_limit_bytes=20 * 2**20),
        cost_estimate=cost(us),
    )(here(), *arrays)


def first_norm_kernel(v_ref, _, low_ref, size_ref):
    v = v_ref[...]
    square = jnp.mean(v * v, axis=-1, keepdims=True) + EPS
    low_ref[...] = (v * lax.rsqrt(square)).astype(BF16)
    size_ref[...] = jnp.broadcast_to(jnp.sqrt(square), size_ref.shape)


def first_norm(residual, part):
    block = pl.BlockSpec((32, D), lambda i: (i, 0))
    return pl.pallas_call(
        first_norm_kernel,
        out_shape=[
            jax.ShapeDtypeStruct((PART, D), BF16), jax.ShapeDtypeStruct((PART, 128), F32)
        ],
        grid=(PART // 32,),
        in_specs=[block, pl.BlockSpec(memory_space=pl.ANY)],
        out_specs=[block, pl.BlockSpec((32, 128), lambda i: (i, 0))],
        compiler_params=pltpu.CompilerParams(vmem_limit_bytes=12 * 2**20),
        cost_estimate=cost(1),
    )(residual, part)


def pair_norm_kernel(
    sum_ref, got_ref, residual_ref, normed_ref, size_ref, own_ref, partner_ref, low_ref
):
    own = pl.program_id(0) < PART // 64
    base = jnp.where(own, residual_ref[...], normed_ref[...].astype(F32) * size_ref[:, :1])
    v = base + (sum_ref[...].astype(F32) + got_ref[...].astype(F32))
    inverse = lax.rsqrt(jnp.mean(v * v, axis=-1, keepdims=True) + EPS)
    low_ref[...] = (v * inverse).astype(BF16)

    @pl.when(own)
    def _():
        own_ref[...] = v

    @pl.when(jnp.logical_not(own))
    def _():
        partner_ref[...] = v.astype(BF16)


def pair_norm_back_kernel(
    sum_ref, got_ref, v_ref, partner_ref, cotangent_ref, low_cotangent_ref, out_ref, low_ref
):
    own = pl.program_id(0) < PART // 64
    base = jnp.where(own, cotangent_ref[...], low_cotangent_ref[...].astype(F32))
    v = jnp.where(own, v_ref[...], partner_ref[...].astype(F32))
    u = sum_ref[...].astype(F32) + got_ref[...].astype(F32)
    inverse = lax.rsqrt(jnp.mean(v * v, axis=-1, keepdims=True) + EPS)
    inner = jnp.mean(u * v, axis=-1, keepdims=True)
    out = base + (inverse * u - v * (inverse * inverse * inverse * inner))
    low_ref[...] = out.astype(BF16)

    @pl.when(own)
    def _():
        out_ref[...] = out


HALF = PART // 64
EACH, ACROSS = (lambda i: i), (lambda i: (i + HALF) % (2 * HALF))
OWN, PARTNER = (lambda i: jnp.minimum(i, HALF - 1)), (lambda i: jnp.maximum(i - HALF, 0))


def by_pair_rows(kernel, ins, outs):
    block = lambda n, at: pl.BlockSpec((64, n), lambda i: (at(i), 0))
    rows = lambda at: 2 * PART if at is EACH else PART
    return pl.pallas_call(
        kernel,
        out_shape=[jax.ShapeDtypeStruct((rows(at), D), t) for t, at in outs],
        grid=(2 * HALF,),
        in_specs=[block(a.shape[1], at) for a, at in ins],
        out_specs=[block(D, at) for _, at in outs],
        compiler_params=pltpu.CompilerParams(vmem_limit_bytes=24 * 2**20),
        cost_estimate=cost(2),
    )(*[a for a, _ in ins])


def norm_back_kernel(near_ref, got_ref, got_own_ref, v_ref, base_ref, out_ref, low_ref):
    u = near_ref[...] + (got_ref[...].astype(F32) + got_own_ref[...].astype(F32))
    v = v_ref[...]
    inverse = lax.rsqrt(jnp.mean(v * v, axis=-1, keepdims=True) + EPS)
    inner = jnp.mean(u * v, axis=-1, keepdims=True)
    out = base_ref[...] + (inverse * u - v * (inverse * inverse * inverse * inner))
    out_ref[...] = out
    low_ref[...] = out.astype(BF16)


def by_rows(kernel, *arrays):
    block = pl.BlockSpec((32, D), lambda i: (i, 0))
    return pl.pallas_call(
        kernel,
        out_shape=[jax.ShapeDtypeStruct((PART, D), t) for t in (F32, BF16)],
        grid=(PART // 32,),
        in_specs=[block] * len(arrays),
        out_specs=[block, block],
        compiler_params=pltpu.CompilerParams(vmem_limit_bytes=12 * 2**20),
        cost_estimate=cost(1.5),
    )(*arrays)


def hidden_kernel(
    near_ref, far_ref, gate_w_ref, up_w_ref, grad_hidden_ref,
    hidden_ref, grad_gate_ref, grad_up_ref, rows_ref,
):
    @pl.when(pl.program_id(0) == 0)
    def _():
        rows_ref[: SEQ // 2, :] = near_ref[...]
        rows_ref[SEQ // 2 :, :] = far_ref[...]

    gate_up = nn(rows_ref[...], jnp.concatenate([gate_w_ref[...], up_w_ref[...]], axis=1))
    grad_hidden = grad_hidden_ref[...]
    gate, up = gate_up[:, :128], gate_up[:, 128:]
    sigmoid = 1.0 / (1.0 + jnp.exp(-gate))
    activated = gate * sigmoid
    slope = sigmoid * (1.0 + gate * (1.0 - sigmoid))
    hidden_ref[...] = (activated * up).astype(BF16)
    grad_gate_ref[...] = (grad_hidden * up * slope).astype(BF16)
    grad_up_ref[...] = (grad_hidden * activated).astype(BF16)


def hidden_units(near, far, grad_hidden, weights):
    steps = HIDDEN // 128
    weight = lambda at: pl.BlockSpec((D, 128), lambda j: (0, at * steps + j))
    return pl.pallas_call(
        hidden_kernel,
        out_shape=[jax.ShapeDtypeStruct((SEQ, HIDDEN), BF16)] * 3,
        grid=(steps,),
        in_specs=whole(2)
        + [weight(0), weight(1), pl.BlockSpec((SEQ, 128), lambda j: (0, j))],
        out_specs=[pl.BlockSpec((SEQ, 128), lambda j: (0, j))] * 3,
        scratch_shapes=[pltpu.VMEM((SEQ, D), BF16)],
        compiler_params=pltpu.CompilerParams(vmem_limit_bytes=24 * 2**20),
        cost_estimate=cost(10),
    )(near, far, weights, weights, grad_hidden)


def turn(x, cosine, sine):
    lane = lax.broadcasted_iota(jnp.int32, x.shape, 1)
    ahead = pltpu.roll(x, 96, 1)
    behind = pltpu.roll(x, 32, 1)
    return x * cosine + jnp.where(lane % HEAD_DIM < HEAD_DIM // 2, ahead, behind) * sine


def mask_bias(ends_ref, block):
    shape = ((block + 1) * PART, PART)
    key = lax.broadcasted_iota(jnp.int32, shape, 0)
    query = lax.broadcasted_iota(jnp.int32, shape, 1) + block * PART
    key_segment = jnp.zeros(shape, jnp.int32)
    query_segment = jnp.zeros(shape, jnp.int32)
    for d in range(4):
        key_segment += (key >= ends_ref[d]).astype(jnp.int32)
        query_segment += (query >= ends_ref[d]).astype(jnp.int32)
    return jnp.where((key_segment == query_segment) & (key <= query), 0.0, -1e30)


def halves(x):
    none = jnp.zeros_like(x)
    return jnp.concatenate([x, none], axis=1), jnp.concatenate([none, x], axis=1)


def in_token_order(slot_ref, kv_ref, ordered_ref):
    for block in range(SIDE):
        rows = pl.ds(pl.multiple_of(slot_ref[block] * PART, PART), PART)
        ordered_ref[block * PART : (block + 1) * PART, :] = kv_ref[rows, :]


def forward_kernel(
    slot_ref, ends_ref, qkv_ref, cos_ref, sin_ref, att_ref, q_ref, kv_ref, lse_ref, ordered_ref
):
    cosine, sine = cos_ref[...], sin_ref[...]
    for pair in range(HEADS_LOCAL // 2):
        cols = slice(pair * 128, pair * 128 + 128)
        q_ref[:, cols] = (turn(qkv_ref[:, cols], cosine, sine).astype(BF16)) * BF16(0.125)
    kv = qkv_ref[:, QUERY_COLS:QKV_COLS]
    lane = lax.broadcasted_iota(jnp.int32, kv.shape, 1)
    kv_ref[...] = jnp.where(lane < HEAD_DIM, turn(kv, cosine, sine), kv).astype(BF16)
    in_token_order(slot_ref, kv_ref, ordered_ref)
    kv = ordered_ref[...]
    keys_both = halves(kv[:, :HEAD_DIM])
    values_turned = kv.astype(F32).T[HEAD_DIM:].astype(BF16)
    heads = range(HEADS_LOCAL)
    for block in range(SIDE):
        seen = (block + 1) * PART
        rows = pl.ds(pl.multiple_of(slot_ref[block] * PART, PART), PART)
        bias = mask_bias(ends_ref, block)
        q = [q_ref[rows, k * 128 : (k + 1) * 128] for k in range(HEADS_LOCAL // 2)]
        s = [nt(keys_both[h % 2][:seen], q[h // 2]) + bias for h in heads]
        top = [jnp.max(v, axis=0, keepdims=True) for v in s]
        e = [jnp.exp(v - t) for v, t in zip(s, top)]
        total = [jnp.sum(v, axis=0, keepdims=True) for v in e]
        p = [(v * (1.0 / t)).astype(BF16) for v, t in zip(e, total)]
        out = [nn(values_turned[:, :seen], v) for v in p]
        for h in heads:
            lse_ref[h : h + 1, block * PART : seen] = top[h] + jnp.log(total[h])
        for k in range(HEADS_LOCAL // 2):
            both = jnp.concatenate(out[2 * k : 2 * k + 2], axis=0)
            att_ref[rows, k * 128 : (k + 1) * 128] = both.T.astype(BF16)


def apart(x):
    lane = lax.broadcasted_iota(jnp.int32, x.shape, 1)
    none = jnp.zeros_like(x)
    first = lane < HEAD_DIM
    return jnp.concatenate([jnp.where(first, x, none), jnp.where(first, none, x)], axis=0)


def backward_kernel(
    slot_ref, ends_ref, q_ref, kv_ref, lse_ref, up_ref, cos_ref, sin_ref,
    out_ref, ordered_ref, dk_ref, dv_ref,
):
    in_token_order(slot_ref, kv_ref, ordered_ref)
    kv = ordered_ref[...]
    keys_both, values_both = halves(kv[:, :HEAD_DIM]), halves(kv[:, HEAD_DIM:])
    keys_turned = kv.astype(F32).T[:HEAD_DIM].astype(BF16)
    dk_ref[...] = jnp.zeros_like(dk_ref)
    dv_ref[...] = jnp.zeros_like(dv_ref)
    heads, pairs = range(HEADS_LOCAL), range(HEADS_LOCAL // 2)
    for block in range(SIDE):
        seen = (block + 1) * PART
        rows = pl.ds(pl.multiple_of(slot_ref[block] * PART, PART), PART)
        bias = mask_bias(ends_ref, block)
        cosine, sine = cos_ref[rows, :], -sin_ref[rows, :]
        q = [q_ref[rows, k * 128 : (k + 1) * 128] for k in pairs]
        up = [up_ref[rows, k * 128 : (k + 1) * 128] for k in pairs]
        s = [nt(keys_both[h % 2][:seen], q[h // 2]) + bias for h in heads]
        dp = [nt(values_both[h % 2][:seen], up[h // 2]) for h in heads]
        p = [jnp.exp(s[h] - lse_ref[h : h + 1, block * PART : seen]) for h in heads]
        inner = [jnp.sum(p[h] * dp[h], axis=0, keepdims=True) for h in heads]
        ds = [(p[h] * (dp[h] - inner[h])).astype(BF16) for h in heads]
        p = [v.astype(BF16) for v in p]
        dq = [nn(keys_turned[:, :seen], v) for v in ds]
        q_apart = jnp.concatenate([apart(v) for v in q], axis=0)
        up_apart = jnp.concatenate([apart(v) for v in up], axis=0)
        dk_ref[:seen, :] += nn(jnp.concatenate(ds, axis=1), q_apart)
        dv_ref[:seen, :] += nn(jnp.concatenate(p, axis=1), up_apart)
        for k in pairs:
            both = jnp.concatenate(dq[2 * k : 2 * k + 2], axis=0).T * 0.125
            out_ref[rows, k * 128 : (k + 1) * 128] = turn(both, cosine, sine).astype(BF16)
    lane = lax.broadcasted_iota(jnp.int32, (SEQ, 128), 1)
    dk, dv = dk_ref[...], dv_ref[...]
    dk, dv = dk + pltpu.roll(dk, HEAD_DIM, 1), dv + pltpu.roll(dv, HEAD_DIM, 1)
    dk_ref[...] = jnp.where(lane < HEAD_DIM, dk, dv)
    for block in range(SIDE):
        rows = pl.ds(pl.multiple_of(slot_ref[block] * PART, PART), PART)
        dkv = dk_ref[block * PART : (block + 1) * PART, :]
        turned = turn(dkv, cos_ref[rows, :], -sin_ref[rows, :])
        dkv = jnp.where(lane[:PART] < HEAD_DIM, turned, dkv)
        out_ref[rows, QUERY_COLS:QKV_COLS] = dkv.astype(BF16)


def small(n):
    return [pl.BlockSpec(memory_space=pltpu.SMEM)] * n


def attend_forward(qkv, tables):
    slot, ends, cosine, sine = tables
    return pl.pallas_call(
        forward_kernel,
        out_shape=(
            jax.ShapeDtypeStruct((SEQ, QUERY_COLS), BF16),
            jax.ShapeDtypeStruct((SEQ, QUERY_COLS), BF16),
            jax.ShapeDtypeStruct((SEQ, 128), BF16),
            jax.ShapeDtypeStruct((HEADS_LOCAL, SEQ), F32),
        ),
        in_specs=small(2) + whole(3),
        out_specs=whole(4),
        scratch_shapes=[pltpu.VMEM((SEQ, 128), BF16)],
        compiler_params=pltpu.CompilerParams(vmem_limit_bytes=24 * 2**20),
        cost_estimate=cost(5),
    )(slot, ends, qkv, cosine, sine)


def attend_backward(q, kv, lse, upstream, tables):
    slot, ends, cosine, sine = tables
    return pl.pallas_call(
        backward_kernel,
        out_shape=jax.ShapeDtypeStruct((SEQ, QKV_COLS), BF16),
        in_specs=small(2) + whole(6),
        out_specs=pl.BlockSpec(memory_space=pltpu.VMEM),
        scratch_shapes=[
            pltpu.VMEM((SEQ, 128), BF16),
            pltpu.VMEM((SEQ, 128), F32),
            pltpu.VMEM((SEQ, 128), F32),
        ],
        compiler_params=pltpu.CompilerParams(vmem_limit_bytes=24 * 2**20),
        cost_estimate=cost(6),
    )(slot, ends, q, kv, lse, upstream, cosine, sine)


def attention_tables(lengths):
    block = lax.axis_index("mp") ^ pair_steps(place()[2])
    slot = jnp.sum(
        jnp.where(block[None, :] == jnp.arange(SIDE)[:, None], jnp.arange(SIDE)[None, :], 0), axis=1
    ).astype(jnp.int32)
    token = (block[:, None] * PART + jnp.arange(PART)[None, :]).reshape(SEQ)
    ends = jnp.cumsum(lengths).astype(jnp.int32)
    starts = ends - lengths
    leading = jnp.max(jnp.where(starts[None, :] <= token[:, None], starts[None, :], 0), axis=1)
    indices = jnp.arange(HEAD_DIM // 2).astype(F32)
    frequency = 1.0 / THETA ** (2.0 * indices / HEAD_DIM)
    angles = (token - leading).astype(F32)[:, None] * frequency[None, :]
    cosine, sine = jnp.cos(angles), jnp.sin(angles)
    cosine = jnp.concatenate([cosine] * 4, axis=1)
    sine = jnp.concatenate([-sine, sine, -sine, sine], axis=1)
    return slot, ends, cosine, sine


def adamw(weight, gradient, moment, square, rate, decay):
    momentum = BETA_ONE * moment + (1.0 - BETA_ONE) * gradient
    variance = BETA_TWO * square + (1.0 - BETA_TWO) * gradient * gradient
    moment_hat = momentum / (1.0 - BETA_ONE**STEP)
    square_hat = variance / (1.0 - BETA_TWO**STEP)
    updated = weight - rate * (moment_hat / (jnp.sqrt(square_hat) + ADAM_EPS) + decay * weight)
    return (momentum, variance, updated)


def after(x, *others):
    return lax.optimization_barrier((x, *others))[0]


def on_device(
    residual, cotangent, document_lengths,
    norm_gains, query_weight, keyvalue_weight, output_weight, gateup_weight, down_weight,
    moment_gains, moment_query, moment_keyvalue, moment_output, moment_gateup, moment_down,
    square_gains, square_query, square_keyvalue, square_output, square_gateup, square_down,
):
    residual, cotangent = residual[0], cotangent[0]
    half = SEQ // 2

    part, ffn_part = prepare(
        norm_gains, query_weight, keyvalue_weight, output_weight, gateup_weight, down_weight
    )
    normed_one, size = first_norm(residual, part)
    got_one = pair_z(normed_one, 0)
    got_size = pair_z(size, 0)
    line = jnp.stack([part, shift_first(part, 1), shift_first(part, -1), shift_first(part, 2)])
    ffn_full = lax.all_gather(ffn_part, "dp", axis=0, tiled=True)
    tables = attention_tables(document_lengths[0])
    line = after(line, *tables)
    plane = [line, shift_second(line, 1), shift_second(line, -1), shift_second(line, 2)]
    one_near = after(jnp.concatenate([normed_one, got_one]), line)
    one_far = pair_z(one_near, 1)
    low_cotangent = after(cotangent.astype(BF16), one_near)
    cot_near = jnp.concatenate([low_cotangent, pair_z(low_cotangent, 0)])
    mine = jnp.stack(plane, axis=1).reshape(SIDE * SIDE, *part.shape)
    mine = after(mine, one_far, cot_near)
    other = swap_core(mine)
    cot_far = pair_z(cot_near, 1)
    qkv_full, output_full = place_attention(mine, other)
    qkv = nn(one_near, qkv_full), nn(one_far, qkv_full)
    attended, q, kv, lse = attend_forward(after(jnp.concatenate(qkv), got_size), tables)

    far = nt(after(attended, cot_far)[half:], output_full).astype(BF16)
    got = pair_z(far, 1)
    near = nt(after(attended, far)[:half], output_full)
    cot_turned = turned(after(cot_near, near), cot_far)
    got = after(got, cot_turned)
    sent = add_low(near, got)
    got_pair = pair_z(sent, 0)
    cot_rows = jnp.concatenate([cot_near, cot_far])
    got_pair = after(got_pair, cot_rows)
    middle, partner_middle, two_near = by_pair_rows(
        pair_norm_kernel,
        ((sent, EACH), (got_pair, ACROSS), (residual, OWN), (one_near, EACH), (got_size, PARTNER)),
        ((F32, OWN), (BF16, PARTNER), (BF16, EACH)),
    )
    two_far = pair_z(two_near, 1)
    down_full = ffn_full[:, 2 * HIDDEN :]
    one_turned = turned(after(one_near, two_near), one_far)
    grad_hidden = nn(after(cot_rows, one_turned), down_full)
    two_far = after(two_far, grad_hidden)

    hidden, grad_gate, grad_up = hidden_units(two_near, two_far, grad_hidden, ffn_full)
    near, far = back_to_rows(grad_gate, grad_up, ffn_full)
    got = pair_z(far, 1)
    rows_turned = turned(after(two_near, far), two_far)
    all_columns = slice(0, HIDDEN)
    pairs_a = (
        (rows_turned, grad_gate, all_columns), (cot_turned, hidden, slice(0, SPLIT))
    )
    pairs_b = (
        (rows_turned, grad_up, all_columns), (cot_turned, hidden, slice(SPLIT, HIDDEN))
    )
    other_a = weight_products(pairs_a, None, True, 4)
    other_b = weight_products(pairs_b, None, False, 4)
    got = after(got, other_a, other_b)
    sent = add_low(near, got)
    got_pair = pair_z(sent, 0)
    got_a = swap_core(after(other_a, sent))
    got_b = swap_core(after(other_b, sent))
    down = nt(after(hidden, sent), down_full)
    down_near, down_far = down[:half], down[half:].astype(BF16)
    near_a, far_a = weight_products(pairs_a, after(got_a, down), True, 4)
    got_a = pair_first(far_a, 1, True)
    got_pair = after(got_pair, near_a)

    grad_middle, rows_near = by_pair_rows(
        pair_norm_back_kernel,
        (
            (sent, EACH), (got_pair, ACROSS), (middle, OWN), (partner_middle, PARTNER),
            (cotangent, OWN), (cot_near, EACH),
        ),
        ((F32, OWN), (BF16, EACH)),
    )
    rows_far = pair_z(rows_near, 1)
    near_b, far_b = weight_products(pairs_b, after(got_b, rows_near), False, 0.001)
    got_b = pair_first(far_b, 1, False)
    grad_attended = nn(after(rows_near, near_b), output_full).astype(BF16)
    rows_far = after(rows_far, grad_attended)
    grad_attended = jnp.concatenate([grad_attended, nn(rows_far, output_full).astype(BF16)])
    grad_projected = attend_backward(q, kv, lse, grad_attended, tables)
    pairs_qkv = ((one_turned, grad_projected, slice(0, QKV_COLS)),)
    other_qkv = weight_products(pairs_qkv, None, True, 1)
    got_qkv = swap_core(other_qkv)
    near, far = product_rows(after(grad_projected, other_qkv), qkv_full, 0, 2)
    got = pair_z(far, 1)
    keep_a, sent_a = split_sum(near_a, after(got_a, far))
    got_a = pair_first(sent_a, 0, True)
    middle_turned = turned(after(rows_near, sent_a), rows_far, 0.001)
    pairs_output = ((middle_turned, attended, slice(0, QUERY_COLS)),)
    other_output = weight_products(pairs_output, None, False, 0.001)
    got_output = swap_core(other_output)
    keep_b, sent_b = split_sum(near_b, after(got_b, other_output))
    got_b = pair_first(sent_b, 0, False)
    near_qkv, far_qkv = weight_products(pairs_qkv, after(got_qkv, sent_b), True, 0.001)
    got_qkv = pair_first(far_qkv, 1, True)
    near_output, far_output = weight_products(
        pairs_output, after(got_output, near_qkv), False, 0.001
    )
    got_output = pair_first(far_output, 1, False)
    got = after(got, near_output)
    sent = send_sum(near, got)
    got_own = pair_z(sent, 0)

    keep_qkv, sent_qkv = split_sum(near_qkv, after(got_qkv, sent))
    got_qkv = pair_first(sent_qkv, 0, True)
    line_a = (keep_a + after(got_a, sent_qkv).astype(F32)).astype(BF16)
    got_a = pair_second(line_a[2:], 1, True)
    keep_output, sent_output = split_sum(near_output, after(got_output, line_a))
    got_output = pair_first(sent_output, 0, False)
    got_own = after(got_own, sent_output)
    input_gradient, _ = by_rows(norm_back_kernel, near, got, got_own, residual, grad_middle)
    got_down = pair_z(after(down_far, got_own), 1)
    line_b = (keep_b + after(got_b, got_own).astype(F32)).astype(BF16)
    got_b = pair_second(line_b[2:], 1, False)
    line_qkv = (keep_qkv + after(got_qkv, line_b).astype(F32)).astype(BF16)
    got_qkv = pair_second(line_qkv[2:], 1, True)
    line_output = (keep_output + after(got_output, line_qkv).astype(F32)).astype(BF16)
    got_output = pair_second(line_output[2:], 1, False)
    keep_a, sent_a = split_sum(line_a[:2], after(got_a, line_output))
    got_a = pair_second(sent_a, 0, True)
    keep_qkv, sent_qkv = split_sum(line_qkv[:2], after(got_qkv, sent_a))
    got_qkv = pair_second(sent_qkv, 0, True)
    got_down = after(got_down, sent_qkv)
    sent_down = send_sum(down_near, got_down)
    got_down_own = pair_z(sent_down, 0)
    keep_b, sent_b = split_sum(line_b[:2], after(got_b, sent_down))
    got_b = pair_second(sent_b, 0, False)
    keep_output, sent_output = split_sum(line_output[:2], after(got_output, sent_b))
    got_output = pair_second(sent_output, 0, False)
    grad_ffn_a = keep_a[0] + got_a[0].astype(F32)
    grad_qkv = keep_qkv[0] + got_qkv[0].astype(F32)
    grad_ffn_b = keep_b[0] + got_b[0].astype(F32)
    block_output = middle + (
        down_near[:PART] + (got_down[:PART].astype(F32) + got_down_own.astype(F32))
    )

    low_gains = norm_gains.astype(BF16).astype(F32)
    gain_one, gain_two = low_gains[0][:, None], low_gains[1][:, None]
    low_qkv = jnp.concatenate(
        (query_weight, keyvalue_weight[0], keyvalue_weight[1]), axis=1
    ).astype(BF16)
    low_gate, low_up = (w.astype(BF16).astype(F32) for w in (gateup_weight[0], gateup_weight[1]))
    gain_parts = jnp.stack(
        (
            jnp.sum(low_qkv.astype(F32) * grad_qkv, axis=1),
            jnp.sum(low_gate * grad_ffn_a[:, :HIDDEN], axis=1)
            + jnp.sum(low_up * grad_ffn_b[:, :HIDDEN], axis=1),
        )
    )
    grad_output = keep_output[0] + after(got_output, gain_parts)[0].astype(F32)
    gains = gain_parts + shift_z(gain_parts, 1) + shift_z(gain_parts, -1) + shift_z(gain_parts, 2)
    grad_qkv = grad_qkv * gain_one
    reduced = (
        gains,
        grad_qkv[:, :QUERY_COLS],
        jnp.stack((grad_qkv[:, QUERY_COLS : QUERY_COLS + 64], grad_qkv[:, QUERY_COLS + 64 :])),
        grad_output.T,
        jnp.stack((grad_ffn_a[:, :HIDDEN] * gain_two, grad_ffn_b[:, :HIDDEN] * gain_two)),
        jnp.concatenate((grad_ffn_a[:, HIDDEN:], grad_ffn_b[:, HIDDEN:]), axis=1).T,
    )
    masters = (norm_gains, query_weight, keyvalue_weight, output_weight, gateup_weight, down_weight)
    moments = (
        moment_gains, moment_query, moment_keyvalue, moment_output, moment_gateup, moment_down,
    )
    squares = (
        square_gains, square_query, square_keyvalue, square_output, square_gateup, square_down,
    )
    results = [
        adamw(masters[i], reduced[i], moments[i], squares[i], RATES[i], DECAYS[i]) for i in range(6)
    ]
    return (
        block_output[None],
        input_gradient[None],
        *reduced,
        *(r[0] for r in results),
        *(r[1] for r in results),
        *(r[2] for r in results),
    )


def solution(mesh):
    rows = P("dp", "mp", None)
    weights = (
        P(None, "dp"),
        P("dp", "mp"),
        P(None, "dp", "mp"),
        P("mp", "dp"),
        P(None, "dp", "mp"),
        P("mp", "dp"),
    )
    return jax.shard_map(
        on_device,
        mesh=mesh,
        in_specs=(rows, rows, P("dp", None), *weights, *weights, *weights),
        out_specs=(rows, rows, *weights, *weights, *weights, *weights),
        check_vma=False,
    )
```
